32 devices in a mesh: seq: 2 (over core), shard: 16 (over z, y, x).
Axes of the slice: x: 2, y: 2, z: 4, core: 2. Of those that a mesh axis runs over, the one named last changes fastest.
Arguments:
- hidden_in: bfloat16 [16, 256, 2048], P('shard', 'seq'), may hold values from -6 to 6
- out_grad: bfloat16 [16, 256, 2048], P('shard', 'seq'), may hold values from -6 to 6
- segments: int32 [16, 256], P('shard'), may hold values from 0 to 2, as said below
- qkv_weight: float32 [2048, 4096], P(('seq', 'shard')), may hold values from -0.09375 to 0.09375
- out_weight: float32 [2048, 2048], P(('seq', 'shard')), may hold values from -0.75 to 0.75
- gateup_weight: float32 [2048, 16384], P(('seq', 'shard')), may hold values from -0.09375 to 0.09375
- down_weight: float32 [8192, 2048], P(('seq', 'shard')), may hold values from -0.0625 to 0.0625
- gain_weight: float32 [2, 2048], P(None, ('seq', 'shard'))
- qkv_first: float32 [2048, 4096], P(('seq', 'shard'))
- out_first: float32 [2048, 2048], P(('seq', 'shard'))
- gateup_first: float32 [2048, 16384], P(('seq', 'shard'))
- down_first: float32 [8192, 2048], P(('seq', 'shard'))
- gain_first: float32 [2, 2048], P(None, ('seq', 'shard'))
- qkv_second: float32 [2048, 4096], P(('seq', 'shard'))
- out_second: float32 [2048, 2048], P(('seq', 'shard'))
- gateup_second: float32 [2048, 16384], P(('seq', 'shard'))
- down_second: float32 [8192, 2048], P(('seq', 'shard'))
- gain_second: float32 [2, 2048], P(None, ('seq', 'shard'))
Outputs:
- output: bfloat16 [16, 256, 2048], P('shard', 'seq')
- input_grad: bfloat16 [16, 256, 2048], P('shard', 'seq')
- qkv_new: float32 [2048, 4096], P(('seq', 'shard'))
- out_new: float32 [2048, 2048], P(('seq', 'shard'))
- gateup_new: float32 [2048, 16384], P(('seq', 'shard'))
- down_new: float32 [8192, 2048], P(('seq', 'shard'))
- gain_new: float32 [2, 2048], P(None, ('seq', 'shard'))
- qkv_momentum: float32 [2048, 4096], P(('seq', 'shard'))
- out_momentum: float32 [2048, 2048], P(('seq', 'shard'))
- gateup_momentum: float32 [2048, 16384], P(('seq', 'shard'))
- down_momentum: float32 [8192, 2048], P(('seq', 'shard'))
- gain_momentum: float32 [2, 2048], P(None, ('seq', 'shard'))
- qkv_variance: float32 [2048, 4096], P(('seq', 'shard'))
- out_variance: float32 [2048, 2048], P(('seq', 'shard'))
- gateup_variance: float32 [2048, 16384], P(('seq', 'shard'))
- down_variance: float32 [8192, 2048], P(('seq', 'shard'))
- gain_variance: float32 [2, 2048], P(None, ('seq', 'shard'))
- qkv_copy: bfloat16 [2048, 4096], P(('seq', 'shard'))
- out_copy: bfloat16 [2048, 2048], P(('seq', 'shard'))
- gateup_copy: bfloat16 [2048, 16384], P(('seq', 'shard'))
- down_copy: bfloat16 [8192, 2048], P(('seq', 'shard'))
- gain_copy: bfloat16 [2, 2048], P(None, ('seq', 'shard'))
- trust_norms: float32 [2, 6], replicated
The draws below stay inside these ranges and needn't reach their ends.
Inputs may be any that keep to these rules, and one draw needn't show every extreme that they name: `segments`: each row is one prompt group: ids never fall along the row; id 0 marks the prompt, which holds more than half of the row; ids 1 to 2 mark the continuations in order, each with one token or more.
All inputs are finite; a program needn't handle non-finite values.
Results may differ from the reference program's by a relative error of at most 0.015.
The reference program's roundings to bfloat16 on the way count: a program that leaves them out, or rounds other values in their place, can miss the bound.
Values may be sent and summed in bfloat16 or wider, within the bound.
No kernel may reach another device: no remote copies, remote signals or barrier semaphores. Data moves between devices by JAX's collectives and lax.ppermute only.
A program may use at most 960 MiB of HBM per device.

```python
import math
import jax
import jax.numpy as jnp
from jax import lax

D = 2048
HQ = 16
KVH = 8
HD = 128
FF = 8192
NCONT = 2
STEP = 10
QKV = 4096
GROUP_TOK = 256
GROUPS = 16
TOKENS = 4096


def first_state(key, shape, size):
    return 0.111 * size * jax.random.normal(key, shape, jnp.float32)


def second_state(key, shape, size):
    spread = jax.random.uniform(key, shape, jnp.float32, 0.0, math.log(4.0))
    return 0.001 * size * size * jnp.exp(spread)


def draw_segments(key, part):
    key = jax.random.fold_in(key, 11)
    first_key, second_key = jax.random.split(key)
    span_size = GROUP_TOK // 4
    prompt = GROUP_TOK // 2 + GROUP_TOK // 8 + jax.random.randint(first_key, (GROUPS, 1), 0, span_size + 1)
    shares = jax.random.randint(second_key, (GROUPS, NCONT), 1, 5)
    cumul = jnp.cumsum(shares, axis=1)
    remain = GROUP_TOK - prompt - NCONT
    cuts = prompt + jnp.arange(NCONT, dtype=jnp.int32)[None, :] + remain * (cumul - shares) // cumul[:, -1:]
    places = jnp.arange(GROUP_TOK, dtype=jnp.int32)
    return jnp.sum((places[None, None, :] >= cuts[:, :, None]).astype(jnp.int32), axis=1).astype(jnp.int32)


def draw_gain_weight(key, part):
    key = jax.random.fold_in(key, 3)
    place = jnp.arange(D, dtype=jnp.float32) / D
    profile = 0.5 * jnp.exp(place * math.log(6.0))
    noise = jax.random.uniform(key, (2, D), jnp.float32, 0.85, 1.15)
    return profile[None, :] * noise


def draw_qkv_first(key, part):
    key = jax.random.fold_in(key, 21)
    return first_state(key, (D, QKV), 1.5 * math.sqrt(TOKENS))


def draw_out_first(key, part):
    key = jax.random.fold_in(key, 22)
    return first_state(key, (HQ * HD, D), 3.6 * math.sqrt(GROUPS))


def draw_gateup_first(key, part):
    key = jax.random.fold_in(key, 23)
    return first_state(key, (D, 2 * FF), math.sqrt(TOKENS))


def draw_down_first(key, part):
    key = jax.random.fold_in(key, 24)
    return first_state(key, (FF, D), 0.65 * math.sqrt(TOKENS))


def draw_gain_first(key, part):
    key = jax.random.fold_in(key, 25)
    return first_state(key, (2, D), math.sqrt(TOKENS))


def draw_qkv_second(key, part):
    key = jax.random.fold_in(key, 31)
    return second_state(key, (D, QKV), 1.5 * math.sqrt(TOKENS))


def draw_out_second(key, part):
    key = jax.random.fold_in(key, 32)
    return second_state(key, (HQ * HD, D), 3.6 * math.sqrt(GROUPS))


def draw_gateup_second(key, part):
    key = jax.random.fold_in(key, 33)
    return second_state(key, (D, 2 * FF), math.sqrt(TOKENS))


def draw_down_second(key, part):
    key = jax.random.fold_in(key, 34)
    return second_state(key, (FF, D), 0.65 * math.sqrt(TOKENS))


def draw_gain_second(key, part):
    key = jax.random.fold_in(key, 35)
    return second_state(key, (2, D), math.sqrt(TOKENS))


def block_scale(key, dims, shards, least, high):
    def one(position, parts):
        heights = jax.random.uniform(jax.random.fold_in(jax.random.fold_in(key, 6), position), (parts,), jnp.float32, least / len(shards), high / len(shards))
        return jnp.repeat(jnp.exp(heights), dims[position] // parts).reshape((-1,) + (1,) * (len(dims) - position - 1))

    factor_of = one(*shards[0])
    for cut in shards[1:]:
        factor_of = factor_of * one(*cut)
    return factor_of


def scatter_about(key, shape, scale, bound, cuts=(), held_as=jnp.bfloat16):
    factor_of = block_scale(key, shape, cuts, -0.22, 0.18) if cuts else 1.0
    array = jax.random.normal(key, shape, jnp.float32) * scale * factor_of
    return jnp.minimum(jnp.maximum(array, -bound), bound).astype(held_as)


def setup_inputs(seed: int = 0) -> dict:
    keys = jax.random.split(jax.random.key(seed), 19)
    hidden_in = scatter_about(keys[0], (GROUPS, GROUP_TOK, D), 1.0, 6.0, ((0, 16), (1, 2)))
    out_grad = scatter_about(keys[1], (GROUPS, GROUP_TOK, D), 1.0, 6.0, ((0, 16), (1, 2)))
    segments = draw_segments(jax.random.fold_in(keys[18], 71), 0)
    qkv_weight = scatter_about(keys[3], (D, QKV), (2 * D) ** -0.5, 0.09375, ((0, 32),), jnp.float32)
    out_weight = scatter_about(keys[4], (HQ * HD, D), (9 * HQ * HD // GROUP_TOK) ** -0.5, 0.75, ((0, 32),), jnp.float32)
    gateup_weight = scatter_about(keys[5], (D, 2 * FF), (2 * D) ** -0.5, 0.09375, ((0, 32),), jnp.float32)
    down_weight = scatter_about(keys[6], (FF, D), FF ** -0.5, 0.0625, ((0, 32),), jnp.float32)
    gain_weight = draw_gain_weight(jax.random.fold_in(keys[18], 71), 0)
    qkv_first = draw_qkv_first(jax.random.fold_in(keys[18], 71), 0)
    out_first = draw_out_first(jax.random.fold_in(keys[18], 71), 0)
    gateup_first = draw_gateup_first(jax.random.fold_in(keys[18], 71), 0)
    down_first = draw_down_first(jax.random.fold_in(keys[18], 71), 0)
    gain_first = draw_gain_first(jax.random.fold_in(keys[18], 71), 0)
    qkv_second = draw_qkv_second(jax.random.fold_in(keys[18], 71), 0)
    out_second = draw_out_second(jax.random.fold_in(keys[18], 71), 0)
    gateup_second = draw_gateup_second(jax.random.fold_in(keys[18], 71), 0)
    down_second = draw_down_second(jax.random.fold_in(keys[18], 71), 0)
    gain_second = draw_gain_second(jax.random.fold_in(keys[18], 71), 0)
    return dict(hidden_in=hidden_in, out_grad=out_grad, segments=segments, qkv_weight=qkv_weight, out_weight=out_weight, gateup_weight=gateup_weight, down_weight=down_weight, gain_weight=gain_weight, qkv_first=qkv_first, out_first=out_first, gateup_first=gateup_first, down_first=down_first, gain_first=gain_first, qkv_second=qkv_second, out_second=out_second, gateup_second=gateup_second, down_second=down_second, gain_second=gain_second)


NORM_EPS = 1e-05
THETA = 1000000.0
BETA1 = 0.9
BETA2 = 0.999
ADAM_EPS = 1e-06
DECAY = 0.01
RATE = 0.5
MASKED = -1e+30

@jax.custom_vjp
def low(v):
    return lax.optimization_barrier(v.astype(jnp.bfloat16)).astype(jnp.float32)

@jax.custom_vjp
def low_back(v):
    return v

def low_keep(v):
    return (low(v), None)

def low_pass(kept, grad):
    return (grad,)

def back_keep(v):
    return (v, None)

def back_low(kept, grad):
    return (low(grad),)
low.defvjp(low_keep, low_pass)
low_back.defvjp(back_keep, back_low)

def norm_scale(values):
    return lax.rsqrt(lax.optimization_barrier(jnp.mean(values * values, axis=-1, keepdims=True)) + NORM_EPS)

def positions_of(seg_row):
    labels = jnp.arange(NCONT + 1, dtype=jnp.int32)
    member = (seg_row[:, None] == labels[None, :]).astype(jnp.int32)
    counts = lax.optimization_barrier(jnp.sum(member, axis=0)).astype(jnp.int32)
    starts = (jnp.cumsum(counts) - counts).astype(jnp.int32)
    own_start = lax.optimization_barrier(jnp.sum(member * starts[None, :], axis=1)).astype(jnp.int32)
    places = jnp.arange(seg_row.shape[0], dtype=jnp.int32)
    return (places - own_start + jnp.where(seg_row > 0, counts[0], 0)).astype(jnp.int32)

def rotary(positions):
    half_size = HD // 2
    frequency = THETA ** (-(jnp.arange(half_size, dtype=jnp.float32) * (2.0 / HD)))
    angles = positions.astype(jnp.float32)[:, None] * frequency[None, :]
    angles = jnp.concatenate([angles, angles], axis=-1)
    return (jnp.cos(angles), jnp.sin(angles))

def turn_half(values):
    half_size = values.shape[-1] // 2
    return jnp.concatenate([-values[..., half_size:], values[..., :half_size]], axis=-1)

def rope(values, cosine, sine):
    return values * cosine[:, None, None, :] + turn_half(values) * sine[:, None, None, :]

def allowed_of(seg_row):
    places = jnp.arange(seg_row.shape[0], dtype=jnp.int32)
    causal = places[None, :] <= places[:, None]
    same_doc = (seg_row[None, :] == 0) | (seg_row[None, :] == seg_row[:, None])
    return causal & same_doc

def layer(params, token_rows, cosine, sine, allowed):
    qkv_matrix, out_matrix, gateup_matrix, down_matrix, gain_rows = params
    highest = lax.Precision.HIGHEST
    row_count = token_rows.shape[0]
    group_size = HQ // KVH
    normed = low(token_rows * norm_scale(token_rows) * gain_rows[0])
    projected = low_back(jnp.dot(normed, qkv_matrix, precision=highest))
    projected = projected.reshape(row_count, KVH, group_size + 2, HD)
    turned = jnp.concatenate([rope(projected[:, :, :group_size + 1], cosine, sine), projected[:, :, group_size + 1:]], axis=2)
    turned = low(low_back(turned))
    queries = turned[:, :, :group_size]
    key_rows = turned[:, :, group_size]
    value_rows = turned[:, :, group_size + 1]
    scores = low_back(jnp.einsum('qgjd,kgd->gjqk', queries, key_rows, precision=highest) * HD ** (-0.5))
    scores = jnp.where(allowed[None, None], scores, MASKED)
    row_max = lax.optimization_barrier(jnp.max(scores, axis=-1, keepdims=True))
    exponent = jnp.exp(scores - row_max)
    attn_probs = low(exponent / lax.optimization_barrier(jnp.sum(exponent, axis=-1, keepdims=True)))
    attended = low(low_back(jnp.einsum('gjqk,kgd->qgjd', attn_probs, value_rows, precision=highest)))
    branch = low_back(jnp.dot(attended.reshape(row_count, HQ * HD), out_matrix, precision=highest))
    middle = token_rows + branch
    normed2 = low(middle * norm_scale(middle) * gain_rows[1])
    gate_up = low_back(jnp.dot(normed2, gateup_matrix, precision=highest))
    activated = low(jax.nn.silu(gate_up[:, :FF]) * gate_up[:, FF:])
    return middle + low_back(jnp.dot(activated, down_matrix, precision=highest))

def square_sums(arrays):
    matrix_sums = jnp.stack([jnp.sum(entry * entry) for entry in arrays[:4]])
    return jnp.concatenate([matrix_sums, lax.optimization_barrier(jnp.sum(arrays[4] * arrays[4], axis=1))])

def lamb_moments(masters, gradients, moment_ones, moment_twos):
    decay_rates = (DECAY, DECAY, DECAY, DECAY, 0.0)
    new_ones, new_twos, updates = ([], [], [])
    for master, gradient, old_one, old_two, decay_rate in zip(masters, gradients, moment_ones, moment_twos, decay_rates):
        new_one = BETA1 * old_one + (1.0 - BETA1) * gradient
        new_two = BETA2 * old_two + (1.0 - BETA2) * gradient * gradient
        update = new_one / (1.0 - BETA1 ** STEP) / (jnp.sqrt(new_two / (1.0 - BETA2 ** STEP)) + ADAM_EPS) + decay_rate * master
        new_ones.append(new_one)
        new_twos.append(new_two)
        updates.append(update)
    return (new_ones, new_twos, updates)

def apply_trust(masters, updates, norms):
    ratios = norms[0] / norms[1]
    news = [masters[slot] - RATE * ratios[slot] * updates[slot] for slot in range(4)]
    news.append(masters[4] - RATE * ratios[4:6][:, None] * updates[4])
    return news

def reference(hidden_in, out_grad, segments, qkv_weight, out_weight, gateup_weight, down_weight, gain_weight, qkv_first, out_first, gateup_first, down_first, gain_first, qkv_second, out_second, gateup_second, down_second, gain_second):
    masters = (qkv_weight, out_weight, gateup_weight, down_weight, gain_weight)

    def one_group(grad_sums, inputs_now):
        token_rows, cotangent, seg_row = inputs_now
        cosine, sine = rotary(positions_of(seg_row))
        allowed = allowed_of(seg_row)

        def forward(params, token_block):
            rounded = tuple((low(param) for param in params))
            return layer(rounded, token_block, cosine, sine, allowed)
        result, pullback = jax.vjp(forward, masters, token_rows.astype(jnp.float32))
        gradients, d_rows = pullback(cotangent.astype(jnp.float32))
        grad_sums = tuple((total + gradient for total, gradient in zip(grad_sums, gradients)))
        return (grad_sums, (result.astype(jnp.bfloat16), d_rows.astype(jnp.bfloat16)))
    zeros = tuple((jnp.zeros_like(master) for master in masters))
    gradients, (output, input_grad) = lax.scan(one_group, zeros, (hidden_in, out_grad, segments))
    new_ones, new_twos, updates = lamb_moments(masters, gradients, (qkv_first, out_first, gateup_first, down_first, gain_first), (qkv_second, out_second, gateup_second, down_second, gain_second))
    norms = jnp.sqrt(jnp.stack([square_sums(masters), square_sums(updates)]))
    news = apply_trust(masters, updates, norms)
    copies = [entry.astype(jnp.bfloat16) for entry in news]
    return (output, input_grad, news[0], news[1], news[2], news[3], news[4], new_ones[0], new_ones[1], new_ones[2], new_ones[3], new_ones[4], new_twos[0], new_twos[1], new_twos[2], new_twos[3], new_twos[4], copies[0], copies[1], copies[2], copies[3], copies[4], norms)
```

```python
import jax
import jax.numpy as jnp
from jax import lax
from jax.sharding import PartitionSpec as P

HQ = 16
KVH = 8
HD = 128
FF = 8192
NCONT = 2
STEP = 10
TP = 4


NORM_EPS = 1e-05
THETA = 1000000.0
BETA1 = 0.9
BETA2 = 0.999
ADAM_EPS = 1e-06
DECAY = 0.01
RATE = 0.5
MASKED = -1e30
GROUP = HQ // KVH
HEAD_COLS = (GROUP + 2) * HD
BF = jnp.bfloat16
F32 = jnp.float32


def dot(left, right):
    return jnp.dot(left, right, preferred_element_type=F32)


def dot_rows(left, right):
    return lax.dot_general(left, right, (((0,), (0,)), ((), ())), preferred_element_type=F32)


def dot_last(left, right):
    return lax.dot_general(left, right, (((1,), (1,)), ((), ())), preferred_element_type=F32)


def shard_size():
    return lax.axis_size("shard")


def place_size():
    return shard_size() // TP


def rotate(values, steps):
    count, places = shard_size(), place_size()
    pairs = [
        (entry, ((entry // places - steps) % TP) * places + entry % places)
        for entry in range(count)
    ]
    return lax.ppermute(values, "shard", pairs)


def hop(values, bit):
    return lax.ppermute(values, "shard", [(i, i ^ (1 << bit)) for i in range(shard_size())])


def flip(values):
    return lax.ppermute(values, "seq", [(0, 1), (1, 0)])


def butterfly(values):
    values = values + flip(values)
    for bit in range(shard_size().bit_length() - 1):
        values = values + hop(values, bit)
    return values


def gather_groups(own):
    chunks = []
    for step in range(TP):
        mine = own if step == 0 else rotate(own, step)
        chunks.append(jnp.concatenate([mine, flip(mine)], axis=0))
    return chunks


def scatter_groups(parts):
    half = parts[0].shape[0] // 2
    total = None
    for step in list(range(1, TP)) + [0]:
        part = parts[step]
        met = part[:half] + flip(part[half:].astype(BF)).astype(F32)
        if step:
            met = rotate(met.astype(BF), -step).astype(F32)
        total = met if total is None else total + met
    return total


def gather_places(own):
    bits = place_size().bit_length() - 1
    if bits == 2:
        rows = own.shape[0] // 2
        one, two = hop(own, 0), hop(own, 1)
        three = jnp.concatenate([hop(one[:rows], 1), hop(two[rows:], 0)], axis=0)
        return [own, one, two, three]
    blocks = {0: own}
    for bit in range(bits):
        for entry in list(blocks):
            blocks[entry | (1 << bit)] = hop(blocks[entry], bit)
    return [blocks[entry] for entry in range(place_size())]


def place_index():
    return lax.axis_index("shard") % place_size()


def column_index():
    return lax.axis_index("shard") // place_size()


def lay_places(blocks, axis):
    shape = blocks[0].shape
    full = jnp.zeros(shape[:axis] + (len(blocks),) + shape[axis:], blocks[0].dtype)
    for entry, block in enumerate(blocks):
        starts = [0] * full.ndim
        starts[axis] = place_index() ^ entry
        full = lax.dynamic_update_slice(full, jnp.expand_dims(block, axis), starts)
    return full


def scatter_places(blocks):
    bits = place_size().bit_length() - 1
    if bits == 2:
        rows = blocks[0].shape[0] // 2
        zero, one, two, three = blocks
        one_b = one[rows:].astype(F32) + hop(three[rows:], 1).astype(F32)
        two_a = two[:rows].astype(F32) + hop(three[:rows], 0).astype(F32)
        upper = (
            zero[:rows].astype(F32)
            + hop(one[:rows], 0).astype(F32)
            + hop(two_a.astype(BF), 1).astype(F32)
        )
        lower = (
            zero[rows:].astype(F32)
            + hop(two[rows:], 1).astype(F32)
            + hop(one_b.astype(BF), 0).astype(F32)
        )
        return jnp.concatenate([upper, lower], axis=0)
    sums = {entry: block.astype(F32) for entry, block in enumerate(blocks)}
    for bit in reversed(range(bits)):
        for entry in range(1 << bit):
            sums[entry] = sums[entry] + hop(sums.pop(entry | (1 << bit)).astype(BF), bit).astype(F32)
    return sums[0]


def ordered_pair(mine, other, axis=0):
    first = lax.axis_index("seq") == 0
    return jnp.stack([jnp.where(first, mine, other), jnp.where(first, other, mine)], axis=axis)


def turn_columns(blocks):
    twice = jnp.stack(blocks + blocks)
    return lax.dynamic_slice_in_dim(twice, (TP - column_index()) % TP, TP, 0)


def spread(weight, cuts):
    rows = weight.shape[0]
    width = weight.shape[1] // (cuts * 2 * TP)
    seq, column = lax.axis_index("seq"), column_index()

    def take(source, index, size):
        span = source.shape[1] // cuts
        return jnp.concatenate(
            [
                lax.dynamic_slice_in_dim(source, cut * span + index * size, size, 1)
                for cut in range(cuts)
            ],
            axis=1,
        )

    mine = take(weight, seq, TP * width)
    other = flip(take(weight, 1 - seq, TP * width))
    pair = ordered_pair(mine, other).reshape(2 * rows, cuts * TP * width)
    blocks = []
    for step in range(TP):
        piece = take(pair, (column - step) % TP, width)
        blocks.append(piece if step == 0 else rotate(piece, step))
    return turn_columns(blocks).reshape(TP, 2, rows, cuts * width)


def full_rows(weight, cuts):
    blocks = gather_places(spread(weight, cuts).reshape(-1, weight.shape[1] // (2 * TP)))
    rows = weight.shape[0]
    blocks = [jnp.swapaxes(block.reshape(TP, 2, rows, -1), 0, 1) for block in blocks]
    return lay_places(blocks, 2).reshape(2 * shard_size() * rows, -1)


def unspread(gradient, cuts, rows):
    span = gradient.shape[1]
    seq, column = lax.axis_index("seq"), column_index()
    view = gradient.reshape(2, TP, place_size(), rows, span)
    blocks = [
        lax.dynamic_index_in_dim(view, place_index() ^ entry, 2, keepdims=False).reshape(-1, span)
        for entry in range(place_size())
    ]
    total = scatter_places(blocks).astype(BF).reshape(2, TP, rows, span)
    pieces = []
    for step in range(TP):
        piece = lax.dynamic_index_in_dim(total, (column - step) % TP, 1, keepdims=False)
        pieces.append(piece if step == 0 else rotate(piece, step))
    laid = turn_columns(pieces)
    mine = lax.dynamic_index_in_dim(laid, seq, 1, keepdims=False)
    other = flip(lax.dynamic_index_in_dim(laid, 1 - seq, 1, keepdims=False))
    both = ordered_pair(mine, other)
    both = both.reshape(2, TP, rows, cuts, span // cuts)
    return jnp.transpose(both, (3, 0, 1, 2, 4)).transpose(3, 0, 1, 2, 4).reshape(rows, -1)


def norm_scale(values):
    return lax.rsqrt(jnp.mean(values * values, axis=-1, keepdims=True) + NORM_EPS)


def positions_of(seg_row):
    labels = jnp.arange(NCONT + 1, dtype=jnp.int32)
    member = (seg_row[:, None] == labels[None, :]).astype(jnp.int32)
    counts = jnp.sum(member, axis=0)
    starts = jnp.cumsum(counts) - counts
    own_start = jnp.sum(member * starts[None, :], axis=1)
    places = jnp.arange(seg_row.shape[0], dtype=jnp.int32)
    return places - own_start + jnp.where(seg_row > 0, counts[0], 0)


def rotary(positions):
    half_size = HD // 2
    frequency = THETA ** (-(jnp.arange(half_size, dtype=F32) * (2.0 / HD)))
    angles = positions.astype(F32)[:, None] * frequency[None, :]
    angles = jnp.concatenate([angles, angles], axis=-1)
    return (jnp.cos(angles), jnp.sin(angles))


def turn_half(values):
    half_size = values.shape[-1] // 2
    return jnp.concatenate([-values[..., half_size:], values[..., :half_size]], axis=-1)


def rope(values, cosine, sine):
    return values * cosine[:, None, :] + turn_half(values) * sine[:, None, :]


def unrope(gradient, cosine, sine):
    return gradient * cosine[:, None, :] - turn_half(gradient * sine[:, None, :])


def norm_back(d_normed, inputs_f, factor_rows, gain_row):
    weighted = d_normed * gain_row
    d_inputs = factor_rows * weighted - inputs_f * factor_rows**3 * jnp.mean(
        weighted * inputs_f, axis=-1, keepdims=True
    )
    d_gain = jnp.sum(d_normed * inputs_f * factor_rows, axis=0)
    return (d_inputs, d_gain)


def square_sums(arrays):
    matrix_sums = jnp.stack([jnp.sum(entry * entry) for entry in arrays[:4]])
    return jnp.concatenate([matrix_sums, jnp.sum(arrays[4] * arrays[4], axis=1)])


def lamb_moments(masters, gradients, moment_ones, moment_twos):
    decay_rates = (DECAY, DECAY, DECAY, DECAY, 0.0)
    new_ones, new_twos, updates = ([], [], [])
    for master, gradient, old_one, old_two, decay_rate in zip(
        masters, gradients, moment_ones, moment_twos, decay_rates
    ):
        new_one = BETA1 * old_one + (1.0 - BETA1) * gradient
        new_two = BETA2 * old_two + (1.0 - BETA2) * gradient * gradient
        update = (
            new_one / (1.0 - BETA1**STEP) / (jnp.sqrt(new_two / (1.0 - BETA2**STEP)) + ADAM_EPS)
            + decay_rate * master
        )
        new_ones.append(new_one)
        new_twos.append(new_two)
        updates.append(update)
    return (new_ones, new_twos, updates)


def attend(normed, qkv_matrix, cosine, sine, allowed):
    projected = dot(normed, qkv_matrix).reshape(-1, GROUP + 2, HD)
    turned = jnp.concatenate(
        [rope(projected[:, : GROUP + 1], cosine, sine), projected[:, GROUP + 1 :]], axis=1
    ).astype(BF)
    queries, key_rows, value_rows = turned[:, :GROUP], turned[:, GROUP], turned[:, GROUP + 1]
    scores = jnp.einsum("qjd,kd->jqk", queries, key_rows, preferred_element_type=F32)
    scores = jnp.where(allowed[None], scores * HD ** (-0.5), MASKED)
    row_max = jnp.max(scores, axis=-1, keepdims=True)
    exponent = jnp.exp(scores - row_max)
    row_total = jnp.sum(exponent, axis=-1, keepdims=True)
    probs = (exponent / row_total).astype(BF)
    attended = jnp.einsum("jqk,kd->qjd", probs, value_rows, preferred_element_type=F32)
    return (turned, row_max + jnp.log(row_total), attended.astype(BF).reshape(-1, GROUP * HD))


def attend_back(turned, log_total, d_attended, cosine, sine, allowed):
    factor = HD ** (-0.5)
    queries, key_rows, value_rows = turned[:, :GROUP], turned[:, GROUP], turned[:, GROUP + 1]
    d_attended = d_attended.reshape(-1, GROUP, HD)
    scores = jnp.einsum("qjd,kd->jqk", queries, key_rows, preferred_element_type=F32)
    scores = jnp.where(allowed[None], scores * factor, MASKED)
    probs = jnp.exp(scores - log_total)
    d_probs = jnp.einsum("qjd,kd->jqk", d_attended, value_rows, preferred_element_type=F32)
    d_scores = (probs * (d_probs - jnp.sum(probs * d_probs, axis=-1, keepdims=True))).astype(BF)
    d_values = jnp.einsum("jqk,qjd->kd", probs.astype(BF), d_attended, preferred_element_type=F32)
    d_queries = jnp.einsum("jqk,kd->qjd", d_scores, key_rows, preferred_element_type=F32) * factor
    d_keys = jnp.einsum("jqk,qjd->kd", d_scores, queries, preferred_element_type=F32) * factor
    d_turned = jnp.concatenate([d_queries, d_keys[:, None], d_values[:, None]], axis=1)
    d_turned = d_turned.astype(BF).astype(F32)
    d_projected = jnp.concatenate(
        [unrope(d_turned[:, : GROUP + 1], cosine, sine), d_turned[:, GROUP + 1 :]], axis=1
    )
    return d_projected.astype(BF).reshape(-1, HEAD_COLS)


def shards(
    hidden_in,
    out_grad,
    segments,
    qkv_weight,
    out_weight,
    gateup_weight,
    down_weight,
    gain_weight,
    qkv_first,
    out_first,
    gateup_first,
    down_first,
    gain_first,
    qkv_second,
    out_second,
    gateup_second,
    down_second,
    gain_second,
):
    seq = lax.axis_index("seq")
    rows = qkv_weight.shape[0]
    tok_local = hidden_in.shape[1]
    group_tok = tok_local * lax.axis_size("seq")
    owner = seq * shard_size() + lax.axis_index("shard")
    chunk_ids = range(TP)

    gain_cols = gain_weight.shape[1]
    gains = lax.dynamic_update_slice(
        jnp.zeros((2, gain_cols * 2 * shard_size()), BF), gain_weight.astype(BF), (0, owner * gain_cols)
    )
    gains = butterfly(gains).astype(F32)
    qkv_matrix = full_rows(qkv_weight.astype(BF), 1)
    out_matrix = lay_places(gather_places(out_weight.astype(BF)), 0).reshape(GROUP * HD, -1)
    gateup_matrix = full_rows(gateup_weight.astype(BF), 2)
    down_matrix = lay_places(gather_places(down_weight.astype(BF)), 0).reshape(
        down_weight.shape[0] * place_size(), -1
    )
    unit = down_matrix.shape[0]

    x_own = hidden_in[0]
    x_chunks = gather_groups(x_own)
    og_own = out_grad[0]
    og_chunks = gather_groups(og_own)
    seg_chunks = [segments if k == 0 else rotate(segments, k) for k in chunk_ids]

    def local_order(values):
        return jnp.where(seq == 0, values, jnp.roll(values, -tok_local, axis=0))

    places = local_order(jnp.arange(group_tok, dtype=jnp.int32))
    turns, masks = [], []
    for k in chunk_ids:
        turns.append(rotary(local_order(positions_of(seg_chunks[k][0]))))
        ids = local_order(seg_chunks[k][0])
        masks.append(
            (places[None, :] <= places[:, None])
            & ((ids[None, :] == 0) | (ids[None, :] == ids[:, None]))
        )

    normed, turned, log_totals, attended, parts = [], [], [], [], []
    for k in chunk_ids:
        x_f = x_chunks[k].astype(F32)
        normed.append((x_f * norm_scale(x_f) * gains[0]).astype(BF))
        heads, log_total, rows_out = attend(normed[k], qkv_matrix, *turns[k], masks[k])
        turned.append(heads)
        log_totals.append(log_total)
        attended.append(rows_out)
        parts.append(dot(rows_out, out_matrix))
    x_local = x_own.astype(F32)
    middle = x_local + scatter_groups(parts)

    factor_two = norm_scale(middle)
    normed2 = gather_groups((middle * factor_two * gains[1]).astype(BF))
    activated, out_parts, d_gate_ups, d_parts = [], [], [], []
    for k in chunk_ids:
        gate_up = dot(normed2[k], gateup_matrix)
        gate, up = gate_up[:, :unit], gate_up[:, unit:]
        sigmoid = jax.nn.sigmoid(gate)
        activated.append((gate * sigmoid * up).astype(BF))
        out_parts.append(dot(activated[k], down_matrix))
        d_act = dot_last(og_chunks[k], down_matrix)
        d_gate = d_act * up * (sigmoid * (1.0 + gate * (1.0 - sigmoid)))
        d_up = d_act * (gate * sigmoid)
        d_gate_ups.append(jnp.concatenate([d_gate, d_up], axis=1).astype(BF))
        d_parts.append(dot_last(d_gate_ups[k], gateup_matrix))
    d_normed2 = scatter_groups(d_parts)
    d_mid_part, d_gain_two = norm_back(d_normed2, middle, factor_two, gains[1])
    d_middle = og_own.astype(F32) + d_mid_part
    output = (middle + scatter_groups(out_parts)).astype(BF)[None]

    og_all = jnp.concatenate(og_chunks, axis=0)
    grad_gateup = dot_rows(
        jnp.concatenate(normed2, axis=0), jnp.concatenate(d_gate_ups, axis=0)
    ).astype(BF)
    grad_gateup = unspread(grad_gateup, 2, rows).astype(F32)
    grad_down = dot_rows(jnp.concatenate(activated, axis=0), og_all).astype(BF)

    def to_places(gradient):
        view = gradient.reshape(place_size(), -1, gradient.shape[1])
        return scatter_places(
            [
                lax.dynamic_index_in_dim(view, place_index() ^ entry, 0, keepdims=False)
                for entry in range(place_size())
            ]
        )

    grad_down = to_places(grad_down)

    d_branch = gather_groups(d_middle.astype(BF))
    d_projected, in_parts = [], []
    for k in chunk_ids:
        d_attended = dot_last(d_branch[k], out_matrix).astype(BF)
        d_projected.append(
            attend_back(turned[k], log_totals[k], d_attended, *turns[k], masks[k])
        )
        in_parts.append(dot_last(d_projected[k], qkv_matrix))
    d_normed = scatter_groups(in_parts)
    factor_one = norm_scale(x_local)
    d_in_part, d_gain_one = norm_back(d_normed, x_local, factor_one, gains[0])
    input_grad = (d_middle + d_in_part).astype(BF)[None]
    grad_out = to_places(
        dot_rows(jnp.concatenate(attended, axis=0), jnp.concatenate(d_branch, axis=0)).astype(BF)
    )
    grad_qkv = dot_rows(
        jnp.concatenate(normed, axis=0), jnp.concatenate(d_projected, axis=0)
    ).astype(BF)
    grad_qkv = unspread(grad_qkv, 1, rows).astype(F32)
    grad_gain = lax.dynamic_slice_in_dim(
        butterfly(jnp.stack([d_gain_one, d_gain_two])), owner * gain_cols, gain_cols, 1
    )

    masters = (qkv_weight, out_weight, gateup_weight, down_weight, gain_weight)
    gradients = (grad_qkv, grad_out, grad_gateup, grad_down, grad_gain)
    new_ones, new_twos, updates = lamb_moments(
        masters,
        gradients,
        (qkv_first, out_first, gateup_first, down_first, gain_first),
        (qkv_second, out_second, gateup_second, down_second, gain_second),
    )
    norms = jnp.sqrt(butterfly(jnp.stack([square_sums(masters), square_sums(updates)])))
    ratios = norms[0] / norms[1]
    news = [masters[slot] - RATE * ratios[slot] * updates[slot] for slot in range(4)]
    news.append(masters[4] - RATE * ratios[4:6][:, None] * updates[4])
    copies = [entry.astype(BF) for entry in news]
    return (output, input_grad, *news, *new_ones, *new_twos, *copies, norms)


def solution(mesh):
    rows, columns = P(("seq", "shard"), None), P(None, ("seq", "shard"))
    tokens = P("shard", "seq", None)
    states = (rows, rows, rows, rows, columns)
    return jax.shard_map(
        shards,
        mesh=mesh,
        in_specs=(tokens, tokens, P("shard", None)) + states * 3,
        out_specs=(tokens, tokens) + states * 4 + (P(),),
        check_vma=False,
    )
```

```python
import jax
import jax.numpy as jnp
from jax import lax
from jax.sharding import PartitionSpec as P

HQ = 16
KVH = 8
HD = 128
FF = 8192
NCONT = 2
STEP = 10
TP = 4


NORM_EPS = 1e-05
THETA = 1000000.0
BETA1 = 0.9
BETA2 = 0.999
ADAM_EPS = 1e-06
DECAY = 0.01
RATE = 0.5
MASKED = -1e30
GROUP = HQ // KVH
HEAD_COLS = (GROUP + 2) * HD
BF = jnp.bfloat16
F32 = jnp.float32


def dot(left, right):
    return jnp.dot(left, right, preferred_element_type=F32)


def dot_rows(left, right):
    return lax.dot_general(left, right, (((0,), (0,)), ((), ())), preferred_element_type=F32)


def dot_last(left, right):
    return lax.dot_general(left, right, (((1,), (1,)), ((), ())), preferred_element_type=F32)


def after(values, *others):
    return lax.optimization_barrier((values, *others))[0]


def shard_size():
    return lax.axis_size("shard")


def place_size():
    return shard_size() // TP


def shard_bits(count):
    return count.bit_length() - 1


def place_index():
    return lax.axis_index("shard") % place_size()


def column_index():
    return lax.axis_index("shard") // place_size()


def corner_index():
    return lax.axis_index("shard") % TP


def line_index():
    return lax.axis_index("shard") // TP


def line_place(line):
    middles = place_size() // TP
    return line % middles * TP + line // middles


def rotate(values, steps):
    count, places = shard_size(), place_size()
    pairs = [
        (entry, ((entry // places - steps) % TP) * places + entry % places)
        for entry in range(count)
    ]
    return lax.ppermute(values, "shard", pairs)


def hop(values, change):
    return lax.ppermute(values, "shard", [(i, i ^ change) for i in range(shard_size())])


def swap_roles(values):
    count, places = shard_size(), place_size()

    def partner(entry):
        column, middle, corner = entry // places, entry % places // TP, entry % TP
        return (corner * (places // TP) + middle) * TP + column

    return lax.ppermute(values, "shard", [(i, partner(i)) for i in range(count)])


def flip(values):
    return lax.ppermute(values, "seq", [(0, 1), (1, 0)])


def butterfly(values):
    values = values + flip(values)
    for bit in range(shard_bits(shard_size())):
        values = values + hop(values, 1 << bit)
    return values


def from_column(values, step):
    return rotate(values, step) if step else values


def to_column(values, step):
    return rotate(values, -step) if step else values


def from_corner(values, step):
    return hop(values, step) if step else values


def gather_tokens(own, move):
    mine = [move(own, step) for step in range(TP)]
    return [jnp.concatenate([entry, flip(entry)], axis=0) for entry in mine]


def scatter_tokens(parts, move):
    half = parts[0].shape[0] // 2
    total = None
    for step in list(range(1, TP)) + [0]:
        part = parts[step]
        met = part[:half] + flip(part[half:].astype(BF)).astype(F32)
        if step:
            met = move(met.astype(BF), step).astype(F32)
        total = met if total is None else total + met
    return total


def gather_bits(own, low_bit, bits):
    blocks = {0: own}
    for bit in range(bits):
        for entry in list(blocks):
            blocks[entry | (1 << bit)] = hop(blocks[entry], 1 << (low_bit + bit))
    return [blocks[entry] for entry in range(1 << bits)]


def scatter_bits(blocks, low_bit, bits):
    sums = {entry: block.astype(F32) for entry, block in enumerate(blocks)}
    for bit in reversed(range(bits)):
        for entry in range(1 << bit):
            came = hop(sums.pop(entry | (1 << bit)).astype(BF), 1 << (low_bit + bit))
            sums[entry] = sums[entry] + came.astype(F32)
    return sums[0]


def gather_places(own):
    if place_size() == 4:
        rows = own.shape[0] // 2
        one, two = hop(own, 1), hop(own, 2)
        three = jnp.concatenate([hop(one[:rows], 2), hop(two[rows:], 1)], axis=0)
        blocks = [own, one, two, three]
    else:
        blocks = gather_bits(own, 0, shard_bits(place_size()))
    return [(place_index() ^ entry, block) for entry, block in enumerate(blocks)]


def scatter_places(block_of):
    blocks = [block_of(place_index() ^ entry) for entry in range(place_size())]
    if place_size() != 4:
        return scatter_bits(blocks, 0, shard_bits(place_size()))
    rows = blocks[0].shape[0] // 2
    zero, one, two, three = blocks
    one_b = one[rows:].astype(F32) + hop(three[rows:], 2).astype(F32)
    two_a = two[:rows].astype(F32) + hop(three[:rows], 1).astype(F32)
    upper = (
        zero[:rows].astype(F32)
        + hop(one[:rows], 1).astype(F32)
        + hop(two_a.astype(BF), 2).astype(F32)
    )
    lower = (
        zero[rows:].astype(F32)
        + hop(two[rows:], 2).astype(F32)
        + hop(one_b.astype(BF), 1).astype(F32)
    )
    return jnp.concatenate([upper, lower], axis=0)


def gather_lines(own):
    if place_size() == TP:
        return [((column_index() + k) % TP, from_column(own, k)) for k in range(TP)]
    blocks = gather_bits(own, 2, shard_bits(place_size()))
    return [(line_index() ^ entry, block) for entry, block in enumerate(blocks)]


def scatter_lines(block_of):
    if place_size() == TP:
        total = None
        for step in range(TP):
            came = to_column(block_of((column_index() + step) % TP), step).astype(F32)
            total = came if total is None else total + came
        return total
    return scatter_bits(
        [block_of(line_index() ^ entry) for entry in range(place_size())],
        2,
        shard_bits(place_size()),
    )


def lay(blocks, axis):
    shape = blocks[0][1].shape
    full = jnp.zeros(shape[:axis] + (len(blocks),) + shape[axis:], blocks[0][1].dtype)
    for index, block in blocks:
        starts = [0] * full.ndim
        starts[axis] = index
        full = lax.dynamic_update_slice(full, jnp.expand_dims(block, axis), starts)
    return full


def pick(values, index, axis):
    return lax.dynamic_index_in_dim(values, index, axis, keepdims=False)


def ordered_pair(mine, other):
    first = lax.axis_index("seq") == 0
    return jnp.stack([jnp.where(first, mine, other), jnp.where(first, other, mine)])


def turn_columns(blocks):
    twice = jnp.stack(blocks + blocks)
    return lax.dynamic_slice_in_dim(twice, (TP - column_index()) % TP, TP, 0)


def turn_corners(blocks):
    laid = jnp.stack(blocks)
    corner = corner_index()
    laid = jnp.where(corner % 2 == 1, laid[jnp.array([1, 0, 3, 2])], laid)
    return jnp.where(corner >= 2, laid[jnp.array([2, 3, 0, 1])], laid)


def columns_of(source, starts, size):
    return jnp.concatenate(
        [lax.dynamic_slice_in_dim(source, start, size, 1) for start in starts], axis=1
    )


def spread_qkv(weight):
    rows = weight.shape[0]
    seq, corner = lax.axis_index("seq"), corner_index()
    half = TP * HEAD_COLS
    mine = columns_of(weight, [seq * half], half)
    other = flip(columns_of(weight, [(1 - seq) * half], half))
    pair = ordered_pair(mine, other).reshape(2 * rows, half)
    blocks = [
        from_corner(columns_of(pair, [(corner ^ j) * HEAD_COLS], HEAD_COLS), j) for j in range(TP)
    ]
    return jnp.swapaxes(turn_corners(blocks).reshape(TP, 2, rows, HEAD_COLS), 0, 1)


def unspread_qkv(gradient, rows):
    view = gradient.reshape(2, place_size(), TP, rows, HEAD_COLS)
    total = scatter_lines(lambda line: pick(view, line, 1).reshape(-1, HEAD_COLS))
    total = total.astype(BF).reshape(2, TP, rows, HEAD_COLS)
    corner, seq = corner_index(), lax.axis_index("seq")
    laid = turn_corners([from_corner(pick(total, corner ^ j, 1), j) for j in range(TP)])
    both = ordered_pair(pick(laid, seq, 1), flip(pick(laid, 1 - seq, 1)))
    return jnp.concatenate([both[s, q] for s in range(2) for q in range(TP)], axis=1)


def spread_half(weight, half, hold):
    rows = weight.shape[0]
    seq, column = lax.axis_index("seq"), column_index()
    width = FF // (2 * TP * 2)

    def one_seq(index):
        starts = [
            gate * FF + (index * TP + c) * 2 * width + half * width
            for c in range(TP)
            for gate in range(2)
        ]
        return columns_of(weight, starts, width)

    pair = ordered_pair(one_seq(seq), flip(one_seq(1 - seq))).reshape(2 * rows, -1)
    pair = after(pair, *hold)
    blocks = [
        from_column(columns_of(pair, [((column - k) % TP) * 2 * width], 2 * width), k)
        for k in range(TP)
    ]
    return jnp.swapaxes(turn_columns(blocks).reshape(TP, 2, rows, 2 * width), 0, 1)


def collect_rows(block, blocks_of, axis):
    shape = block.shape
    blocks = [
        (index, came.reshape(shape)) for index, came in blocks_of(block.reshape(-1, shape[-1]))
    ]
    return lay(blocks, axis).reshape(-1, shape[-1])


def unspread_half_places(gradient, rows):
    span = gradient.shape[1]
    view = gradient.reshape(2, TP, place_size(), rows, span)
    total = scatter_places(lambda place: pick(view, place, 2).reshape(-1, span))
    return total.astype(BF).reshape(2, TP, rows, span)


def unspread_half_columns(total):
    column, seq = column_index(), lax.axis_index("seq")
    pieces = [from_column(pick(total, (column - k) % TP, 1), k) for k in range(TP)]
    laid = turn_columns(pieces)
    return ordered_pair(pick(laid, seq, 1), flip(pick(laid, 1 - seq, 1)))


def join_halves(halves):
    width = halves[0].shape[-1] // 2
    return jnp.concatenate(
        [
            halves[half][s, c, :, gate * width : (gate + 1) * width]
            for gate in range(2)
            for s in range(2)
            for c in range(TP)
            for half in range(2)
        ],
        axis=1,
    )


def norm_scale(values):
    return lax.rsqrt(jnp.mean(values * values, axis=-1, keepdims=True) + NORM_EPS)


def positions_of(seg_row):
    labels = jnp.arange(NCONT + 1, dtype=jnp.int32)
    member = (seg_row[:, None] == labels[None, :]).astype(jnp.int32)
    counts = jnp.sum(member, axis=0)
    starts = jnp.cumsum(counts) - counts
    own_start = jnp.sum(member * starts[None, :], axis=1)
    places = jnp.arange(seg_row.shape[0], dtype=jnp.int32)
    return places - own_start + jnp.where(seg_row > 0, counts[0], 0)


def rotary(positions):
    half_size = HD // 2
    frequency = THETA ** (-(jnp.arange(half_size, dtype=F32) * (2.0 / HD)))
    angles = positions.astype(F32)[:, None] * frequency[None, :]
    angles = jnp.concatenate([angles, angles], axis=-1)
    return (jnp.cos(angles), jnp.sin(angles))


def turn_half(values):
    half_size = values.shape[-1] // 2
    return jnp.concatenate([-values[..., half_size:], values[..., :half_size]], axis=-1)


def rope(values, cosine, sine):
    return values * cosine[:, None, :] + turn_half(values) * sine[:, None, :]


def unrope(gradient, cosine, sine):
    return gradient * cosine[:, None, :] - turn_half(gradient * sine[:, None, :])


def norm_back(d_normed, inputs_f, factor_rows, gain_row):
    weighted = d_normed * gain_row
    d_inputs = factor_rows * weighted - inputs_f * factor_rows**3 * jnp.mean(
        weighted * inputs_f, axis=-1, keepdims=True
    )
    d_gain = jnp.sum(d_normed * inputs_f * factor_rows, axis=0)
    return (d_inputs, d_gain)


def lamb_moments(masters, gradients, moment_ones, moment_twos):
    decay_rates = (DECAY, DECAY, DECAY, DECAY, 0.0)
    new_ones, new_twos, updates = ([], [], [])
    for master, gradient, old_one, old_two, decay_rate in zip(
        masters, gradients, moment_ones, moment_twos, decay_rates
    ):
        new_one = BETA1 * old_one + (1.0 - BETA1) * gradient
        new_two = BETA2 * old_two + (1.0 - BETA2) * gradient * gradient
        update = (
            new_one / (1.0 - BETA1**STEP) / (jnp.sqrt(new_two / (1.0 - BETA2**STEP)) + ADAM_EPS)
            + decay_rate * master
        )
        new_ones.append(new_one)
        new_twos.append(new_two)
        updates.append(update)
    return (new_ones, new_twos, updates)


def attend(normed, qkv_matrix, cosine, sine, allowed):
    projected = dot(normed, qkv_matrix).reshape(-1, GROUP + 2, HD)
    turned = jnp.concatenate(
        [rope(projected[:, : GROUP + 1], cosine, sine), projected[:, GROUP + 1 :]], axis=1
    ).astype(BF)
    queries, key_rows, value_rows = turned[:, :GROUP], turned[:, GROUP], turned[:, GROUP + 1]
    scores = jnp.einsum("qjd,kd->jqk", queries, key_rows, preferred_element_type=F32)
    scores = jnp.where(allowed[None], scores * HD ** (-0.5), MASKED)
    row_max = jnp.max(scores, axis=-1, keepdims=True)
    exponent = jnp.exp(scores - row_max)
    row_total = jnp.sum(exponent, axis=-1, keepdims=True)
    probs = (exponent / row_total).astype(BF)
    attended = jnp.einsum("jqk,kd->qjd", probs, value_rows, preferred_element_type=F32)
    return (turned, row_max + jnp.log(row_total), attended.astype(BF).reshape(-1, GROUP * HD))


def attend_back(turned, log_total, d_attended, cosine, sine, allowed):
    factor = HD ** (-0.5)
    queries, key_rows, value_rows = turned[:, :GROUP], turned[:, GROUP], turned[:, GROUP + 1]
    d_attended = d_attended.reshape(-1, GROUP, HD)
    scores = jnp.einsum("qjd,kd->jqk", queries, key_rows, preferred_element_type=F32)
    scores = jnp.where(allowed[None], scores * factor, MASKED)
    probs = jnp.exp(scores - log_total)
    d_probs = jnp.einsum("qjd,kd->jqk", d_attended, value_rows, preferred_element_type=F32)
    d_scores = (probs * (d_probs - jnp.sum(probs * d_probs, axis=-1, keepdims=True))).astype(BF)
    d_values = jnp.einsum("jqk,qjd->kd", probs.astype(BF), d_attended, preferred_element_type=F32)
    d_queries = jnp.einsum("jqk,kd->qjd", d_scores, key_rows, preferred_element_type=F32) * factor
    d_keys = jnp.einsum("jqk,qjd->kd", d_scores, queries, preferred_element_type=F32) * factor
    d_turned = jnp.concatenate([d_queries, d_keys[:, None], d_values[:, None]], axis=1)
    d_turned = d_turned.astype(BF).astype(F32)
    d_projected = jnp.concatenate(
        [unrope(d_turned[:, : GROUP + 1], cosine, sine), d_turned[:, GROUP + 1 :]], axis=1
    )
    return d_projected.astype(BF).reshape(-1, HEAD_COLS)


def shards(
    hidden_in,
    out_grad,
    segments,
    qkv_weight,
    out_weight,
    gateup_weight,
    down_weight,
    gain_weight,
    qkv_first,
    out_first,
    gateup_first,
    down_first,
    gain_first,
    qkv_second,
    out_second,
    gateup_second,
    down_second,
    gain_second,
):
    seq = lax.axis_index("seq")
    rows = qkv_weight.shape[0]
    tok_local = hidden_in.shape[1]
    group_tok = tok_local * lax.axis_size("seq")
    owner = seq * shard_size() + lax.axis_index("shard")
    chunk_ids = range(TP)

    gain_cols = gain_weight.shape[1]
    gains = lax.dynamic_update_slice(
        jnp.zeros((2, gain_cols * 2 * shard_size()), BF), gain_weight.astype(BF), (0, owner * gain_cols)
    )
    gains = butterfly(gains).astype(F32)
    x_own, og_own = hidden_in[0], out_grad[0]
    qkv_block = spread_qkv(qkv_weight.astype(BF))
    qkv_matrix = collect_rows(qkv_block, gather_lines, 1)
    x_chunks = gather_tokens(x_own, from_corner)
    seg_chunks = [from_corner(segments, j) for j in chunk_ids]
    out_block = after(swap_roles(out_weight.astype(BF)), qkv_matrix)
    out_matrix = lay(
        [(line_place(line), block) for line, block in gather_lines(out_block)], 0
    ).reshape(GROUP * HD, -1)

    down_own = after(down_weight.astype(BF), qkv_block, x_chunks[3])
    down_matrix = lay(gather_places(down_own), 0).reshape(
        down_weight.shape[0] * place_size(), -1
    )
    unit = down_matrix.shape[0]
    gateup_low = gateup_weight.astype(BF)
    gateup_blocks = [spread_half(gateup_low, 0, (out_matrix,))]
    gateup_blocks.append(spread_half(gateup_low, 1, (gateup_blocks[0],)))

    def local_order(values):
        return jnp.where(seq == 0, values, jnp.roll(values, -tok_local, axis=0))

    places = local_order(jnp.arange(group_tok, dtype=jnp.int32))
    turns, masks = [], []
    for k in chunk_ids:
        turns.append(rotary(local_order(positions_of(seg_chunks[k][0]))))
        ids = local_order(seg_chunks[k][0])
        masks.append(
            (places[None, :] <= places[:, None])
            & ((ids[None, :] == 0) | (ids[None, :] == ids[:, None]))
        )

    normed, turned, log_totals, attended, parts = [], [], [], [], []
    for k in chunk_ids:
        x_f = x_chunks[k].astype(F32)
        normed.append((x_f * norm_scale(x_f) * gains[0]).astype(BF))
        heads, log_total, rows_out = attend(normed[k], qkv_matrix, *turns[k], masks[k])
        turned.append(heads)
        log_totals.append(log_total)
        attended.append(rows_out)
        parts.append(after(dot(rows_out, out_matrix), down_matrix))
    x_local = x_own.astype(F32)
    middle = x_local + scatter_tokens(parts, from_corner)

    gateup_matrix = [collect_rows(after(gateup_blocks[0], middle), gather_places, 2)]
    gateup_matrix.append(
        collect_rows(after(gateup_blocks[1], gateup_matrix[0]), gather_places, 2)
    )
    factor_two = norm_scale(middle)
    normed2_own = (middle * factor_two * gains[1]).astype(BF)
    normed2 = jnp.concatenate(
        gather_tokens(after(normed2_own, gateup_blocks[1]), from_column), axis=0
    )
    og_all = jnp.concatenate(gather_tokens(after(og_own, normed2), from_column), axis=0)
    activated, d_gate_ups = [], []
    for half in range(2):
        width = unit // 2
        gate_up = dot(normed2, gateup_matrix[half])
        gate, up = gate_up[:, :width], gate_up[:, width:]
        sigmoid = jax.nn.sigmoid(gate)
        activated.append((gate * sigmoid * up).astype(BF))
        d_act = dot_last(og_all, down_matrix[half * width : (half + 1) * width])
        d_gate = d_act * up * (sigmoid * (1.0 + gate * (1.0 - sigmoid)))
        d_up = d_act * (gate * sigmoid)
        d_gate_ups.append(jnp.concatenate([d_gate, d_up], axis=1).astype(BF))
    activated = jnp.concatenate(activated, axis=1)

    def chunk_rows(values, k):
        return values[k * group_tok : (k + 1) * group_tok]

    d_parts = [
        dot_last(chunk_rows(d_gate_ups[0], k), gateup_matrix[0])
        + dot_last(chunk_rows(d_gate_ups[1], k), gateup_matrix[1])
        for k in chunk_ids
    ]
    d_normed2 = scatter_tokens(d_parts, to_column)
    d_mid_part, d_gain_two = norm_back(d_normed2, middle, factor_two, gains[1])
    d_middle = og_own.astype(F32) + d_mid_part

    def to_places(gradient):
        view = gradient.reshape(place_size(), -1, gradient.shape[1])
        return scatter_places(lambda place: pick(view, place, 0))

    grad_down = to_places(dot_rows(activated, og_all).astype(BF))
    grad_half_a = dot_rows(normed2, d_gate_ups[0]).astype(BF)
    grad_half_b = dot_rows(normed2, d_gate_ups[1]).astype(BF)
    total_a = unspread_half_places(after(grad_half_a, grad_down), rows)

    d_branch_own = after(d_middle.astype(BF), total_a)
    d_branch = gather_tokens(d_branch_own, from_corner)
    total_b = unspread_half_places(after(grad_half_b, d_branch[3]), rows)
    d_projected, in_parts = [], []
    for k in chunk_ids:
        d_attended = dot_last(d_branch[k], out_matrix).astype(BF)
        d_projected.append(
            attend_back(turned[k], log_totals[k], d_attended, *turns[k], masks[k])
        )
        in_parts.append(dot_last(d_projected[k], qkv_matrix))
    d_normed = scatter_tokens([after(part, total_b) for part in in_parts], from_corner)
    factor_one = norm_scale(x_local)
    d_in_part, d_gain_one = norm_back(d_normed, x_local, factor_one, gains[0])
    input_grad = (d_middle + d_in_part).astype(BF)[None]

    out_parts = [
        after(dot(chunk_rows(activated, k), down_matrix), d_normed2) for k in chunk_ids
    ]
    result = middle + scatter_tokens(out_parts, to_column)
    output = result.astype(BF)[None]
    halves = [unspread_half_columns(after(total_a, result))]
    grad_out = dot_rows(
        jnp.concatenate(attended, axis=0), jnp.concatenate(d_branch, axis=0)
    ).astype(BF)
    view = after(grad_out, halves[0]).reshape(place_size(), -1, grad_out.shape[1])
    grad_out = scatter_lines(lambda line: pick(view, line_place(line), 0))
    halves.append(unspread_half_columns(after(total_b, grad_out)))
    grad_out = swap_roles(grad_out.astype(BF)).astype(F32)
    grad_gateup = join_halves(halves).astype(F32)
    grad_qkv = dot_rows(
        jnp.concatenate(normed, axis=0), jnp.concatenate(d_projected, axis=0)
    ).astype(BF)
    grad_qkv = unspread_qkv(after(grad_qkv, halves[1]), rows).astype(F32)
    grad_gain = lax.dynamic_slice_in_dim(
        butterfly(jnp.stack([d_gain_one, d_gain_two])), owner * gain_cols, gain_cols, 1
    )

    masters = (qkv_weight, out_weight, gateup_weight, down_weight, gain_weight)
    gradients = (grad_qkv, grad_out, grad_gateup, grad_down, grad_gain)
    new_ones, new_twos, updates = lamb_moments(
        masters,
        gradients,
        (qkv_first, out_first, gateup_first, down_first, gain_first),
        (qkv_second, out_second, gateup_second, down_second, gain_second),
    )
    def squares(arrays):
        return jnp.stack([jnp.sum(entry * entry) for entry in arrays])

    def rows_squares(values):
        return jnp.sum(values * values, axis=1)

    early = jnp.stack([squares(masters[2:4]), squares(updates[2:4])])
    late = jnp.stack(
        [
            jnp.concatenate([squares(masters[:2]), rows_squares(masters[4])]),
            jnp.concatenate([squares(updates[:2]), rows_squares(updates[4])]),
        ]
    )
    early, late = jnp.sqrt(butterfly(early)), jnp.sqrt(butterfly(late))
    norms = jnp.concatenate([late[:, :2], early, late[:, 2:]], axis=1)
    early, late = early[0] / early[1], late[0] / late[1]
    ratios = (late[0], late[1], early[0], early[1])
    news = [masters[slot] - RATE * ratios[slot] * updates[slot] for slot in range(4)]
    news.append(masters[4] - RATE * late[2:][:, None] * updates[4])
    copies = [entry.astype(BF) for entry in news]
    return (output, input_grad, *news, *new_ones, *new_twos, *copies, norms)


def solution(mesh):
    rows, columns = P(("seq", "shard"), None), P(None, ("seq", "shard"))
    tokens = P("shard", "seq", None)
    states = (rows, rows, rows, rows, columns)
    return jax.shard_map(
        shards,
        mesh=mesh,
        in_specs=(tokens, tokens, P("shard", None)) + states * 3,
        out_specs=(tokens, tokens) + states * 4 + (P(),),
        check_vma=False,
    )
```

```python
import jax
import jax.numpy as jnp
from jax import lax
from jax.sharding import PartitionSpec as P

HQ = 16
KVH = 8
HD = 128
FF = 8192
NCONT = 2
STEP = 10
TP = 4


NORM_EPS = 1e-05
THETA = 1000000.0
BETA1 = 0.9
BETA2 = 0.999
ADAM_EPS = 1e-06
DECAY = 0.01
RATE = 0.5
MASKED = -1e30
GROUP = HQ // KVH
HEAD_COLS = (GROUP + 2) * HD
BF = jnp.bfloat16
F32 = jnp.float32


def dot(left, right):
    return jnp.dot(left, right, preferred_element_type=F32)


def dot_rows(left, right):
    return lax.dot_general(left, right, (((0,), (0,)), ((), ())), preferred_element_type=F32)


def dot_last(left, right):
    return lax.dot_general(left, right, (((1,), (1,)), ((), ())), preferred_element_type=F32)


def after(values, *others):
    return lax.optimization_barrier((values, *others))[0]


def shard_size():
    return lax.axis_size("shard")


def place_size():
    return shard_size() // TP


def shard_bits(count):
    return count.bit_length() - 1


def place_index():
    return lax.axis_index("shard") % place_size()


def column_index():
    return lax.axis_index("shard") // place_size()


def corner_index():
    return lax.axis_index("shard") % TP


def line_index():
    return lax.axis_index("shard") // TP


def line_place(line):
    middles = place_size() // TP
    return line % middles * TP + line // middles


def rotate(values, steps):
    count, places = shard_size(), place_size()
    pairs = [
        (entry, ((entry // places - steps) % TP) * places + entry % places)
        for entry in range(count)
    ]
    return lax.ppermute(values, "shard", pairs)


def hop(values, change):
    return lax.ppermute(values, "shard", [(i, i ^ change) for i in range(shard_size())])


def swap_roles(values):
    count, places = shard_size(), place_size()

    def partner(entry):
        column, middle, corner = entry // places, entry % places // TP, entry % TP
        return (corner * (places // TP) + middle) * TP + column

    return lax.ppermute(values, "shard", [(i, partner(i)) for i in range(count)])


def flip(values):
    return lax.ppermute(values, "seq", [(0, 1), (1, 0)])


def butterfly(values):
    values = values + flip(values)
    for bit in range(shard_bits(shard_size())):
        values = values + hop(values, 1 << bit)
    return values


def from_column(values, step):
    return rotate(values, step) if step else values


def to_column(values, step):
    return rotate(values, -step) if step else values


def from_corner(values, step):
    return hop(values, step) if step else values


def both_halves(mine):
    mine = jnp.concatenate(mine, axis=0)
    return jnp.concatenate([mine, flip(mine)], axis=0)


def meet_halves(mine, other):
    met = mine + flip(other.astype(BF)).astype(F32)
    return jnp.split(met, TP)


def gather_bits(own, low_bit, bits):
    blocks = {0: own}
    for bit in range(bits):
        for entry in list(blocks):
            blocks[entry | (1 << bit)] = hop(blocks[entry], 1 << (low_bit + bit))
    return [blocks[entry] for entry in range(1 << bits)]


def scatter_bits(blocks, low_bit, bits):
    sums = {entry: block.astype(F32) for entry, block in enumerate(blocks)}
    for bit in reversed(range(bits)):
        for entry in range(1 << bit):
            came = hop(sums.pop(entry | (1 << bit)).astype(BF), 1 << (low_bit + bit))
            sums[entry] = sums[entry] + came.astype(F32)
    return sums[0]


def gather_places(own, hold=()):
    if place_size() == 4:
        rows = own.shape[0] // 2
        one, two = hop(own, 1), hop(own, 2)
        held_one, held_two = (after(one, *hold), after(two, *hold)) if hold else (one, two)
        three = jnp.concatenate([hop(held_one[:rows], 2), hop(held_two[rows:], 1)], axis=0)
        blocks = [own, one, two, three]
    else:
        blocks = gather_bits(own, 0, shard_bits(place_size()))
    return [(place_index() ^ entry, block) for entry, block in enumerate(blocks)]


def scatter_places(block_of):
    blocks = [block_of(place_index() ^ entry) for entry in range(place_size())]
    if place_size() != 4:
        return scatter_bits(blocks, 0, shard_bits(place_size()))
    rows = blocks[0].shape[0] // 2
    zero, one, two, three = blocks
    came_a = hop(jnp.concatenate([one[:rows], three[:rows]], axis=0), 1)
    came_b = hop(jnp.concatenate([two[rows:], three[rows:]], axis=0), 2)
    two_a = (two[:rows].astype(F32) + came_a[rows:].astype(F32)).astype(BF)
    one_b = (one[rows:].astype(F32) + came_b[rows:].astype(F32)).astype(BF)
    upper = zero[:rows].astype(F32) + came_a[:rows].astype(F32) + hop(two_a, 2).astype(F32)
    lower = zero[rows:].astype(F32) + came_b[:rows].astype(F32) + hop(one_b, 1).astype(F32)
    return jnp.concatenate([upper, lower], axis=0)


def gather_lines(own):
    if place_size() == TP:
        return [((column_index() + k) % TP, from_column(own, k)) for k in range(TP)]
    blocks = gather_bits(own, 2, shard_bits(place_size()))
    return [(line_index() ^ entry, block) for entry, block in enumerate(blocks)]


def scatter_lines(block_of):
    if place_size() == TP:
        total = None
        for step in range(TP):
            came = to_column(block_of((column_index() + step) % TP), step).astype(F32)
            total = came if total is None else total + came
        return total
    return scatter_bits(
        [block_of(line_index() ^ entry) for entry in range(place_size())],
        2,
        shard_bits(place_size()),
    )


def lay(blocks, axis):
    shape = blocks[0][1].shape
    full = jnp.zeros(shape[:axis] + (len(blocks),) + shape[axis:], blocks[0][1].dtype)
    for index, block in blocks:
        starts = [0] * full.ndim
        starts[axis] = index
        full = lax.dynamic_update_slice(full, jnp.expand_dims(block, axis), starts)
    return full


def pick(values, index, axis):
    return lax.dynamic_index_in_dim(values, index, axis, keepdims=False)


def ordered_pair(mine, other):
    first = lax.axis_index("seq") == 0
    return jnp.stack([jnp.where(first, mine, other), jnp.where(first, other, mine)])


def turn_columns(blocks):
    twice = jnp.stack(blocks + blocks)
    return lax.dynamic_slice_in_dim(twice, (TP - column_index()) % TP, TP, 0)


def turn_corners(blocks):
    laid = jnp.stack(blocks)
    corner = corner_index()
    laid = jnp.where(corner % 2 == 1, laid[jnp.array([1, 0, 3, 2])], laid)
    return jnp.where(corner >= 2, laid[jnp.array([2, 3, 0, 1])], laid)


def columns_of(source, starts, size):
    return jnp.concatenate(
        [lax.dynamic_slice_in_dim(source, start, size, 1) for start in starts], axis=1
    )


def pair_qkv(weight):
    seq = lax.axis_index("seq")
    half = TP * HEAD_COLS
    mine = columns_of(weight, [seq * half], half)
    other = flip(columns_of(weight, [(1 - seq) * half], half))
    return ordered_pair(mine, other).reshape(-1, half)


def spread_qkv(pair):
    corner = corner_index()
    blocks = [
        from_corner(columns_of(pair, [(corner ^ j) * HEAD_COLS], HEAD_COLS), j) for j in range(TP)
    ]
    laid = turn_corners(blocks).reshape(TP, 2, pair.shape[0] // 2, HEAD_COLS)
    return jnp.swapaxes(laid, 0, 1)


def unspread_qkv(gradient, rows):
    view = gradient.reshape(2, place_size(), TP, rows, HEAD_COLS)
    total = scatter_lines(lambda line: pick(view, line, 1).reshape(-1, HEAD_COLS))
    total = total.astype(BF).reshape(2, TP, rows, HEAD_COLS)
    corner, seq = corner_index(), lax.axis_index("seq")
    laid = turn_corners([from_corner(pick(total, corner ^ j, 1), j) for j in range(TP)])
    both = ordered_pair(pick(laid, seq, 1), flip(pick(laid, 1 - seq, 1)))
    return jnp.concatenate([both[s, q] for s in range(2) for q in range(TP)], axis=1)


def pair_half(weight, half):
    seq = lax.axis_index("seq")
    width = FF // (2 * TP * 2)

    def one_seq(index):
        starts = [
            gate * FF + (index * TP + c) * 2 * width + half * width
            for c in range(TP)
            for gate in range(2)
        ]
        return columns_of(weight, starts, width)

    mine, other = one_seq(seq), flip(one_seq(1 - seq))
    return ordered_pair(mine, other).reshape(-1, mine.shape[1])


def spread_half(pair):
    column, span = column_index(), pair.shape[1] // TP
    blocks = [
        from_column(columns_of(pair, [((column - k) % TP) * span], span), k) for k in range(TP)
    ]
    laid = turn_columns(blocks).reshape(TP, 2, pair.shape[0] // 2, span)
    return jnp.swapaxes(laid, 0, 1)


def collect_rows(block, blocks_of, axis):
    shape = block.shape
    blocks = [
        (index, came.reshape(shape)) for index, came in blocks_of(block.reshape(-1, shape[-1]))
    ]
    return lay(blocks, axis).reshape(-1, shape[-1])


def unspread_half_places(gradient, rows):
    span = gradient.shape[1]
    view = gradient.reshape(2, TP, place_size(), rows, span)
    total = scatter_places(lambda place: pick(view, place, 2).reshape(-1, span))
    return total.astype(BF).reshape(2, TP, rows, span)


def unspread_half_columns(total):
    column, seq = column_index(), lax.axis_index("seq")
    pieces = [from_column(pick(total, (column - k) % TP, 1), k) for k in range(TP)]
    laid = turn_columns(pieces)
    return ordered_pair(pick(laid, seq, 1), flip(pick(laid, 1 - seq, 1)))


def join_halves(halves):
    width = halves[0].shape[-1] // 2
    return jnp.concatenate(
        [
            halves[half][s, c, :, gate * width : (gate + 1) * width]
            for gate in range(2)
            for s in range(2)
            for c in range(TP)
            for half in range(2)
        ],
        axis=1,
    )


def norm_scale(values):
    return lax.rsqrt(jnp.mean(values * values, axis=-1, keepdims=True) + NORM_EPS)


def positions_of(seg_row):
    labels = jnp.arange(NCONT + 1, dtype=jnp.int32)
    member = (seg_row[:, None] == labels[None, :]).astype(jnp.int32)
    counts = jnp.sum(member, axis=0)
    starts = jnp.cumsum(counts) - counts
    own_start = jnp.sum(member * starts[None, :], axis=1)
    places = jnp.arange(seg_row.shape[0], dtype=jnp.int32)
    return places - own_start + jnp.where(seg_row > 0, counts[0], 0)


def rotary(positions):
    half_size = HD // 2
    frequency = THETA ** (-(jnp.arange(half_size, dtype=F32) * (2.0 / HD)))
    angles = positions.astype(F32)[:, None] * frequency[None, :]
    angles = jnp.concatenate([angles, angles], axis=-1)
    return (jnp.cos(angles), jnp.sin(angles))


def turn_half(values):
    half_size = values.shape[-1] // 2
    return jnp.concatenate([-values[..., half_size:], values[..., :half_size]], axis=-1)


def rope(values, cosine, sine):
    return values * cosine[..., None, :] + turn_half(values) * sine[..., None, :]


def unrope(gradient, cosine, sine):
    return gradient * cosine[..., None, :] - turn_half(gradient * sine[..., None, :])


def norm_back(d_normed, inputs_f, factor_rows, gain_row):
    weighted = d_normed * gain_row
    d_inputs = factor_rows * weighted - inputs_f * factor_rows**3 * jnp.mean(
        weighted * inputs_f, axis=-1, keepdims=True
    )
    d_gain = jnp.sum(d_normed * inputs_f * factor_rows, axis=0)
    return (d_inputs, d_gain)


def lamb_moments(masters, gradients, moment_ones, moment_twos):
    decay_rates = (DECAY, DECAY, DECAY, DECAY, 0.0)
    new_ones, new_twos, updates = ([], [], [])
    for master, gradient, old_one, old_two, decay_rate in zip(
        masters, gradients, moment_ones, moment_twos, decay_rates
    ):
        new_one = BETA1 * old_one + (1.0 - BETA1) * gradient
        new_two = BETA2 * old_two + (1.0 - BETA2) * gradient * gradient
        update = (
            new_one / (1.0 - BETA1**STEP) / (jnp.sqrt(new_two / (1.0 - BETA2**STEP)) + ADAM_EPS)
            + decay_rate * master
        )
        new_ones.append(new_one)
        new_twos.append(new_two)
        updates.append(update)
    return (new_ones, new_twos, updates)


def by_group(values):
    laid = jnp.swapaxes(values.reshape(2, TP, -1, *values.shape[1:]), 0, 1)
    return laid.reshape(TP, -1, *values.shape[1:])


def by_half(values):
    laid = jnp.swapaxes(values.reshape(TP, 2, -1, *values.shape[2:]), 0, 1)
    return laid.reshape(-1, *values.shape[2:])


def attend(projected, cosine, sine, allowed):
    turned = jnp.concatenate(
        [rope(projected[:, :, : GROUP + 1], cosine, sine), projected[:, :, GROUP + 1 :]], axis=2
    ).astype(BF)
    queries, key_rows, value_rows = turned[:, :, :GROUP], turned[:, :, GROUP], turned[:, :, GROUP + 1]
    scores = jnp.einsum("gqjd,gkd->gjqk", queries, key_rows, preferred_element_type=F32)
    scores = jnp.where(allowed[:, None], scores * HD ** (-0.5), MASKED)
    row_max = jnp.max(scores, axis=-1, keepdims=True)
    exponent = jnp.exp(scores - row_max)
    row_total = jnp.sum(exponent, axis=-1, keepdims=True)
    probs = (exponent / row_total).astype(BF)
    attended = jnp.einsum("gjqk,gkd->gqjd", probs, value_rows, preferred_element_type=F32)
    return (turned, row_max + jnp.log(row_total), attended.astype(BF))


def attend_back(turned, log_total, d_attended, cosine, sine, allowed):
    factor = HD ** (-0.5)
    queries, key_rows, value_rows = turned[:, :, :GROUP], turned[:, :, GROUP], turned[:, :, GROUP + 1]
    scores = jnp.einsum("gqjd,gkd->gjqk", queries, key_rows, preferred_element_type=F32)
    scores = jnp.where(allowed[:, None], scores * factor, MASKED)
    probs = jnp.exp(scores - log_total)
    d_probs = jnp.einsum("gqjd,gkd->gjqk", d_attended, value_rows, preferred_element_type=F32)
    d_scores = (probs * (d_probs - jnp.sum(probs * d_probs, axis=-1, keepdims=True))).astype(BF)
    d_values = jnp.einsum("gjqk,gqjd->gkd", probs.astype(BF), d_attended, preferred_element_type=F32)
    d_queries = jnp.einsum("gjqk,gkd->gqjd", d_scores, key_rows, preferred_element_type=F32) * factor
    d_keys = jnp.einsum("gjqk,gqjd->gkd", d_scores, queries, preferred_element_type=F32) * factor
    d_turned = jnp.concatenate([d_queries, d_keys[:, :, None], d_values[:, :, None]], axis=2)
    d_turned = d_turned.astype(BF).astype(F32)
    d_projected = jnp.concatenate(
        [unrope(d_turned[:, :, : GROUP + 1], cosine, sine), d_turned[:, :, GROUP + 1 :]], axis=2
    )
    return d_projected.astype(BF)


def shards(
    hidden_in,
    out_grad,
    segments,
    qkv_weight,
    out_weight,
    gateup_weight,
    down_weight,
    gain_weight,
    qkv_first,
    out_first,
    gateup_first,
    down_first,
    gain_first,
    qkv_second,
    out_second,
    gateup_second,
    down_second,
    gain_second,
):
    seq = lax.axis_index("seq")
    rows = qkv_weight.shape[0]
    tok_local = hidden_in.shape[1]
    group_tok = tok_local * lax.axis_size("seq")
    owner = seq * shard_size() + lax.axis_index("shard")

    span = TP * tok_local

    def to_places(gradient):
        view = gradient.reshape(place_size(), -1, gradient.shape[1])
        return scatter_places(lambda place: pick(view, place, 0))

    x_own, og_own = hidden_in[0], out_grad[0]
    x_local = x_own.astype(F32)

    og_mine = [og_own, rotate(og_own, 1), None, rotate(og_own, 3)]
    x_mine = [from_corner(x_own, j) for j in range(TP)]
    seg_chunks = [from_corner(segments, j) for j in range(TP)]
    gain_cols = gain_weight.shape[1]
    gains = lax.dynamic_update_slice(
        jnp.zeros((2, gain_cols * 2 * shard_size()), BF), gain_weight.astype(BF), (0, owner * gain_cols)
    )
    gains = butterfly(gains).astype(F32)
    gateup_low = gateup_weight.astype(BF)
    pairs = [pair_half(gateup_low, 0), pair_half(gateup_low, 1)]
    qkv_pair = pair_qkv(qkv_weight.astype(BF))
    slot = (og_mine[1], og_mine[3], *x_mine[1:])

    half_0 = spread_half(after(pairs[0], *slot))
    qkv_block = spread_qkv(after(qkv_pair, *slot))
    out_block = swap_roles(after(out_weight.astype(BF), *slot))
    slot = (half_0, qkv_block, out_block)

    qkv_matrix = collect_rows(after(qkv_block, *slot), gather_lines, 1)
    gateup_0 = collect_rows(after(half_0, *slot), gather_places, 2)
    x_all = both_halves(x_mine)
    slot = (qkv_matrix, gateup_0)

    out_matrix = lay(
        [(line_place(line), block) for line, block in gather_lines(after(out_block, *slot))], 0
    ).reshape(GROUP * HD, -1)
    down_own = after(down_weight.astype(BF), *slot)
    down_blocks = gather_places(down_own, (out_matrix,))
    down_matrix = lay(down_blocks, 0).reshape(down_weight.shape[0] * place_size(), -1)
    unit = down_matrix.shape[0]

    def local_order(values):
        return jnp.where(seq == 0, values, jnp.roll(values, -tok_local, axis=0))

    places = local_order(jnp.arange(group_tok, dtype=jnp.int32))
    positions = jnp.stack([local_order(positions_of(entry[0])) for entry in seg_chunks])
    cosine, sine = rotary(positions.reshape(-1))
    cosine, sine = cosine.reshape(TP, group_tok, HD), sine.reshape(TP, group_tok, HD)
    ids = jnp.stack([local_order(entry[0]) for entry in seg_chunks])
    allowed = (places[None, None, :] <= places[None, :, None]) & (
        (ids[:, None, :] == 0) | (ids[:, None, :] == ids[:, :, None])
    )
    x_f = x_all.astype(F32)
    normed = (x_f * norm_scale(x_f) * gains[0]).astype(BF)
    projected = by_group(dot(normed, qkv_matrix)).reshape(TP, group_tok, GROUP + 2, HD)
    turned, log_total, attended = attend(projected, cosine, sine, allowed)
    attended = by_half(attended.reshape(TP, group_tok, GROUP * HD))
    met = meet_halves(dot(attended[:span], out_matrix), dot(attended[span:], out_matrix))
    slot = (out_matrix, down_blocks[1][1], down_blocks[2][1])

    half_1 = spread_half(after(pairs[1], *slot))
    sends = [after(entry.astype(BF), *slot) for entry in met]
    middle = x_local + met[0]
    for j in range(1, TP):
        middle = middle + from_corner(sends[j], j).astype(F32)
    factor_two = norm_scale(middle)
    slot = (half_1, middle)

    normed2_own = after((middle * factor_two * gains[1]).astype(BF), *slot)
    normed2_mine = [from_column(normed2_own, k) for k in range(TP)]
    gateup_1 = collect_rows(after(half_1, *slot), gather_places, 2)
    gateup_matrix = [gateup_0, gateup_1]
    slot = (*normed2_mine[1:], gateup_1)

    og_mine[2] = rotate(after(og_own, *slot), 2)
    normed2 = both_halves(normed2_mine)
    width = unit // 2
    gates, ups, activated = [], [], []
    for half in range(2):
        gate_up = dot(normed2, gateup_matrix[half])
        gates.append(gate_up[:, :width])
        ups.append(gate_up[:, width:])
        activated.append((jax.nn.silu(gates[half]) * ups[half]).astype(BF))
    activated = jnp.concatenate(activated, axis=1)
    out_met = meet_halves(dot(activated[:span], down_matrix), dot(activated[span:], down_matrix))
    og_all = both_halves(og_mine)
    slot = (og_all,)

    sends = [after(entry.astype(BF), *slot) for entry in out_met]
    result = middle + out_met[0]
    for k in range(1, TP):
        result = result + to_column(sends[k], k).astype(F32)
    output = result.astype(BF)[None]
    grad_down = to_places(dot_rows(activated, og_all).astype(BF))
    d_gate_ups = []
    for half in range(2):
        gate, up = gates[half], ups[half]
        sigmoid = jax.nn.sigmoid(gate)
        d_act = dot_last(og_all, down_matrix[half * width : (half + 1) * width])
        d_gate = d_act * up * (sigmoid * (1.0 + gate * (1.0 - sigmoid)))
        d_up = d_act * (gate * sigmoid)
        d_gate_ups.append(jnp.concatenate([d_gate, d_up], axis=1).astype(BF))

    def normed2_back(rows_of):
        return dot_last(d_gate_ups[0][rows_of], gateup_0) + dot_last(d_gate_ups[1][rows_of], gateup_1)

    grad_half_0 = dot_rows(normed2, d_gate_ups[0]).astype(BF)
    d_met = meet_halves(normed2_back(slice(None, span)), normed2_back(slice(span, None)))
    slot = (result, grad_down)

    sends = [after(entry.astype(BF), *slot) for entry in d_met]
    d_normed2 = d_met[0]
    for k in range(1, TP):
        d_normed2 = d_normed2 + to_column(sends[k], k).astype(F32)
    total_0 = unspread_half_places(after(grad_half_0, *slot), rows)
    grad_half_1 = dot_rows(normed2, d_gate_ups[1]).astype(BF)
    d_mid_part, d_gain_two = norm_back(d_normed2, middle, factor_two, gains[1])
    d_middle = og_own.astype(F32) + d_mid_part
    slot = (d_middle, total_0)

    d_branch_own = after(d_middle.astype(BF), *slot)
    d_branch_mine = [from_corner(d_branch_own, j) for j in range(TP)]
    laid_0 = unspread_half_columns(after(total_0, *slot))
    d_branch = both_halves(d_branch_mine)
    slot = (laid_0, d_branch)

    grad_out = after(dot_rows(attended, d_branch).astype(BF), *slot)
    grad_out = grad_out.reshape(place_size(), -1, grad_out.shape[1])
    grad_out = scatter_lines(lambda line: pick(grad_out, line_place(line), 0))
    total_1 = unspread_half_places(after(grad_half_1, *slot), rows)
    d_attended = by_group(dot_last(d_branch, out_matrix).astype(BF))
    d_attended = d_attended.reshape(TP, group_tok, GROUP, HD)
    d_projected = attend_back(turned, log_total, d_attended, cosine, sine, allowed)
    d_projected = by_half(d_projected.reshape(TP, group_tok, HEAD_COLS))
    in_met = meet_halves(
        dot_last(d_projected[:span], qkv_matrix), dot_last(d_projected[span:], qkv_matrix)
    )
    grad_qkv = dot_rows(normed, d_projected).astype(BF)
    slot = (grad_out, total_1)

    sends = [after(entry.astype(BF), *slot) for entry in in_met]
    d_normed = in_met[0]
    for j in range(1, TP):
        d_normed = d_normed + from_corner(sends[j], j).astype(F32)
    factor_one = norm_scale(x_local)
    d_in_part, d_gain_one = norm_back(d_normed, x_local, factor_one, gains[0])
    input_grad = (d_middle + d_in_part).astype(BF)[None]
    laid_1 = unspread_half_columns(after(total_1, *slot))
    grad_gateup = join_halves([laid_0, laid_1]).astype(F32)
    slot = (laid_1, d_normed)

    grad_qkv = unspread_qkv(after(grad_qkv, *slot), rows).astype(F32)
    grad_out = swap_roles(after(grad_out.astype(BF), *slot)).astype(F32)
    grad_gain = lax.dynamic_slice_in_dim(
        butterfly(jnp.stack([d_gain_one, d_gain_two])), owner * gain_cols, gain_cols, 1
    )

    masters = (qkv_weight, out_weight, gateup_weight, down_weight, gain_weight)
    gradients = (grad_qkv, grad_out, grad_gateup, grad_down, grad_gain)
    new_ones, new_twos, updates = lamb_moments(
        masters,
        gradients,
        (qkv_first, out_first, gateup_first, down_first, gain_first),
        (qkv_second, out_second, gateup_second, down_second, gain_second),
    )
    def squares(arrays):
        return jnp.stack([jnp.sum(entry * entry) for entry in arrays])

    def rows_squares(values):
        return jnp.sum(values * values, axis=1)

    early = jnp.stack([squares(masters[2:4]), squares(updates[2:4])])
    late = jnp.stack(
        [
            jnp.concatenate([squares(masters[:2]), rows_squares(masters[4])]),
            jnp.concatenate([squares(updates[:2]), rows_squares(updates[4])]),
        ]
    )
    early, late = jnp.sqrt(butterfly(early)), jnp.sqrt(butterfly(late))
    norms = jnp.concatenate([late[:, :2], early, late[:, 2:]], axis=1)
    early, late = early[0] / early[1], late[0] / late[1]
    ratios = (late[0], late[1], early[0], early[1])
    news = [masters[slot] - RATE * ratios[slot] * updates[slot] for slot in range(4)]
    news.append(masters[4] - RATE * late[2:][:, None] * updates[4])
    copies = [entry.astype(BF) for entry in news]
    return (output, input_grad, *news, *new_ones, *new_twos, *copies, norms)


def solution(mesh):
    rows, columns = P(("seq", "shard"), None), P(None, ("seq", "shard"))
    tokens = P("shard", "seq", None)
    states = (rows, rows, rows, rows, columns)
    return jax.shard_map(
        shards,
        mesh=mesh,
        in_specs=(tokens, tokens, P("shard", None)) + states * 3,
        out_specs=(tokens, tokens) + states * 4 + (P(),),
        check_vma=False,
    )
```

```python
import jax
import jax.numpy as jnp
from jax import lax
from jax.experimental import pallas as pl
from jax.experimental.pallas import tpu as pltpu
from jax.sharding import PartitionSpec as P

HQ = 16
KVH = 8
HD = 128
FF = 8192
NCONT = 2
STEP = 10
TP = 4


NORM_EPS = 1e-05
THETA = 1000000.0
BETA1 = 0.9
BETA2 = 0.999
ADAM_EPS = 1e-06
DECAY = 0.01
RATE = 0.5
MASKED = -1e30
GROUP = HQ // KVH
HEAD_COLS = (GROUP + 2) * HD
BF = jnp.bfloat16
F32 = jnp.float32


def dot(left, right):
    return jnp.dot(left, right, preferred_element_type=F32)


def dot_rows(left, right):
    return lax.dot_general(left, right, (((0,), (0,)), ((), ())), preferred_element_type=F32)


def dot_last(left, right):
    return lax.dot_general(left, right, (((1,), (1,)), ((), ())), preferred_element_type=F32)


def after(values, *others):
    return lax.optimization_barrier((values, *others))[0]


RECENT = []


def permute(values, axis, pairs):
    RECENT.append(lax.ppermute(values, axis, pairs))
    return RECENT[-1]


def recent():
    arrivals = tuple(RECENT)
    RECENT.clear()
    return arrivals


def shard_size():
    return lax.axis_size("shard")


def place_size():
    return shard_size() // TP


def shard_bits(count):
    return count.bit_length() - 1


def place_index():
    return lax.axis_index("shard") % place_size()


def column_index():
    return lax.axis_index("shard") // place_size()


def corner_index():
    return lax.axis_index("shard") % TP


def line_index():
    return lax.axis_index("shard") // TP


def line_place(line):
    middles = place_size() // TP
    return line % middles * TP + line // middles


def rotate(values, steps):
    count, places = shard_size(), place_size()
    pairs = [
        (entry, ((entry // places - steps) % TP) * places + entry % places)
        for entry in range(count)
    ]
    return permute(values, "shard", pairs)


def hop(values, change):
    return permute(values, "shard", [(i, i ^ change) for i in range(shard_size())])


def swap_roles(values):
    count, places = shard_size(), place_size()

    def partner(entry):
        column, middle, corner = entry // places, entry % places // TP, entry % TP
        return (corner * (places // TP) + middle) * TP + column

    return permute(values, "shard", [(i, partner(i)) for i in range(count)])


def flip(values):
    return permute(values, "seq", [(0, 1), (1, 0)])


def butterfly(values):
    values = values + flip(values)
    for bit in range(shard_bits(shard_size())):
        values = values + hop(values, 1 << bit)
    return values


def from_column(values, step):
    return rotate(values, step) if step else values


def to_column(values, step):
    return rotate(values, -step) if step else values


def from_corner(values, step):
    return hop(values, step) if step else values


def both_halves(mine):
    mine = jnp.concatenate(mine, axis=0)
    return jnp.concatenate([mine, flip(mine)], axis=0)


def meet_halves(mine, other):
    return jnp.split(mine + flip(other).astype(F32), TP)


def gather_bits(own, low_bit, bits):
    blocks = {0: own}
    for bit in range(bits):
        for entry in list(blocks):
            blocks[entry | (1 << bit)] = hop(blocks[entry], 1 << (low_bit + bit))
    return [blocks[entry] for entry in range(1 << bits)]


def scatter_bits(blocks, low_bit, bits):
    sums = {entry: block.astype(F32) for entry, block in enumerate(blocks)}
    for bit in reversed(range(bits)):
        for entry in range(1 << bit):
            came = hop(sums.pop(entry | (1 << bit)).astype(BF), 1 << (low_bit + bit))
            sums[entry] = sums[entry] + came.astype(F32)
    return sums[0]


def gather_places(own, hold=()):
    if place_size() == 4:
        rows = own.shape[0] // 2
        one, two = hop(own, 1), hop(own, 2)
        held_one, held_two = (after(one, *hold), after(two, *hold)) if hold else (one, two)
        three = jnp.concatenate([hop(held_one[:rows], 2), hop(held_two[rows:], 1)], axis=0)
        blocks = [own, one, two, three]
    else:
        blocks = gather_bits(own, 0, shard_bits(place_size()))
    return [(place_index() ^ entry, block) for entry, block in enumerate(blocks)]


def scatter_places(block_of, hold=()):
    blocks = [block_of(place_index() ^ entry) for entry in range(place_size())]
    if place_size() != 4:
        return scatter_bits(blocks, 0, shard_bits(place_size()))
    rows = blocks[0].shape[0] // 2
    zero, one, two, three = blocks
    came_a = hop(jnp.concatenate([one[:rows], three[:rows]], axis=0), 1)
    came_b = hop(jnp.concatenate([two[rows:], three[rows:]], axis=0), 2)
    two_a = (two[:rows].astype(F32) + came_a[rows:].astype(F32)).astype(BF)
    one_b = (one[rows:].astype(F32) + came_b[rows:].astype(F32)).astype(BF)
    if hold:
        two_a, one_b = after(two_a, *hold), after(one_b, *hold)
    upper = zero[:rows].astype(F32) + came_a[:rows].astype(F32) + hop(two_a, 2).astype(F32)
    lower = zero[rows:].astype(F32) + came_b[:rows].astype(F32) + hop(one_b, 1).astype(F32)
    return jnp.concatenate([upper, lower], axis=0)


def gather_lines(own):
    if place_size() == TP:
        return [((column_index() + k) % TP, from_column(own, k)) for k in range(TP)]
    blocks = gather_bits(own, 2, shard_bits(place_size()))
    return [(line_index() ^ entry, block) for entry, block in enumerate(blocks)]


def scatter_lines(block_of):
    if place_size() == TP:
        total = None
        for step in range(TP):
            came = to_column(block_of((column_index() + step) % TP), step).astype(F32)
            total = came if total is None else total + came
        return total
    return scatter_bits(
        [block_of(line_index() ^ entry) for entry in range(place_size())],
        2,
        shard_bits(place_size()),
    )


def lay(blocks, axis):
    shape = blocks[0][1].shape
    full = jnp.zeros(shape[:axis] + (len(blocks),) + shape[axis:], blocks[0][1].dtype)
    for index, block in blocks:
        starts = [0] * full.ndim
        starts[axis] = index
        full = lax.dynamic_update_slice(full, jnp.expand_dims(block, axis), starts)
    return full


def pick(values, index, axis):
    return lax.dynamic_index_in_dim(values, index, axis, keepdims=False)


def ordered_pair(mine, other):
    first = lax.axis_index("seq") == 0
    return jnp.stack([jnp.where(first, mine, other), jnp.where(first, other, mine)])


def turn_columns(blocks):
    twice = jnp.stack(blocks + blocks)
    return lax.dynamic_slice_in_dim(twice, (TP - column_index()) % TP, TP, 0)


def turn_corners(blocks):
    laid = jnp.stack(blocks)
    corner = corner_index()
    laid = jnp.where(corner % 2 == 1, laid[jnp.array([1, 0, 3, 2])], laid)
    return jnp.where(corner >= 2, laid[jnp.array([2, 3, 0, 1])], laid)


def columns_of(source, starts, size):
    return jnp.concatenate(
        [lax.dynamic_slice_in_dim(source, start, size, 1) for start in starts], axis=1
    )


def pair_qkv(weight):
    seq = lax.axis_index("seq")
    half = TP * HEAD_COLS
    mine = columns_of(weight, [seq * half], half)
    other = flip(columns_of(weight, [(1 - seq) * half], half))
    return ordered_pair(mine, other).reshape(-1, half)


def qkv_piece(pair, step):
    return columns_of(pair, [(corner_index() ^ step) * HEAD_COLS], HEAD_COLS)


def unspread_qkv(gradient, rows):
    view = gradient.reshape(2, place_size(), TP, rows, HEAD_COLS)
    total = scatter_lines(lambda line: pick(view, line, 1).reshape(-1, HEAD_COLS))
    total = total.astype(BF).reshape(2, TP, rows, HEAD_COLS)
    corner, seq = corner_index(), lax.axis_index("seq")
    laid = turn_corners([from_corner(pick(total, corner ^ j, 1), j) for j in range(TP)])
    both = ordered_pair(pick(laid, seq, 1), flip(pick(laid, 1 - seq, 1)))
    return jnp.concatenate([both[s, q] for s in range(2) for q in range(TP)], axis=1)


def pair_halves(weight):
    seq = lax.axis_index("seq")
    width = FF // (2 * TP * 2)

    def one_seq(index):
        starts = [
            gate * FF + (index * TP + c) * 2 * width + half * width
            for half in range(2)
            for c in range(TP)
            for gate in range(2)
        ]
        return columns_of(weight, starts, width)

    mine, other = one_seq(seq), flip(one_seq(1 - seq))
    pair = ordered_pair(mine, other).reshape(-1, mine.shape[1])
    return jnp.split(pair, 2, axis=1)


def spread_half(pair):
    column, span = column_index(), pair.shape[1] // TP
    blocks = [
        from_column(columns_of(pair, [((column - k) % TP) * span], span), k) for k in range(TP)
    ]
    laid = turn_columns(blocks).reshape(TP, 2, pair.shape[0] // 2, span)
    return jnp.swapaxes(laid, 0, 1)


def collect_rows(block, blocks_of, axis):
    shape = block.shape
    blocks = [
        (index, came.reshape(shape)) for index, came in blocks_of(block.reshape(-1, shape[-1]))
    ]
    return lay(blocks, axis).reshape(-1, shape[-1])


def unspread_half_places(gradient, rows, hold=()):
    span = gradient.shape[1]
    view = gradient.reshape(2, TP, place_size(), rows, span)
    total = scatter_places(lambda place: pick(view, place, 2).reshape(-1, span), hold)
    return total.astype(BF).reshape(2, TP, rows, span)


def unspread_half_columns(total):
    column, seq = column_index(), lax.axis_index("seq")
    pieces = [from_column(pick(total, (column - k) % TP, 1), k) for k in range(TP)]
    laid = turn_columns(pieces)
    return ordered_pair(pick(laid, seq, 1), flip(pick(laid, 1 - seq, 1)))


def join_halves(halves):
    width = halves[0].shape[-1] // 2
    return jnp.concatenate(
        [
            halves[half][s, c, :, gate * width : (gate + 1) * width]
            for gate in range(2)
            for s in range(2)
            for c in range(TP)
            for half in range(2)
        ],
        axis=1,
    )


def norm_scale(values):
    return lax.rsqrt(jnp.mean(values * values, axis=-1, keepdims=True) + NORM_EPS)


def positions_of(seg_row):
    labels = jnp.arange(NCONT + 1, dtype=jnp.int32)
    member = (seg_row[:, None] == labels[None, :]).astype(jnp.int32)
    counts = jnp.sum(member, axis=0)
    starts = jnp.cumsum(counts) - counts
    own_start = jnp.sum(member * starts[None, :], axis=1)
    places = jnp.arange(seg_row.shape[0], dtype=jnp.int32)
    return places - own_start + jnp.where(seg_row > 0, counts[0], 0)


def rotary(positions):
    half_size = HD // 2
    frequency = THETA ** (-(jnp.arange(half_size, dtype=F32) * (2.0 / HD)))
    angles = positions.astype(F32)[:, None] * frequency[None, :]
    angles = jnp.concatenate([angles, angles], axis=-1)
    return (jnp.cos(angles), jnp.sin(angles))


def norm_back(d_normed, inputs_f, factor_rows, gain_row):
    weighted = d_normed * gain_row
    d_inputs = factor_rows * weighted - inputs_f * factor_rows**3 * jnp.mean(
        weighted * inputs_f, axis=-1, keepdims=True
    )
    d_gain = jnp.sum(d_normed * inputs_f * factor_rows, axis=0)
    return (d_inputs, d_gain)


def lamb_moments(masters, gradients, moment_ones, moment_twos):
    decay_rates = (DECAY, DECAY, DECAY, DECAY, 0.0)
    new_ones, new_twos, updates = ([], [], [])
    for master, gradient, old_one, old_two, decay_rate in zip(
        masters, gradients, moment_ones, moment_twos, decay_rates
    ):
        new_one = BETA1 * old_one + (1.0 - BETA1) * gradient
        new_two = BETA2 * old_two + (1.0 - BETA2) * gradient * gradient
        update = (
            new_one / (1.0 - BETA1**STEP) / (jnp.sqrt(new_two / (1.0 - BETA2**STEP)) + ADAM_EPS)
            + decay_rate * master
        )
        new_ones.append(new_one)
        new_twos.append(new_two)
        updates.append(update)
    return (new_ones, new_twos, updates)


SMALL = pl.CostEstimate(flops=10**9, bytes_accessed=1, transcendentals=0)
MIB = 1 << 20


def params(mebibytes):
    return pltpu.CompilerParams(vmem_limit_bytes=mebibytes * MIB)


def whole(shape):
    return pl.BlockSpec(shape, lambda step: (0,) * len(shape), pipeline_mode=pl.Buffered(1))


def at_group(shape, axis):
    return pl.BlockSpec(shape, lambda step: tuple(step if d == axis else 0 for d in range(len(shape))))


def half_sign():
    lane = lax.broadcasted_iota(jnp.int32, (1, HD), 1)
    return jnp.where(lane < HD // 2, -1.0, 1.0)


def scores_of(query, key_rows, allowed):
    return jnp.where(allowed, dot_last(query, key_rows) * HD ** (-0.5), MASKED)


def allowed_of(place_col, place_row, id_col, id_row):
    return (place_row <= place_col) & ((id_row == 0) | (id_row == id_col))


def attend_kernel(
    x_ref, gain_ref, qkv_ref, cos_ref, sin_ref, place_col, place_row, id_col, id_row,
    normed_ref, turned_ref, lse_ref, attended_ref,
):
    tokens = cos_ref.shape[1]
    x = x_ref[...].reshape(tokens, -1).astype(F32)
    scale = lax.rsqrt(jnp.mean(x * x, axis=-1, keepdims=True) + NORM_EPS)
    normed = (x * scale * gain_ref[...]).astype(BF)
    normed_ref[...] = normed.reshape(normed_ref.shape)
    projected = dot(normed, qkv_ref[...])
    cosine, sine = cos_ref[0], sin_ref[0] * half_sign()
    turned = []
    for head in range(GROUP + 2):
        values = projected[:, head * HD : (head + 1) * HD]
        if head <= GROUP:
            values = values * cosine + pltpu.roll(values, HD // 2, 1) * sine
        turned.append(values.astype(BF))
        turned_ref[0, :, head * HD : (head + 1) * HD] = turned[head]
    allowed = allowed_of(place_col[...], place_row[...], id_col[0], id_row[0])
    for head in range(GROUP):
        scores = scores_of(turned[head], turned[GROUP], allowed)
        row_max = jnp.max(scores, axis=-1, keepdims=True)
        exponent = jnp.exp(scores - row_max)
        row_total = jnp.sum(exponent, axis=-1, keepdims=True)
        lse_ref[0, head] = row_max + jnp.log(row_total)
        rows_out = dot((exponent / row_total).astype(BF), turned[GROUP + 1]).astype(BF)
        attended_ref[:, 0, :, head * HD : (head + 1) * HD] = rows_out.reshape(2, tokens // 2, HD)


def attend(x_all, gain, qkv_matrix, cosine, sine, marks):
    _, groups, half_tok, width = x_all.shape
    tokens = 2 * half_tok
    by_half = lambda columns: at_group((2, 1, half_tok, columns), 1)
    return pl.pallas_call(
        attend_kernel,
        grid=(groups,),
        in_specs=[
            by_half(width),
            whole((1, width)),
            whole((width, HEAD_COLS)),
            at_group((1, tokens, HD), 0),
            at_group((1, tokens, HD), 0),
            whole((tokens, 1)),
            whole((1, tokens)),
            at_group((1, tokens, 1), 0),
            at_group((1, 1, tokens), 0),
        ],
        out_specs=[
            by_half(width),
            at_group((1, tokens, HEAD_COLS), 0),
            at_group((1, GROUP, tokens, 1), 0),
            by_half(GROUP * HD),
        ],
        out_shape=[
            jax.ShapeDtypeStruct(x_all.shape, BF),
            jax.ShapeDtypeStruct((groups, tokens, HEAD_COLS), BF),
            jax.ShapeDtypeStruct((groups, GROUP, tokens, 1), F32),
            jax.ShapeDtypeStruct((2, groups, half_tok, GROUP * HD), BF),
        ],
        compiler_params=params(32),
        cost_estimate=SMALL,
    )(x_all, gain, qkv_matrix, cosine, sine, *marks)


def attend_back_kernel(
    branch_ref, out_ref, qkv_ref, turned_ref, lse_ref, cos_ref, sin_ref, place_col, place_row, id_col,
    id_row, projected_ref, mine_ref, other_ref,
):
    tokens = cos_ref.shape[1]
    factor = HD ** (-0.5)
    d_attended = dot_last(branch_ref[...].reshape(tokens, -1), out_ref[...]).astype(BF)
    turned = [turned_ref[0, :, head * HD : (head + 1) * HD] for head in range(GROUP + 2)]
    key_rows, value_rows = turned[GROUP], turned[GROUP + 1]
    allowed = allowed_of(place_col[...], place_row[...], id_col[0], id_row[0])
    cosine, sine, sign = cos_ref[0], sin_ref[0], half_sign()

    def unrope(values):
        values = values.astype(BF).astype(F32)
        return (values * cosine - sign * pltpu.roll(values * sine, HD // 2, 1)).astype(BF)

    d_keys = d_values = None
    columns = []
    for head in range(GROUP):
        d_rows = d_attended[:, head * HD : (head + 1) * HD]
        probs = jnp.exp(scores_of(turned[head], key_rows, allowed) - lse_ref[0, head])
        d_probs = dot_last(d_rows, value_rows)
        row_sum = jnp.sum(probs * d_probs, axis=-1, keepdims=True)
        d_scores = (probs * (d_probs - row_sum)).astype(BF)
        columns.append(unrope(dot(d_scores, key_rows) * factor))
        key_part = dot_rows(d_scores, turned[head]) * factor
        value_part = dot_rows(probs.astype(BF), d_rows)
        d_keys = key_part if d_keys is None else d_keys + key_part
        d_values = value_part if d_values is None else d_values + value_part
    columns.append(unrope(d_keys))
    columns.append(d_values.astype(BF))
    projected = jnp.concatenate(columns, axis=1)
    projected_ref[...] = projected.reshape(projected_ref.shape)
    d_normed = dot_last(projected, qkv_ref[...])
    mine_ref[0] = d_normed[: tokens // 2]
    other_ref[0] = d_normed[tokens // 2 :].astype(BF)


def attend_back(d_branch, out_matrix, qkv_matrix, turned, lse, cosine, sine, marks):
    _, groups, half_tok, width = d_branch.shape
    tokens = 2 * half_tok
    return pl.pallas_call(
        attend_back_kernel,
        grid=(groups,),
        in_specs=[
            at_group((2, 1, half_tok, width), 1),
            whole((GROUP * HD, width)),
            whole((width, HEAD_COLS)),
            at_group((1, tokens, HEAD_COLS), 0),
            at_group((1, GROUP, tokens, 1), 0),
            at_group((1, tokens, HD), 0),
            at_group((1, tokens, HD), 0),
            whole((tokens, 1)),
            whole((1, tokens)),
            at_group((1, tokens, 1), 0),
            at_group((1, 1, tokens), 0),
        ],
        out_specs=[
            at_group((2, 1, half_tok, HEAD_COLS), 1),
            at_group((1, half_tok, width), 0),
            at_group((1, half_tok, width), 0),
        ],
        out_shape=[
            jax.ShapeDtypeStruct((2, groups, half_tok, HEAD_COLS), BF),
            jax.ShapeDtypeStruct((groups, half_tok, width), F32),
            jax.ShapeDtypeStruct((groups, half_tok, width), BF),
        ],
        compiler_params=params(32),
        cost_estimate=SMALL,
    )(d_branch, out_matrix, qkv_matrix, turned, lse, cosine, sine, *marks)


def half_specs(rows, columns, steps):
    first = pl.BlockSpec((rows, columns), lambda step: (jnp.minimum(step, steps // 2 - 1), 0))
    second = pl.BlockSpec((rows, columns), lambda step: (jnp.maximum(step - steps // 2, 0), 0))
    shapes = [
        jax.ShapeDtypeStruct((rows * steps // 2, columns), F32),
        jax.ShapeDtypeStruct((rows * steps // 2, columns), BF),
    ]
    return [first, second], shapes


def store_halves(values, mine_ref, other_ref):
    step, half = pl.program_id(0), pl.num_programs(0) // 2

    @pl.when(step < half)
    def _():
        mine_ref[...] = values

    @pl.when(step >= half)
    def _():
        other_ref[...] = values.astype(BF)


def partial_kernel(left_ref, right_ref, mine_ref, other_ref):
    store_halves(dot(left_ref[...], right_ref[...]), mine_ref, other_ref)


def partial_product(left, right):
    tokens, depth = left.shape
    rows, steps = tokens // 4, 4
    specs, shapes = half_specs(rows, right.shape[1], steps)
    return pl.pallas_call(
        partial_kernel,
        grid=(steps,),
        in_specs=[at_group((rows, depth), 0), whole(right.shape)],
        out_specs=specs,
        out_shape=shapes,
        compiler_params=params(32),
        cost_estimate=SMALL,
    )(left, right)


def forward_back_kernel(
    normed_ref, og_ref, first_ref, second_ref, down_ref,
    activated_ref, d_first_ref, d_second_ref, mine_ref, other_ref,
):
    width = first_ref.shape[1] // 2
    normed, og = normed_ref[...], og_ref[...]
    total = None
    for half, (matrix_ref, d_ref) in enumerate(((first_ref, d_first_ref), (second_ref, d_second_ref))):
        gate = dot(normed, matrix_ref[:, :width])
        up = dot(normed, matrix_ref[:, width:])
        d_act = dot_last(og, down_ref[half * width : (half + 1) * width])
        sigmoid = jax.nn.sigmoid(gate)
        silu = gate * sigmoid
        activated_ref[:, half * width : (half + 1) * width] = (silu * up).astype(BF)
        d_ref[:, :width] = (d_act * up * (sigmoid * (1.0 + gate * (1.0 - sigmoid)))).astype(BF)
        d_ref[:, width:] = (d_act * silu).astype(BF)
        back = dot_last(d_ref[...], matrix_ref[...])
        total = back if total is None else total + back
    store_halves(total, mine_ref, other_ref)


def forward_back(normed2, og_all, gateup_matrix, down_matrix):
    tokens, width = normed2.shape
    unit = down_matrix.shape[0]
    rows, steps = tokens // 4, 4
    specs, shapes = half_specs(rows, width, steps)
    return pl.pallas_call(
        forward_back_kernel,
        grid=(steps,),
        in_specs=[
            at_group((rows, width), 0),
            at_group((rows, width), 0),
            whole((width, unit)),
            whole((width, unit)),
            whole((unit, width)),
        ],
        out_specs=[at_group((rows, unit), 0)] * 3 + specs,
        out_shape=[jax.ShapeDtypeStruct((tokens, unit), BF)] * 3 + shapes,
        compiler_params=params(48),
        cost_estimate=SMALL,
    )(normed2, og_all, *gateup_matrix, down_matrix)


def gradient_kernel(left_ref, right_ref, out_ref):
    out_ref[...] = dot_rows(left_ref[...], right_ref[...]).astype(BF)


def gradient(left, right):
    tokens, rows = left.shape
    block = min(rows, 256)
    return pl.pallas_call(
        gradient_kernel,
        grid=(rows // block,),
        in_specs=[at_group((tokens, block), 1), whole(right.shape)],
        out_specs=at_group((block, right.shape[1]), 0),
        out_shape=jax.ShapeDtypeStruct((rows, right.shape[1]), BF),
        compiler_params=params(32),
        cost_estimate=SMALL,
    )(left, right)


def shards(
    hidden_in,
    out_grad,
    segments,
    qkv_weight,
    out_weight,
    gateup_weight,
    down_weight,
    gain_weight,
    qkv_first,
    out_first,
    gateup_first,
    down_first,
    gain_first,
    qkv_second,
    out_second,
    gateup_second,
    down_second,
    gain_second,
):
    seq = lax.axis_index("seq")
    rows = qkv_weight.shape[0]
    tok_local = hidden_in.shape[1]
    group_tok = tok_local * lax.axis_size("seq")
    owner = seq * shard_size() + lax.axis_index("shard")


    def to_places(values):
        view = values.reshape(place_size(), -1, values.shape[1])
        return scatter_places(lambda place: pick(view, place, 0))

    x_own, og_own = hidden_in[0], out_grad[0]
    x_local = x_own.astype(F32)
    recent()

    gain_cols, width = gain_weight.shape[1], x_own.shape[1]
    known = jnp.zeros((2 + shard_size() * group_tok // width, width), BF)
    known = lax.dynamic_update_slice(known, gain_weight.astype(BF), (0, owner * gain_cols))
    ids_own = jnp.where(seq == 0, segments, 0).astype(BF)
    per_row = width // group_tok
    shard = lax.axis_index("shard")
    known = lax.dynamic_update_slice(
        known, ids_own, (2 + shard // per_row, shard % per_row * group_tok)
    )
    known = butterfly(known)
    gains = known[:2].astype(F32)
    recent()
    og_mine = [from_column(og_own, k) for k in range(TP)]
    pairs = pair_halves(gateup_weight.astype(BF))
    qkv_pair = pair_qkv(qkv_weight.astype(BF))
    slot = recent()

    half_0 = spread_half(after(pairs[0], *slot))
    held = after(qkv_pair, *slot)
    loads = [
        jnp.concatenate([x_own, qkv_piece(held, j).reshape(tok_local, -1)], axis=1) for j in range(TP)
    ]
    loads = [from_corner(loads[j], j) for j in range(TP)]
    x_mine = [entry[:, :width] for entry in loads]
    qkv_block = turn_corners([entry[:, width:].reshape(-1, HEAD_COLS) for entry in loads])
    qkv_block = jnp.swapaxes(qkv_block.reshape(TP, 2, rows, HEAD_COLS), 0, 1)
    slot = recent()

    qkv_matrix = collect_rows(after(qkv_block, *slot), gather_lines, 1)
    gateup_0 = collect_rows(after(half_0, *slot), gather_places, 2)
    out_block = swap_roles(after(out_weight.astype(BF), *slot))
    ids = known[2:].reshape(-1, group_tok).astype(jnp.int32)
    places = jnp.arange(group_tok, dtype=jnp.int32)

    def local_order(values):
        return jnp.where(seq == 0, values, jnp.roll(values, -tok_local, axis=-1))

    ids = [pick(ids, shard ^ j, 0) for j in range(TP)]
    positions = jnp.stack([local_order(positions_of(entry)) for entry in ids])
    ids = jnp.stack([local_order(entry) for entry in ids])
    places = local_order(places)
    marks = (places[:, None], places[None, :], ids[:, :, None], ids[:, None, :])
    cosine, sine = rotary(positions.reshape(-1))
    cosine, sine = cosine.reshape(TP, group_tok, HD), sine.reshape(TP, group_tok, HD)
    slot = recent()

    out_matrix = lay(
        [(line_place(line), block) for line, block in gather_lines(after(out_block, *slot))], 0
    ).reshape(GROUP * HD, -1)
    x_all = both_halves([x_mine[0], *(after(entry, *slot) for entry in x_mine[1:])])
    x_came = RECENT[-1]
    down_blocks = gather_places(after(down_weight.astype(BF), *slot))
    down_matrix = lay(down_blocks, 0).reshape(down_weight.shape[0] * place_size(), -1)
    x_all = x_all.reshape(2, TP, tok_local, width)
    normed, turned, lse, attended = attend(x_all, gains[:1], qkv_matrix, cosine, sine, marks)
    normed = normed.reshape(-1, width)
    attended = attended.reshape(-1, GROUP * HD)
    og_all = both_halves([og_own, *(after(entry, x_came) for entry in og_mine[1:])])
    slot = (*recent(), attended)

    met = meet_halves(*partial_product(after(attended, *slot), out_matrix))
    slot = recent()
    sends = [entry.astype(BF) for entry in met]
    half_1 = spread_half(after(pairs[1], *slot))
    middle = x_local + met[0]
    for j in range(1, TP):
        middle = middle + from_corner(sends[j], j).astype(F32)
    factor_two = norm_scale(middle)
    slot = recent()

    normed2_own = after((middle * factor_two * gains[1]).astype(BF), *slot)
    normed2_mine = [from_column(normed2_own, k) for k in range(TP)]
    gateup_1 = collect_rows(after(half_1, *slot), gather_places, 2)
    normed2 = both_halves(normed2_mine)
    slot = recent()

    activated, d_gate_up_0, d_gate_up_1, d_mine, d_other = forward_back(
        after(normed2, *slot), og_all, (gateup_0, gateup_1), down_matrix
    )

    d_met = meet_halves(d_mine, d_other)
    slot = recent()
    sends = [entry.astype(BF) for entry in d_met[1:]]
    grad_half_0 = gradient(after(normed2, d_other), d_gate_up_0)
    total_0 = unspread_half_places(after(grad_half_0, *slot), rows)
    out_mine, out_other = partial_product(after(activated, *slot, grad_half_0), down_matrix)
    d_normed2 = d_met[0]
    for k in range(1, TP):
        came = after(to_column(sends[k - 1], k), out_other)
        d_normed2 = d_normed2 + came.astype(F32)
    d_mid_part, d_gain_two = norm_back(d_normed2, middle, factor_two, gains[1])
    d_middle = og_own.astype(F32) + d_mid_part
    slot = recent()

    d_branch_own = after(d_middle.astype(BF), *slot)
    d_branch_mine = [from_corner(d_branch_own, j) for j in range(TP)]
    laid_0 = unspread_half_columns(after(total_0, *slot, d_branch_own))
    grad_half_1 = gradient(after(normed2, *slot), d_gate_up_1)
    grad_down = gradient(after(activated, *slot), og_all)
    out_met = meet_halves(out_mine, after(out_other, *slot))
    slot = (*recent(), grad_half_1, grad_down)

    sends = [after(entry.astype(BF), *slot) for entry in out_met]
    result = middle + out_met[0]
    for k in range(1, TP):
        result = result + to_column(sends[k], k).astype(F32)
    output = result.astype(BF)[None]
    out_came = recent()
    d_branch = both_halves([after(entry, *slot) for entry in d_branch_mine])
    d_projected, in_mine, in_other = attend_back(
        d_branch.reshape(2, TP, tok_local, width),
        out_matrix,
        qkv_matrix,
        turned,
        lse,
        cosine,
        sine,
        marks,
    )
    d_projected = d_projected.reshape(-1, HEAD_COLS)
    grad_qkv = gradient(after(normed, in_other), d_projected)
    grad_out = gradient(attended, after(d_branch, in_other))
    in_met = meet_halves(in_mine.reshape(-1, width), in_other.reshape(-1, width))
    in_came = (*recent(), *out_came)
    total_1 = unspread_half_places(after(grad_half_1, *slot), rows, in_came)
    recent()
    slot = (*in_came, grad_qkv, grad_out)

    view = after(grad_out, *slot).reshape(place_size(), -1, width)
    grad_out = scatter_lines(lambda line: pick(view, line_place(line), 0))
    d_normed = in_met[0]
    for j in range(1, TP):
        d_normed = d_normed + from_corner(after(in_met[j].astype(BF), *slot), j).astype(F32)
    factor_one = norm_scale(x_local)
    d_in_part, d_gain_one = norm_back(d_normed, x_local, factor_one, gains[0])
    input_grad = (d_middle + d_in_part).astype(BF)[None]
    slot = recent()

    laid_1 = unspread_half_columns(after(total_1, *slot))
    grad_out = swap_roles(after(grad_out.astype(BF), *slot)).astype(F32)
    slot = recent()
    grad_gain = butterfly(after(jnp.stack([d_gain_one, d_gain_two]), *slot))
    grad_gain = lax.dynamic_slice_in_dim(grad_gain, owner * gain_cols, gain_cols, 1)
    grad_gateup = join_halves([laid_0, laid_1]).astype(F32)

    grad_down = to_places(after(grad_down, *slot))
    grad_qkv = unspread_qkv(after(grad_qkv, *slot), rows).astype(F32)

    masters = (qkv_weight, out_weight, gateup_weight, down_weight, gain_weight)
    gradients = (grad_qkv, grad_out, grad_gateup, grad_down, grad_gain)
    new_ones, new_twos, updates = lamb_moments(
        masters,
        gradients,
        (qkv_first, out_first, gateup_first, down_first, gain_first),
        (qkv_second, out_second, gateup_second, down_second, gain_second),
    )
    def squares(arrays):
        return jnp.stack([jnp.sum(entry * entry) for entry in arrays])

    def rows_squares(values):
        return jnp.sum(values * values, axis=1)

    early = jnp.stack([squares(masters[2:3]), squares(updates[2:3])])
    late_ones, late_twos = (
        jnp.concatenate([squares((entry[0], entry[1], entry[3])), rows_squares(entry[4])])
        for entry in (masters, updates)
    )
    early, late = jnp.sqrt(butterfly(early)), jnp.sqrt(butterfly(jnp.stack([late_ones, late_twos])))
    norms = jnp.concatenate([late[:, :2], early, late[:, 2:]], axis=1)
    early, late = early[0] / early[1], late[0] / late[1]
    ratios = (late[0], late[1], early[0], late[2])
    news = [masters[slot] - RATE * ratios[slot] * updates[slot] for slot in range(4)]
    news.append(masters[4] - RATE * late[3:][:, None] * updates[4])
    copies = [entry.astype(BF) for entry in news]
    recent()
    return (output, input_grad, *news, *new_ones, *new_twos, *copies, norms)


def solution(mesh):
    rows, columns = P(("seq", "shard"), None), P(None, ("seq", "shard"))
    tokens = P("shard", "seq", None)
    states = (rows, rows, rows, rows, columns)
    return jax.shard_map(
        shards,
        mesh=mesh,
        in_specs=(tokens, tokens, P("shard", None)) + states * 3,
        out_specs=(tokens, tokens) + states * 4 + (P(),),
        check_vma=False,
    )
```

```python
import jax
import jax.numpy as jnp
from jax import lax
from jax.experimental import pallas as pl
from jax.experimental.pallas import tpu as pltpu
from jax.sharding import PartitionSpec as P

HQ = 16
KVH = 8
HD = 128
FF = 8192
NCONT = 2
STEP = 10
TP = 4


NORM_EPS = 1e-05
THETA = 1000000.0
BETA1 = 0.9
BETA2 = 0.999
ADAM_EPS = 1e-06
DECAY = 0.01
RATE = 0.5
MASKED = -1e30
GROUP = HQ // KVH
HEAD_COLS = (GROUP + 2) * HD
BF = jnp.bfloat16
F32 = jnp.float32


def dot(left, right):
    return jnp.dot(left, right, preferred_element_type=F32)


def dot_rows(left, right):
    return lax.dot_general(left, right, (((0,), (0,)), ((), ())), preferred_element_type=F32)


def dot_last(left, right):
    return lax.dot_general(left, right, (((1,), (1,)), ((), ())), preferred_element_type=F32)


def after(values, *others):
    return lax.optimization_barrier((values, *others))[0]


RECENT = []


def permute(values, axis, pairs):
    RECENT.append(lax.ppermute(values, axis, pairs))
    return RECENT[-1]


def recent():
    arrivals = tuple(RECENT)
    RECENT.clear()
    return arrivals


def shard_size():
    return lax.axis_size("shard")


def place_size():
    return shard_size() // TP


def shard_bits(count):
    return count.bit_length() - 1


def place_index():
    return lax.axis_index("shard") % place_size()


def column_index():
    return lax.axis_index("shard") // place_size()


def corner_index():
    return lax.axis_index("shard") % TP


def line_index():
    return lax.axis_index("shard") // TP


def line_place(line):
    middles = place_size() // TP
    return line % middles * TP + line // middles


def rotate(values, steps):
    count, places = shard_size(), place_size()
    pairs = [
        (entry, ((entry // places - steps) % TP) * places + entry % places)
        for entry in range(count)
    ]
    return permute(values, "shard", pairs)


def hop(values, change):
    return permute(values, "shard", [(i, i ^ change) for i in range(shard_size())])


def swap_roles(values):
    count, places = shard_size(), place_size()

    def partner(entry):
        column, middle, corner = entry // places, entry % places // TP, entry % TP
        return (corner * (places // TP) + middle) * TP + column

    return permute(values, "shard", [(i, partner(i)) for i in range(count)])


def flip(values):
    return permute(values, "seq", [(0, 1), (1, 0)])


def butterfly(values):
    values = values + flip(values)
    for bit in range(shard_bits(shard_size())):
        values = values + hop(values, 1 << bit)
    return values


def from_column(values, step):
    return rotate(values, step) if step else values


def to_column(values, step):
    return rotate(values, -step) if step else values


def from_corner(values, step):
    return hop(values, step) if step else values


def both_halves(mine):
    mine = jnp.concatenate(mine, axis=0)
    return jnp.concatenate([mine, flip(mine)], axis=0)


def meet_halves(mine, other):
    return jnp.split(mine + flip(other).astype(F32), TP)


def gather_bits(own, low_bit, bits):
    blocks = {0: own}
    for bit in range(bits):
        for entry in list(blocks):
            blocks[entry | (1 << bit)] = hop(blocks[entry], 1 << (low_bit + bit))
    return [blocks[entry] for entry in range(1 << bits)]


def scatter_bits(blocks, low_bit, bits):
    sums = {entry: block.astype(F32) for entry, block in enumerate(blocks)}
    for bit in reversed(range(bits)):
        for entry in range(1 << bit):
            came = hop(sums.pop(entry | (1 << bit)).astype(BF), 1 << (low_bit + bit))
            sums[entry] = sums[entry] + came.astype(F32)
    return sums[0]


def gather_places(own):
    if place_size() == TP:
        blocks = [from_corner(own, j) for j in range(TP)]
    else:
        blocks = gather_bits(own, 0, shard_bits(place_size()))
    return [(place_index() ^ entry, block) for entry, block in enumerate(blocks)]


def scatter_places(block_of, hold=()):
    blocks = [block_of(place_index() ^ entry) for entry in range(place_size())]
    if place_size() != TP:
        return scatter_bits(blocks, 0, shard_bits(place_size()))
    blocks[3] = after(blocks[3], *hold)
    total = blocks[0].astype(F32)
    for j in range(1, TP):
        total = total + from_corner(blocks[j], j).astype(F32)
    return total


def gather_lines(own):
    if place_size() == TP:
        return [((column_index() + k) % TP, from_column(own, k)) for k in range(TP)]
    blocks = gather_bits(own, 2, shard_bits(place_size()))
    return [(line_index() ^ entry, block) for entry, block in enumerate(blocks)]


def scatter_lines(block_of):
    if place_size() == TP:
        total = None
        for step in range(TP):
            came = to_column(block_of((column_index() + step) % TP), step).astype(F32)
            total = came if total is None else total + came
        return total
    return scatter_bits(
        [block_of(line_index() ^ entry) for entry in range(place_size())],
        2,
        shard_bits(place_size()),
    )


def lay(blocks, axis):
    shape = blocks[0][1].shape
    full = jnp.zeros(shape[:axis] + (len(blocks),) + shape[axis:], blocks[0][1].dtype)
    for index, block in blocks:
        starts = [0] * full.ndim
        starts[axis] = index
        full = lax.dynamic_update_slice(full, jnp.expand_dims(block, axis), starts)
    return full


def pick(values, index, axis):
    return lax.dynamic_index_in_dim(values, index, axis, keepdims=False)


def ordered_pair(mine, other):
    first = lax.axis_index("seq") == 0
    return jnp.stack([jnp.where(first, mine, other), jnp.where(first, other, mine)])


def turn_columns(blocks):
    twice = jnp.stack(blocks + blocks)
    return lax.dynamic_slice_in_dim(twice, (TP - column_index()) % TP, TP, 0)


def turn_corners(blocks):
    laid = jnp.stack(blocks)
    corner = corner_index()
    laid = jnp.where(corner % 2 == 1, laid[jnp.array([1, 0, 3, 2])], laid)
    return jnp.where(corner >= 2, laid[jnp.array([2, 3, 0, 1])], laid)


def columns_of(source, starts, size):
    return jnp.concatenate(
        [lax.dynamic_slice_in_dim(source, start, size, 1) for start in starts], axis=1
    )


def pair_qkv(weight):
    seq = lax.axis_index("seq")
    half = TP * HEAD_COLS
    mine = columns_of(weight, [seq * half], half)
    other = flip(columns_of(weight, [(1 - seq) * half], half))
    return ordered_pair(mine, other).reshape(-1, half)


def qkv_piece(pair, step):
    return columns_of(pair, [(corner_index() ^ step) * HEAD_COLS], HEAD_COLS)


def unspread_qkv(gradient, rows):
    view = gradient.reshape(2, place_size(), TP, rows, HEAD_COLS)
    total = scatter_lines(lambda line: pick(view, line, 1).reshape(-1, HEAD_COLS))
    total = total.astype(BF).reshape(2, TP, rows, HEAD_COLS)
    corner, seq = corner_index(), lax.axis_index("seq")
    laid = turn_corners([from_corner(pick(total, corner ^ j, 1), j) for j in range(TP)])
    both = ordered_pair(pick(laid, seq, 1), flip(pick(laid, 1 - seq, 1)))
    return jnp.concatenate([both[s, q] for s in range(2) for q in range(TP)], axis=1)


def pair_halves(weight):
    seq = lax.axis_index("seq")
    width = FF // (2 * TP * 2)

    def one_seq(index):
        starts = [
            gate * FF + (index * TP + c) * 2 * width + half * width
            for c in range(TP)
            for half in range(2)
            for gate in range(2)
        ]
        return columns_of(weight, starts, width)

    mine, other = one_seq(seq), flip(one_seq(1 - seq))
    return ordered_pair(mine, other).reshape(-1, mine.shape[1])


def spread_halves(pair):
    column, span = column_index(), pair.shape[1] // TP
    blocks = [
        from_column(columns_of(pair, [((column - k) % TP) * span], span), k) for k in range(TP)
    ]
    laid = turn_columns(blocks).reshape(TP, 2, pair.shape[0] // 2, span)
    return [jnp.swapaxes(entry, 0, 1) for entry in jnp.split(laid, 2, axis=3)]


def collect_rows(block, blocks_of, axis):
    shape = block.shape
    blocks = [
        (index, came.reshape(shape)) for index, came in blocks_of(block.reshape(-1, shape[-1]))
    ]
    return lay(blocks, axis).reshape(-1, shape[-1])


def unspread_places(values, rows, hold=()):
    span = values.shape[1]
    view = values.reshape(2, TP, place_size(), rows, span)
    total = scatter_places(lambda place: pick(view, place, 2).reshape(-1, span), hold)
    return total.astype(BF).reshape(2, TP, rows, span)


def column_piece(total, step):
    return pick(total, (column_index() - step) % TP, 1)


def lay_columns(pieces):
    laid = turn_columns(pieces)
    seq = lax.axis_index("seq")
    return ordered_pair(pick(laid, seq, 1), flip(pick(laid, 1 - seq, 1)))


def join_halves(halves):
    width = halves[0].shape[-1] // 2
    return jnp.concatenate(
        [
            halves[half][s, c, :, gate * width : (gate + 1) * width]
            for gate in range(2)
            for s in range(2)
            for c in range(TP)
            for half in range(2)
        ],
        axis=1,
    )


def norm_scale(values):
    return lax.rsqrt(jnp.mean(values * values, axis=-1, keepdims=True) + NORM_EPS)


def positions_of(seg_row):
    labels = jnp.arange(NCONT + 1, dtype=jnp.int32)
    member = (seg_row[:, None] == labels[None, :]).astype(jnp.int32)
    counts = jnp.sum(member, axis=0)
    starts = jnp.cumsum(counts) - counts
    own_start = jnp.sum(member * starts[None, :], axis=1)
    places = jnp.arange(seg_row.shape[0], dtype=jnp.int32)
    return places - own_start + jnp.where(seg_row > 0, counts[0], 0)


def rotary(positions):
    half_size = HD // 2
    frequency = THETA ** (-(jnp.arange(half_size, dtype=F32) * (2.0 / HD)))
    angles = positions.astype(F32)[:, None] * frequency[None, :]
    angles = jnp.concatenate([angles, angles], axis=-1)
    return (jnp.cos(angles), jnp.sin(angles))


def norm_back(d_normed, inputs_f, factor_rows, gain_row):
    weighted = d_normed * gain_row
    d_inputs = factor_rows * weighted - inputs_f * factor_rows**3 * jnp.mean(
        weighted * inputs_f, axis=-1, keepdims=True
    )
    d_gain = jnp.sum(d_normed * inputs_f * factor_rows, axis=0)
    return (d_inputs, d_gain)


def lamb_moments(masters, gradients, moment_ones, moment_twos):
    decay_rates = (DECAY, DECAY, DECAY, DECAY, 0.0)
    new_ones, new_twos, updates = ([], [], [])
    for master, gradient, old_one, old_two, decay_rate in zip(
        masters, gradients, moment_ones, moment_twos, decay_rates
    ):
        new_one = BETA1 * old_one + (1.0 - BETA1) * gradient
        new_two = BETA2 * old_two + (1.0 - BETA2) * gradient * gradient
        update = (
            new_one / (1.0 - BETA1**STEP) / (jnp.sqrt(new_two / (1.0 - BETA2**STEP)) + ADAM_EPS)
            + decay_rate * master
        )
        new_ones.append(new_one)
        new_twos.append(new_two)
        updates.append(update)
    return (new_ones, new_twos, updates)


SMALL = pl.CostEstimate(flops=10**9, bytes_accessed=1, transcendentals=0)
MIB = 1 << 20


def params(mebibytes):
    return pltpu.CompilerParams(vmem_limit_bytes=mebibytes * MIB)


def whole(shape):
    return pl.BlockSpec(shape, lambda step: (0,) * len(shape), pipeline_mode=pl.Buffered(1))


def at_group(shape, axis):
    return pl.BlockSpec(shape, lambda step: tuple(step if d == axis else 0 for d in range(len(shape))))


def half_sign():
    lane = lax.broadcasted_iota(jnp.int32, (1, HD), 1)
    return jnp.where(lane < HD // 2, -1.0, 1.0)


def scores_of(query, key_rows, allowed):
    return jnp.where(allowed, dot_last(query, key_rows) * HD ** (-0.5), MASKED)


def allowed_of(place_col, place_row, id_col, id_row):
    return (place_row <= place_col) & ((id_row == 0) | (id_row == id_col))


def attend_kernel(
    x_ref, gain_ref, qkv_ref, cos_ref, sin_ref, place_col, place_row, id_col, id_row,
    normed_ref, turned_ref, lse_ref, attended_ref,
):
    tokens = cos_ref.shape[1]
    x = x_ref[...].reshape(tokens, -1).astype(F32)
    scale = lax.rsqrt(jnp.mean(x * x, axis=-1, keepdims=True) + NORM_EPS)
    normed = (x * scale * gain_ref[...]).astype(BF)
    normed_ref[...] = normed.reshape(normed_ref.shape)
    projected = dot(normed, qkv_ref[...])
    cosine, sine = cos_ref[0], sin_ref[0] * half_sign()
    turned = []
    for head in range(GROUP + 2):
        values = projected[:, head * HD : (head + 1) * HD]
        if head <= GROUP:
            values = values * cosine + pltpu.roll(values, HD // 2, 1) * sine
        turned.append(values.astype(BF))
        turned_ref[0, :, head * HD : (head + 1) * HD] = turned[head]
    allowed = allowed_of(place_col[...], place_row[...], id_col[0], id_row[0])
    for head in range(GROUP):
        scores = scores_of(turned[head], turned[GROUP], allowed)
        row_max = jnp.max(scores, axis=-1, keepdims=True)
        exponent = jnp.exp(scores - row_max)
        row_total = jnp.sum(exponent, axis=-1, keepdims=True)
        lse_ref[0, head] = row_max + jnp.log(row_total)
        rows_out = dot((exponent / row_total).astype(BF), turned[GROUP + 1]).astype(BF)
        attended_ref[:, 0, :, head * HD : (head + 1) * HD] = rows_out.reshape(2, tokens // 2, HD)


def attend(x_all, gain, qkv_matrix, cosine, sine, marks):
    _, groups, half_tok, width = x_all.shape
    tokens = 2 * half_tok
    by_half = lambda columns: at_group((2, 1, half_tok, columns), 1)
    return pl.pallas_call(
        attend_kernel,
        grid=(groups,),
        in_specs=[
            by_half(width),
            whole((1, width)),
            whole((width, HEAD_COLS)),
            at_group((1, tokens, HD), 0),
            at_group((1, tokens, HD), 0),
            whole((tokens, 1)),
            whole((1, tokens)),
            at_group((1, tokens, 1), 0),
            at_group((1, 1, tokens), 0),
        ],
        out_specs=[
            by_half(width),
            at_group((1, tokens, HEAD_COLS), 0),
            at_group((1, GROUP, tokens, 1), 0),
            by_half(GROUP * HD),
        ],
        out_shape=[
            jax.ShapeDtypeStruct(x_all.shape, BF),
            jax.ShapeDtypeStruct((groups, tokens, HEAD_COLS), BF),
            jax.ShapeDtypeStruct((groups, GROUP, tokens, 1), F32),
            jax.ShapeDtypeStruct((2, groups, half_tok, GROUP * HD), BF),
        ],
        compiler_params=params(32),
        cost_estimate=SMALL,
    )(x_all, gain, qkv_matrix, cosine, sine, *marks)


def attend_back_kernel(
    branch_ref, out_ref, qkv_ref, turned_ref, lse_ref, cos_ref, sin_ref, place_col, place_row, id_col,
    id_row, projected_ref, mine_ref, other_ref,
):
    tokens = cos_ref.shape[1]
    factor = HD ** (-0.5)
    d_attended = dot_last(branch_ref[...].reshape(tokens, -1), out_ref[...]).astype(BF)
    turned = [turned_ref[0, :, head * HD : (head + 1) * HD] for head in range(GROUP + 2)]
    key_rows, value_rows = turned[GROUP], turned[GROUP + 1]
    allowed = allowed_of(place_col[...], place_row[...], id_col[0], id_row[0])
    cosine, sine, sign = cos_ref[0], sin_ref[0], half_sign()

    def unrope(values):
        values = values.astype(BF).astype(F32)
        return (values * cosine - sign * pltpu.roll(values * sine, HD // 2, 1)).astype(BF)

    d_keys = d_values = None
    columns = []
    for head in range(GROUP):
        d_rows = d_attended[:, head * HD : (head + 1) * HD]
        probs = jnp.exp(scores_of(turned[head], key_rows, allowed) - lse_ref[0, head])
        d_probs = dot_last(d_rows, value_rows)
        row_sum = jnp.sum(probs * d_probs, axis=-1, keepdims=True)
        d_scores = (probs * (d_probs - row_sum)).astype(BF)
        columns.append(unrope(dot(d_scores, key_rows) * factor))
        key_part = dot_rows(d_scores, turned[head]) * factor
        value_part = dot_rows(probs.astype(BF), d_rows)
        d_keys = key_part if d_keys is None else d_keys + key_part
        d_values = value_part if d_values is None else d_values + value_part
    columns.append(unrope(d_keys))
    columns.append(d_values.astype(BF))
    projected = jnp.concatenate(columns, axis=1)
    projected_ref[...] = projected.reshape(projected_ref.shape)
    d_normed = dot_last(projected, qkv_ref[...])
    mine_ref[0] = d_normed[: tokens // 2]
    other_ref[0] = d_normed[tokens // 2 :].astype(BF)


def attend_back(d_branch, out_matrix, qkv_matrix, turned, lse, cosine, sine, marks):
    _, groups, half_tok, width = d_branch.shape
    tokens = 2 * half_tok
    return pl.pallas_call(
        attend_back_kernel,
        grid=(groups,),
        in_specs=[
            at_group((2, 1, half_tok, width), 1),
            whole((GROUP * HD, width)),
            whole((width, HEAD_COLS)),
            at_group((1, tokens, HEAD_COLS), 0),
            at_group((1, GROUP, tokens, 1), 0),
            at_group((1, tokens, HD), 0),
            at_group((1, tokens, HD), 0),
            whole((tokens, 1)),
            whole((1, tokens)),
            at_group((1, tokens, 1), 0),
            at_group((1, 1, tokens), 0),
        ],
        out_specs=[
            at_group((2, 1, half_tok, HEAD_COLS), 1),
            at_group((1, half_tok, width), 0),
            at_group((1, half_tok, width), 0),
        ],
        out_shape=[
            jax.ShapeDtypeStruct((2, groups, half_tok, HEAD_COLS), BF),
            jax.ShapeDtypeStruct((groups, half_tok, width), F32),
            jax.ShapeDtypeStruct((groups, half_tok, width), BF),
        ],
        compiler_params=params(32),
        cost_estimate=SMALL,
    )(d_branch, out_matrix, qkv_matrix, turned, lse, cosine, sine, *marks)


def half_specs(rows, columns, steps):
    first = pl.BlockSpec((rows, columns), lambda step: (jnp.minimum(step, steps // 2 - 1), 0))
    second = pl.BlockSpec((rows, columns), lambda step: (jnp.maximum(step - steps // 2, 0), 0))
    shapes = [
        jax.ShapeDtypeStruct((rows * steps // 2, columns), F32),
        jax.ShapeDtypeStruct((rows * steps // 2, columns), BF),
    ]
    return [first, second], shapes


def store_halves(values, mine_ref, other_ref):
    step, half = pl.program_id(0), pl.num_programs(0) // 2

    @pl.when(step < half)
    def _():
        mine_ref[...] = values

    @pl.when(step >= half)
    def _():
        other_ref[...] = values.astype(BF)


def partial_kernel(left_ref, right_ref, mine_ref, other_ref):
    store_halves(dot(left_ref[...], right_ref[...]), mine_ref, other_ref)


def partial_product(left, right):
    tokens, depth = left.shape
    rows, steps = tokens // 4, 4
    specs, shapes = half_specs(rows, right.shape[1], steps)
    return pl.pallas_call(
        partial_kernel,
        grid=(steps,),
        in_specs=[at_group((rows, depth), 0), whole(right.shape)],
        out_specs=specs,
        out_shape=shapes,
        compiler_params=params(32),
        cost_estimate=SMALL,
    )(left, right)


def forward_back_kernel(
    normed_ref, og_ref, first_ref, second_ref, down_ref,
    activated_ref, d_first_ref, d_second_ref, mine_ref, other_ref,
):
    width = first_ref.shape[1] // 2
    normed, og = normed_ref[...], og_ref[...]
    total = None
    for half, (matrix_ref, d_ref) in enumerate(((first_ref, d_first_ref), (second_ref, d_second_ref))):
        gate = dot(normed, matrix_ref[:, :width])
        up = dot(normed, matrix_ref[:, width:])
        d_act = dot_last(og, down_ref[half * width : (half + 1) * width])
        sigmoid = jax.nn.sigmoid(gate)
        silu = gate * sigmoid
        activated_ref[:, half * width : (half + 1) * width] = (silu * up).astype(BF)
        d_ref[:, :width] = (d_act * up * (sigmoid * (1.0 + gate * (1.0 - sigmoid)))).astype(BF)
        d_ref[:, width:] = (d_act * silu).astype(BF)
        back = dot_last(d_ref[...], matrix_ref[...])
        total = back if total is None else total + back
    store_halves(total, mine_ref, other_ref)


def forward_back(normed2, og_all, gateup_matrix, down_matrix):
    tokens, width = normed2.shape
    unit = down_matrix.shape[0]
    rows, steps = tokens // 4, 4
    specs, shapes = half_specs(rows, width, steps)
    return pl.pallas_call(
        forward_back_kernel,
        grid=(steps,),
        in_specs=[
            at_group((rows, width), 0),
            at_group((rows, width), 0),
            whole((width, unit)),
            whole((width, unit)),
            whole((unit, width)),
        ],
        out_specs=[at_group((rows, unit), 0)] * 3 + specs,
        out_shape=[jax.ShapeDtypeStruct((tokens, unit), BF)] * 3 + shapes,
        compiler_params=params(48),
        cost_estimate=SMALL,
    )(normed2, og_all, *gateup_matrix, down_matrix)


def gradient_kernel(left_ref, right_ref, out_ref):
    out_ref[...] = dot_rows(left_ref[...], right_ref[...]).astype(BF)


def gradient(left, right):
    tokens, rows = left.shape
    block = min(rows, 256)
    return pl.pallas_call(
        gradient_kernel,
        grid=(rows // block,),
        in_specs=[at_group((tokens, block), 1), whole(right.shape)],
        out_specs=at_group((block, right.shape[1]), 0),
        out_shape=jax.ShapeDtypeStruct((rows, right.shape[1]), BF),
        compiler_params=params(32),
        cost_estimate=SMALL,
    )(left, right)


def shards(
    hidden_in,
    out_grad,
    segments,
    qkv_weight,
    out_weight,
    gateup_weight,
    down_weight,
    gain_weight,
    qkv_first,
    out_first,
    gateup_first,
    down_first,
    gain_first,
    qkv_second,
    out_second,
    gateup_second,
    down_second,
    gain_second,
):
    seq = lax.axis_index("seq")
    rows = qkv_weight.shape[0]
    tok_local = hidden_in.shape[1]
    group_tok = tok_local * lax.axis_size("seq")
    span = TP * tok_local
    owner = seq * shard_size() + lax.axis_index("shard")


    def to_places(values):
        view = values.reshape(place_size(), -1, values.shape[1])
        return scatter_places(lambda place: pick(view, place, 0))

    x_own, og_own = hidden_in[0], out_grad[0]
    x_local = x_own.astype(F32)
    recent()

    og_mine = [og_own, from_column(og_own, 1), None, from_column(og_own, 3)]
    down_own = down_weight.astype(BF)
    if place_size() == TP:
        down_blocks = [down_own, from_corner(down_own, 1), from_corner(down_own, 2), None]
    out_block = swap_roles(out_weight.astype(BF))
    pair = pair_halves(gateup_weight.astype(BF))
    qkv_pair = pair_qkv(qkv_weight.astype(BF))
    slot = recent()

    half_0, half_1 = spread_halves(after(pair, *slot))
    width = x_own.shape[1]
    held = after(qkv_pair, *slot)
    loads = [
        jnp.concatenate([x_own, qkv_piece(held, j).reshape(tok_local, -1)], axis=1) for j in range(TP)
    ]
    loads = [from_corner(loads[j], j) for j in range(TP)]
    x_mine = [entry[:, :width] for entry in loads]
    qkv_block = turn_corners([entry[:, width:].reshape(-1, HEAD_COLS) for entry in loads])
    qkv_block = jnp.swapaxes(qkv_block.reshape(TP, 2, rows, HEAD_COLS), 0, 1)
    came = recent()
    gain_cols = gain_weight.shape[1]
    known = jnp.zeros((2 + shard_size() * group_tok // width, width), BF)
    known = lax.dynamic_update_slice(known, gain_weight.astype(BF), (0, owner * gain_cols))
    ids_own = jnp.where(seq == 0, segments, 0).astype(BF)
    per_row = width // group_tok
    shard = lax.axis_index("shard")
    known = lax.dynamic_update_slice(
        known, ids_own, (2 + shard // per_row, shard % per_row * group_tok)
    )
    known = butterfly(after(known, *slot))
    gains = known[:2].astype(F32)
    recent()
    slot = came

    qkv_matrix = collect_rows(after(qkv_block, *slot), gather_lines, 1)
    gateup_0 = collect_rows(after(half_0, *slot), gather_places, 2)
    ids = known[2:].reshape(-1, group_tok).astype(jnp.int32)
    places = jnp.arange(group_tok, dtype=jnp.int32)

    def local_order(values):
        return jnp.where(seq == 0, values, jnp.roll(values, -tok_local, axis=-1))

    ids = [pick(ids, shard ^ j, 0) for j in range(TP)]
    positions = jnp.stack([local_order(positions_of(entry)) for entry in ids])
    ids = jnp.stack([local_order(entry) for entry in ids])
    places = local_order(places)
    marks = (places[:, None], places[None, :], ids[:, :, None], ids[:, None, :])
    cosine, sine = rotary(positions.reshape(-1))
    cosine, sine = cosine.reshape(TP, group_tok, HD), sine.reshape(TP, group_tok, HD)
    slot = recent()

    if place_size() == TP:
        down_blocks[3] = from_corner(after(down_own, *slot), 3)
        down_blocks = [(place_index() ^ j, block) for j, block in enumerate(down_blocks)]
    else:
        down_blocks = gather_places(after(down_own, *slot))
    down_matrix = lay(down_blocks, 0).reshape(down_weight.shape[0] * place_size(), -1)
    out_matrix = lay(
        [(line_place(line), block) for line, block in gather_lines(after(out_block, *slot))], 0
    ).reshape(GROUP * HD, -1)
    x_all = both_halves([x_mine[0], *(after(entry, *slot) for entry in x_mine[1:])])
    x_all = x_all.reshape(2, TP, tok_local, width)
    normed, turned, lse, attended = attend(x_all, gains[:1], qkv_matrix, cosine, sine, marks)
    normed = normed.reshape(-1, width)
    attended = attended.reshape(-1, GROUP * HD)
    slot = (*recent(), attended)

    og_mine[2] = from_column(after(og_own, *slot), 2)
    og_near = jnp.concatenate([after(og_mine[k], *slot) for k in (0, 1, 3)], axis=0)
    og_near = (og_near, flip(og_near))
    met = meet_halves(*partial_product(after(attended, *slot), out_matrix))
    middle = x_local + met[0]
    for j in range(1, TP):
        middle = middle + from_corner(met[j].astype(BF), j).astype(F32)
    factor_two = norm_scale(middle)
    slot = recent()

    normed2_own = after((middle * factor_two * gains[1]).astype(BF), *slot)
    normed2_mine = [from_column(normed2_own, k) for k in range(TP)]
    gateup_1 = collect_rows(after(half_1, *slot), gather_places, 2)
    came = recent()
    normed2 = jnp.concatenate([after(entry, *came) for entry in normed2_mine], axis=0)
    met = flip(jnp.concatenate([normed2, og_mine[2]], axis=0))
    normed2 = jnp.concatenate([normed2, met[:span]], axis=0)
    og_all = [og_near[0][: 2 * tok_local], og_mine[2], og_near[0][2 * tok_local :]]
    og_all += [og_near[1][: 2 * tok_local], met[span:], og_near[1][2 * tok_local :]]
    og_all = jnp.concatenate(og_all, axis=0)
    slot = recent()

    activated, d_gate_up_0, d_gate_up_1, d_mine, d_other = forward_back(
        after(normed2, *slot), og_all, (gateup_0, gateup_1), down_matrix
    )

    d_met = meet_halves(d_mine, d_other)
    slot = recent()
    sends = [entry.astype(BF) for entry in d_met[1:]]
    grad_half_0 = gradient(after(normed2, d_other), d_gate_up_0)
    total_0 = unspread_places(after(grad_half_0, *slot), rows)
    out_mine, out_other = partial_product(after(activated, *slot, grad_half_0), down_matrix)
    d_normed2 = d_met[0]
    for k in range(1, TP):
        came = after(to_column(sends[k - 1], k), out_other)
        d_normed2 = d_normed2 + came.astype(F32)
    d_mid_part, d_gain_two = norm_back(d_normed2, middle, factor_two, gains[1])
    d_middle = og_own.astype(F32) + d_mid_part
    slot = recent()

    d_branch_own = after(d_middle.astype(BF), *slot)
    d_branch_mine = [from_corner(d_branch_own, j) for j in range(TP)]
    held = after(total_0, *slot, d_branch_own)
    laid_0 = lay_columns([from_column(column_piece(held, k), k) for k in range(TP)])
    grad_half_1 = gradient(after(normed2, *slot), d_gate_up_1)
    grad_down = gradient(after(activated, *slot), og_all)
    out_met = meet_halves(out_mine, after(out_other, *slot))
    slot = (*recent(), grad_half_1, grad_down)

    sends = [after(entry.astype(BF), *slot) for entry in out_met]
    result = middle + out_met[0]
    for k in range(1, TP):
        result = result + to_column(sends[k], k).astype(F32)
    output = result.astype(BF)[None]
    out_came = recent()
    total_1 = unspread_places(after(grad_half_1, *slot), rows, out_came)
    out_came = (*out_came, *recent()[:2])
    d_branch = both_halves([after(entry, *slot) for entry in d_branch_mine])
    d_projected, in_mine, in_other = attend_back(
        d_branch.reshape(2, TP, tok_local, width),
        out_matrix,
        qkv_matrix,
        turned,
        lse,
        cosine,
        sine,
        marks,
    )
    d_projected = d_projected.reshape(-1, HEAD_COLS)
    grad_qkv = gradient(after(normed, in_other), d_projected)
    grad_out = gradient(attended, after(d_branch, in_other))
    in_other = after(in_other.reshape(-1, width), *out_came)
    in_met = meet_halves(in_mine.reshape(-1, width), in_other)
    slot = (*recent(), *out_came, grad_qkv, grad_out)

    d_normed = in_met[0]
    for j in range(1, TP):
        d_normed = d_normed + from_corner(after(in_met[j].astype(BF), *slot), j).astype(F32)
    held = after(total_1, *slot)
    view = after(grad_out, *slot).reshape(place_size(), -1, width)
    if place_size() == TP:
        column, out_rows = column_index(), view.shape[1]
        loads = [
            jnp.concatenate(
                [pick(view, (column - k) % TP, 0), column_piece(held, k).reshape(-1, width)], axis=0
            )
            for k in range(TP)
        ]
        loads = [from_column(loads[k], k) for k in range(TP)]
        grad_out = sum(entry[:out_rows].astype(F32) for entry in loads)
        pieces = [entry[out_rows:].reshape(2, rows, -1) for entry in loads]
    else:
        grad_out = scatter_lines(lambda line: pick(view, line_place(line), 0))
        pieces = [from_column(column_piece(held, k), k) for k in range(TP)]
    factor_one = norm_scale(x_local)
    d_in_part, d_gain_one = norm_back(d_normed, x_local, factor_one, gains[0])
    input_grad = (d_middle + d_in_part).astype(BF)[None]
    slot = recent()
    laid_1 = lay_columns(pieces)
    grad_gateup = join_halves([laid_0, laid_1]).astype(F32)

    grad_qkv = unspread_qkv(after(grad_qkv, *slot), rows).astype(F32)
    grad_out = swap_roles(after(grad_out.astype(BF), *slot)).astype(F32)
    grad_down = to_places(after(grad_down, *slot))
    grad_gain = butterfly(after(jnp.stack([d_gain_one, d_gain_two]), *slot))
    grad_gain = lax.dynamic_slice_in_dim(grad_gain, owner * gain_cols, gain_cols, 1)

    masters = (qkv_weight, out_weight, gateup_weight, down_weight, gain_weight)
    gradients = (grad_qkv, grad_out, grad_gateup, grad_down, grad_gain)
    new_ones, new_twos, updates = lamb_moments(
        masters,
        gradients,
        (qkv_first, out_first, gateup_first, down_first, gain_first),
        (qkv_second, out_second, gateup_second, down_second, gain_second),
    )
    def squares(arrays):
        return jnp.stack([jnp.sum(entry * entry) for entry in arrays])

    def rows_squares(values):
        return jnp.sum(values * values, axis=1)

    early = jnp.stack([squares(masters[2:3]), squares(updates[2:3])])
    late_ones, late_twos = (
        jnp.concatenate([squares((entry[0], entry[1], entry[3])), rows_squares(entry[4])])
        for entry in (masters, updates)
    )
    early, late = jnp.sqrt(butterfly(early)), jnp.sqrt(butterfly(jnp.stack([late_ones, late_twos])))
    norms = jnp.concatenate([late[:, :2], early, late[:, 2:]], axis=1)
    early, late = early[0] / early[1], late[0] / late[1]
    ratios = (late[0], late[1], early[0], late[2])
    news = [masters[slot] - RATE * ratios[slot] * updates[slot] for slot in range(4)]
    news.append(masters[4] - RATE * late[3:][:, None] * updates[4])
    copies = [entry.astype(BF) for entry in news]
    recent()
    return (output, input_grad, *news, *new_ones, *new_twos, *copies, norms)


def solution(mesh):
    rows, columns = P(("seq", "shard"), None), P(None, ("seq", "shard"))
    tokens = P("shard", "seq", None)
    states = (rows, rows, rows, rows, columns)
    return jax.shard_map(
        shards,
        mesh=mesh,
        in_specs=(tokens, tokens, P("shard", None)) + states * 3,
        out_specs=(tokens, tokens) + states * 4 + (P(),),
        check_vma=False,
    )
```

```python
import jax
import jax.numpy as jnp
from jax import lax
from jax.experimental import pallas as pl
from jax.experimental.pallas import tpu as pltpu
from jax.sharding import PartitionSpec as P

HQ = 16
KVH = 8
HD = 128
FF = 8192
NCONT = 2
STEP = 10
TP = 4


NORM_EPS = 1e-05
THETA = 1000000.0
BETA1 = 0.9
BETA2 = 0.999
ADAM_EPS = 1e-06
DECAY = 0.01
RATE = 0.5
MASKED = -1e30
GROUP = HQ // KVH
HEAD_COLS = (GROUP + 2) * HD
BF = jnp.bfloat16
F32 = jnp.float32


def dot(left, right):
    return jnp.dot(left, right, preferred_element_type=F32)


def dot_rows(left, right):
    return lax.dot_general(left, right, (((0,), (0,)), ((), ())), preferred_element_type=F32)


def dot_last(left, right):
    return lax.dot_general(left, right, (((1,), (1,)), ((), ())), preferred_element_type=F32)


def after(values, *others):
    return lax.optimization_barrier((values, *others))[0]


RECENT = []


def permute(values, axis, pairs):
    RECENT.append(lax.ppermute(values, axis, pairs))
    return RECENT[-1]


def recent():
    arrivals = tuple(RECENT)
    RECENT.clear()
    return arrivals


def shard_size():
    return lax.axis_size("shard")


def place_size():
    return shard_size() // TP


def shard_bits(count):
    return count.bit_length() - 1


def place_index():
    return lax.axis_index("shard") % place_size()


def column_index():
    return lax.axis_index("shard") // place_size()


def corner_index():
    return lax.axis_index("shard") % TP


def line_index():
    return lax.axis_index("shard") // TP


def line_place(line):
    middles = place_size() // TP
    return line % middles * TP + line // middles


def rotate(values, steps):
    count, places = shard_size(), place_size()
    pairs = [
        (entry, ((entry // places - steps) % TP) * places + entry % places)
        for entry in range(count)
    ]
    return permute(values, "shard", pairs)


def hop(values, change):
    return permute(values, "shard", [(i, i ^ change) for i in range(shard_size())])


def swap_roles(values):
    count, places = shard_size(), place_size()

    def partner(entry):
        column, middle, corner = entry // places, entry % places // TP, entry % TP
        return (corner * (places // TP) + middle) * TP + column

    return permute(values, "shard", [(i, partner(i)) for i in range(count)])


def flip(values):
    return permute(values, "seq", [(0, 1), (1, 0)])


def butterfly(values):
    for bit in reversed(range(shard_bits(shard_size()))):
        values = values + hop(values, 1 << bit)
    return values + flip(values)


def from_column(values, step):
    return rotate(values, step) if step else values


def to_column(values, step):
    return rotate(values, -step) if step else values


def from_corner(values, step):
    return hop(values, step) if step else values


def both_halves(mine):
    mine = jnp.concatenate(mine, axis=0)
    return jnp.concatenate([mine, flip(mine)], axis=0)


def meet_halves(mine, other):
    return jnp.split(mine + flip(other).astype(F32), TP)


def gather_bits(own, low_bit, bits):
    blocks = {0: own}
    for bit in range(bits):
        for entry in list(blocks):
            blocks[entry | (1 << bit)] = hop(blocks[entry], 1 << (low_bit + bit))
    return [blocks[entry] for entry in range(1 << bits)]


def scatter_bits(blocks, low_bit, bits):
    sums = {entry: block.astype(F32) for entry, block in enumerate(blocks)}
    for bit in reversed(range(bits)):
        for entry in range(1 << bit):
            came = hop(sums.pop(entry | (1 << bit)).astype(BF), 1 << (low_bit + bit))
            sums[entry] = sums[entry] + came.astype(F32)
    return sums[0]


def gather_places(own):
    places = place_size()
    groups = [[column * places + place for place in range(places)] for column in range(TP)]
    return lax.all_gather(own, "shard", axis_index_groups=groups)


def scatter_places(block_of, hold=()):
    blocks = [block_of(place_index() ^ entry) for entry in range(place_size())]
    if place_size() != TP:
        return scatter_bits(blocks, 0, shard_bits(place_size()))
    blocks[3] = after(blocks[3], *hold)
    total = blocks[0].astype(F32)
    for j in range(1, TP):
        total = total + from_corner(blocks[j], j).astype(F32)
    return total


def gather_lines(own):
    if place_size() == TP:
        return [((column_index() + k) % TP, from_column(own, k)) for k in range(TP)]
    blocks = gather_bits(own, 2, shard_bits(place_size()))
    return [(line_index() ^ entry, block) for entry, block in enumerate(blocks)]


def scatter_lines(block_of):
    if place_size() == TP:
        total = None
        for step in range(TP):
            came = to_column(block_of((column_index() + step) % TP), step).astype(F32)
            total = came if total is None else total + came
        return total
    return scatter_bits(
        [block_of(line_index() ^ entry) for entry in range(place_size())],
        2,
        shard_bits(place_size()),
    )


def lay(blocks, axis):
    shape = blocks[0][1].shape
    full = jnp.zeros(shape[:axis] + (len(blocks),) + shape[axis:], blocks[0][1].dtype)
    for index, block in blocks:
        starts = [0] * full.ndim
        starts[axis] = index
        full = lax.dynamic_update_slice(full, jnp.expand_dims(block, axis), starts)
    return full


def pick(values, index, axis):
    return lax.dynamic_index_in_dim(values, index, axis, keepdims=False)


def ordered_pair(mine, other):
    first = lax.axis_index("seq") == 0
    return jnp.stack([jnp.where(first, mine, other), jnp.where(first, other, mine)])


def turn_columns(blocks):
    twice = jnp.stack(blocks + blocks)
    return lax.dynamic_slice_in_dim(twice, (TP - column_index()) % TP, TP, 0)


def turn_corners(blocks):
    laid = jnp.stack(blocks)
    corner = corner_index()
    laid = jnp.where(corner % 2 == 1, laid[jnp.array([1, 0, 3, 2])], laid)
    return jnp.where(corner >= 2, laid[jnp.array([2, 3, 0, 1])], laid)


def columns_of(source, starts, size):
    return jnp.concatenate(
        [lax.dynamic_slice_in_dim(source, start, size, 1) for start in starts], axis=1
    )


def pair_qkv(weight):
    seq = lax.axis_index("seq")
    half = TP * HEAD_COLS
    mine = columns_of(weight, [seq * half], half)
    other = flip(columns_of(weight, [(1 - seq) * half], half))
    return ordered_pair(mine, other).reshape(-1, half)


def qkv_piece(pair, step):
    return columns_of(pair, [(corner_index() ^ step) * HEAD_COLS], HEAD_COLS)


def ride(load, extra):
    columns = load.shape[1]
    count = -(-extra.size // (16 * columns)) * 16 * columns
    extra = jnp.pad(extra.reshape(-1).astype(BF), (0, count - extra.size))
    return jnp.concatenate([load, extra.reshape(-1, columns)], axis=0)


def alight(load, rows, shape):
    size = 1
    for entry in shape:
        size *= entry
    return load[:rows], load[rows:].reshape(-1)[:size].reshape(shape)


def unspread_qkv(gradient, rows, rider):
    view = gradient.reshape(2, place_size(), TP, rows, HEAD_COLS)
    total = scatter_lines(lambda line: pick(view, line, 1).reshape(-1, HEAD_COLS))
    total = total.astype(BF).reshape(2, TP, rows, HEAD_COLS)
    corner, seq = corner_index(), lax.axis_index("seq")
    count = rider.shape[-1]
    loads = [
        ride(pick(total, corner ^ j, 1).reshape(-1, HEAD_COLS), pick(rider, corner ^ j, 2))
        for j in range(TP)
    ]
    loads = [alight(from_corner(loads[j], j), 2 * rows, (2, 2, count)) for j in range(TP)]
    laid = turn_corners([load.reshape(2, rows, HEAD_COLS) for load, _ in loads])
    rider = sum(extra.astype(F32) for _, extra in loads)
    load = ride(pick(laid, 1 - seq, 1).reshape(-1, HEAD_COLS), pick(rider, 1 - seq, 1))
    other, extra = alight(flip(load), TP * rows, (2, count))
    rider = pick(rider, seq, 1) + extra.astype(F32)
    both = ordered_pair(pick(laid, seq, 1), other.reshape(TP, rows, HEAD_COLS))
    return jnp.concatenate([both[s, q] for s in range(2) for q in range(TP)], axis=1), rider


def pair_halves(weight):
    seq = lax.axis_index("seq")
    width = FF // (2 * TP * 2)

    def one_seq(index):
        starts = [
            gate * FF + (index * TP + c) * 2 * width + half * width
            for c in range(TP)
            for half in range(2)
            for gate in range(2)
        ]
        return columns_of(weight, starts, width)

    mine, other = one_seq(seq), flip(one_seq(1 - seq))
    return ordered_pair(mine, other).reshape(-1, mine.shape[1])


def spread_halves(pair):
    column, span = column_index(), pair.shape[1] // TP
    blocks = [
        from_column(columns_of(pair, [((column - k) % TP) * span], span), k) for k in range(TP)
    ]
    laid = turn_columns(blocks).reshape(TP, 2, pair.shape[0] // 2, span)
    return jnp.swapaxes(laid, 0, 1)


def collect_lines(block):
    shape = block.shape
    blocks = [
        (index, came.reshape(shape)) for index, came in gather_lines(block.reshape(-1, shape[-1]))
    ]
    return lay(blocks, 1).reshape(-1, shape[-1])


def collect_places(block):
    full = gather_places(block.reshape(-1, block.shape[-1]))
    full = full.reshape(-1, *block.shape)
    return jnp.transpose(full, (1, 2, 0, 3, 4)).reshape(-1, block.shape[-1])


def unspread_places(values, rows, hold=()):
    span = values.shape[1]
    view = values.reshape(2, TP, place_size(), rows, span)
    total = scatter_places(lambda place: pick(view, place, 2).reshape(-1, span), hold)
    return total.astype(BF).reshape(2, TP, rows, span)


def column_piece(total, step):
    return pick(total, (column_index() - step) % TP, 1)


def lay_columns(pieces):
    laid = turn_columns(pieces)
    seq = lax.axis_index("seq")
    return ordered_pair(pick(laid, seq, 1), flip(pick(laid, 1 - seq, 1)))


def join_halves(halves):
    width = halves[0].shape[-1] // 2
    return jnp.concatenate(
        [
            halves[half][s, c, :, gate * width : (gate + 1) * width]
            for gate in range(2)
            for s in range(2)
            for c in range(TP)
            for half in range(2)
        ],
        axis=1,
    )


def norm_scale(values):
    return lax.rsqrt(jnp.mean(values * values, axis=-1, keepdims=True) + NORM_EPS)


def positions_of(seg_row):
    labels = jnp.arange(NCONT + 1, dtype=jnp.int32)
    member = (seg_row[:, None] == labels[None, :]).astype(jnp.int32)
    counts = jnp.sum(member, axis=0)
    starts = jnp.cumsum(counts) - counts
    own_start = jnp.sum(member * starts[None, :], axis=1)
    places = jnp.arange(seg_row.shape[0], dtype=jnp.int32)
    return places - own_start + jnp.where(seg_row > 0, counts[0], 0)


def rotary(positions):
    half_size = HD // 2
    frequency = THETA ** (-(jnp.arange(half_size, dtype=F32) * (2.0 / HD)))
    angles = positions.astype(F32)[:, None] * frequency[None, :]
    angles = jnp.concatenate([angles, angles], axis=-1)
    return (jnp.cos(angles), jnp.sin(angles))


def norm_back(d_normed, inputs_f, factor_rows, gain_row):
    weighted = d_normed * gain_row
    d_inputs = factor_rows * weighted - inputs_f * factor_rows**3 * jnp.mean(
        weighted * inputs_f, axis=-1, keepdims=True
    )
    d_gain = jnp.sum(d_normed * inputs_f * factor_rows, axis=0)
    return (d_inputs, d_gain)


def lamb_moments(masters, gradients, moment_ones, moment_twos):
    decay_rates = (DECAY, DECAY, DECAY, DECAY, 0.0)
    new_ones, new_twos, updates = ([], [], [])
    for master, gradient, old_one, old_two, decay_rate in zip(
        masters, gradients, moment_ones, moment_twos, decay_rates
    ):
        new_one = BETA1 * old_one + (1.0 - BETA1) * gradient
        new_two = BETA2 * old_two + (1.0 - BETA2) * gradient * gradient
        update = (
            new_one / (1.0 - BETA1**STEP) / (jnp.sqrt(new_two / (1.0 - BETA2**STEP)) + ADAM_EPS)
            + decay_rate * master
        )
        new_ones.append(new_one)
        new_twos.append(new_two)
        updates.append(update)
    return (new_ones, new_twos, updates)


SMALL = pl.CostEstimate(flops=10**9, bytes_accessed=1, transcendentals=0)
MIB = 1 << 20


def params(mebibytes):
    return pltpu.CompilerParams(vmem_limit_bytes=mebibytes * MIB)


def whole(shape):
    return pl.BlockSpec(shape, lambda step: (0,) * len(shape), pipeline_mode=pl.Buffered(1))


def at_group(shape, axis):
    return pl.BlockSpec(shape, lambda step: tuple(step if d == axis else 0 for d in range(len(shape))))


def half_sign():
    lane = lax.broadcasted_iota(jnp.int32, (1, HD), 1)
    return jnp.where(lane < HD // 2, -1.0, 1.0)


def scores_of(query, key_rows, allowed):
    return jnp.where(allowed, dot_last(query, key_rows) * HD ** (-0.5), MASKED)


def allowed_of(place_col, place_row, id_col, id_row):
    return (place_row <= place_col) & ((id_row == 0) | (id_row == id_col))


def attend_kernel(
    x_ref, gain_ref, qkv_ref, cos_ref, sin_ref, place_col, place_row, id_col, id_row,
    turned_ref, lse_ref, attended_ref,
):
    tokens = cos_ref.shape[1]
    x = x_ref[...].reshape(tokens, -1).astype(F32)
    normed = (x * norm_scale(x) * gain_ref[...]).astype(BF)
    projected = dot(normed, qkv_ref[...])
    cosine, sine = cos_ref[0], sin_ref[0] * half_sign()
    turned = []
    for head in range(GROUP + 2):
        values = projected[:, head * HD : (head + 1) * HD]
        if head <= GROUP:
            values = values * cosine + pltpu.roll(values, HD // 2, 1) * sine
        turned.append(values.astype(BF))
        turned_ref[0, :, head * HD : (head + 1) * HD] = turned[head]
    allowed = allowed_of(place_col[...], place_row[...], id_col[0], id_row[0])
    for head in range(GROUP):
        scores = scores_of(turned[head], turned[GROUP], allowed)
        row_max = jnp.max(scores, axis=-1, keepdims=True)
        exponent = jnp.exp(scores - row_max)
        row_total = jnp.sum(exponent, axis=-1, keepdims=True)
        lse_ref[0, head] = row_max + jnp.log(row_total)
        rows_out = dot((exponent / row_total).astype(BF), turned[GROUP + 1]).astype(BF)
        attended_ref[:, 0, :, head * HD : (head + 1) * HD] = rows_out.reshape(2, tokens // 2, HD)


def attend(x_all, gain, qkv_matrix, cosine, sine, marks):
    _, groups, half_tok, width = x_all.shape
    tokens = 2 * half_tok
    by_half = lambda columns: at_group((2, 1, half_tok, columns), 1)
    return pl.pallas_call(
        attend_kernel,
        grid=(groups,),
        in_specs=[
            by_half(width),
            whole((1, width)),
            whole((width, HEAD_COLS)),
            at_group((1, tokens, HD), 0),
            at_group((1, tokens, HD), 0),
            whole((tokens, 1)),
            whole((1, tokens)),
            at_group((1, tokens, 1), 0),
            at_group((1, 1, tokens), 0),
        ],
        out_specs=[
            at_group((1, tokens, HEAD_COLS), 0),
            at_group((1, GROUP, tokens, 1), 0),
            by_half(GROUP * HD),
        ],
        out_shape=[
            jax.ShapeDtypeStruct((groups, tokens, HEAD_COLS), BF),
            jax.ShapeDtypeStruct((groups, GROUP, tokens, 1), F32),
            jax.ShapeDtypeStruct((2, groups, half_tok, GROUP * HD), BF),
        ],
        compiler_params=params(32),
        cost_estimate=SMALL,
    )(x_all, gain, qkv_matrix, cosine, sine, *marks)


def attend_back_kernel(
    branch_ref, out_ref, qkv_ref, x_ref, gain_ref, attended_ref, turned_ref, lse_ref, cos_ref, sin_ref,
    place_col, place_row, id_col, id_row,
    mine_ref, other_ref, grad_qkv_ref, grad_out_ref, grad_gain_ref, qkv_sum, out_sum,
):
    tokens = cos_ref.shape[1]
    factor = HD ** (-0.5)
    first = pl.program_id(0) == 0
    last = pl.program_id(0) == pl.num_programs(0) - 1
    branch = branch_ref[...].reshape(tokens, -1)
    d_attended = dot_last(branch, out_ref[...]).astype(BF)
    turned = [turned_ref[0, :, head * HD : (head + 1) * HD] for head in range(GROUP + 2)]
    key_rows, value_rows = turned[GROUP], turned[GROUP + 1]
    allowed = allowed_of(place_col[...], place_row[...], id_col[0], id_row[0])
    cosine, sine, sign = cos_ref[0], sin_ref[0], half_sign()

    def unrope(values):
        values = values.astype(BF).astype(F32)
        return (values * cosine - sign * pltpu.roll(values * sine, HD // 2, 1)).astype(BF)

    d_keys = d_values = None
    columns = []
    for head in range(GROUP):
        d_rows = d_attended[:, head * HD : (head + 1) * HD]
        probs = jnp.exp(scores_of(turned[head], key_rows, allowed) - lse_ref[0, head])
        d_probs = dot_last(d_rows, value_rows)
        row_sum = jnp.sum(probs * d_probs, axis=-1, keepdims=True)
        d_scores = (probs * (d_probs - row_sum)).astype(BF)
        columns.append(unrope(dot(d_scores, key_rows) * factor))
        key_part = dot_rows(d_scores, turned[head]) * factor
        value_part = dot_rows(probs.astype(BF), d_rows)
        d_keys = key_part if d_keys is None else d_keys + key_part
        d_values = value_part if d_values is None else d_values + value_part
    columns.append(unrope(d_keys))
    columns.append(d_values.astype(BF))
    projected = jnp.concatenate(columns, axis=1)
    d_normed = dot_last(projected, qkv_ref[...])
    mine_ref[0] = d_normed[: tokens // 2]
    other_ref[0] = d_normed[tokens // 2 :].astype(BF)

    @pl.when(first)
    def _():
        qkv_sum[...] = jnp.zeros_like(qkv_sum)
        out_sum[...] = jnp.zeros_like(out_sum)
        grad_gain_ref[...] = jnp.zeros_like(grad_gain_ref)

    x = x_ref[...].reshape(tokens, -1).astype(F32)
    scaled = x * norm_scale(x)
    grad_gain_ref[...] += jnp.sum(d_normed * scaled, axis=0, keepdims=True)
    qkv_sum[...] += dot_rows((scaled * gain_ref[...]).astype(BF), projected)
    out_sum[...] += dot_rows(attended_ref[...].reshape(tokens, -1), branch)

    @pl.when(last)
    def _():
        grad_qkv_ref[...] = qkv_sum[...].astype(BF)
        grad_out_ref[...] = out_sum[...].astype(BF)


def attend_back(d_branch, out_matrix, qkv_matrix, x_all, gain, attended, turned, lse, cosine, sine, marks):
    _, groups, half_tok, width = d_branch.shape
    tokens = 2 * half_tok
    return pl.pallas_call(
        attend_back_kernel,
        grid=(groups,),
        in_specs=[
            at_group((2, 1, half_tok, width), 1),
            whole((GROUP * HD, width)),
            whole((width, HEAD_COLS)),
            at_group((2, 1, half_tok, width), 1),
            whole((1, width)),
            at_group((2, 1, half_tok, GROUP * HD), 1),
            at_group((1, tokens, HEAD_COLS), 0),
            at_group((1, GROUP, tokens, 1), 0),
            at_group((1, tokens, HD), 0),
            at_group((1, tokens, HD), 0),
            whole((tokens, 1)),
            whole((1, tokens)),
            at_group((1, tokens, 1), 0),
            at_group((1, 1, tokens), 0),
        ],
        out_specs=[
            at_group((1, half_tok, width), 0),
            at_group((1, half_tok, width), 0),
            whole((width, HEAD_COLS)),
            whole((GROUP * HD, width)),
            whole((1, width)),
        ],
        out_shape=[
            jax.ShapeDtypeStruct((groups, half_tok, width), F32),
            jax.ShapeDtypeStruct((groups, half_tok, width), BF),
            jax.ShapeDtypeStruct((width, HEAD_COLS), BF),
            jax.ShapeDtypeStruct((GROUP * HD, width), BF),
            jax.ShapeDtypeStruct((1, width), F32),
        ],
        scratch_shapes=[pltpu.VMEM((width, HEAD_COLS), F32), pltpu.VMEM((GROUP * HD, width), F32)],
        compiler_params=params(48),
        cost_estimate=SMALL,
    )(d_branch, out_matrix, qkv_matrix, x_all, gain, attended, turned, lse, cosine, sine, *marks)


def half_specs(rows, columns, steps):
    first = pl.BlockSpec((rows, columns), lambda step: (jnp.minimum(step, steps // 2 - 1), 0))
    second = pl.BlockSpec((rows, columns), lambda step: (jnp.maximum(step - steps // 2, 0), 0))
    shapes = [
        jax.ShapeDtypeStruct((rows * steps // 2, columns), F32),
        jax.ShapeDtypeStruct((rows * steps // 2, columns), BF),
    ]
    return [first, second], shapes


def store_halves(values, mine_ref, other_ref):
    step, half = pl.program_id(0), pl.num_programs(0) // 2

    @pl.when(step < half)
    def _():
        mine_ref[...] = values

    @pl.when(step >= half)
    def _():
        other_ref[...] = values.astype(BF)


def partial_kernel(left_ref, right_ref, mine_ref, other_ref):
    store_halves(dot(left_ref[...], right_ref[...]), mine_ref, other_ref)


def partial_product(left, right):
    tokens, depth = left.shape
    rows, steps = tokens // 4, 4
    specs, shapes = half_specs(rows, right.shape[1], steps)
    return pl.pallas_call(
        partial_kernel,
        grid=(steps,),
        in_specs=[at_group((rows, depth), 0), whole(right.shape)],
        out_specs=specs,
        out_shape=shapes,
        compiler_params=params(32),
        cost_estimate=SMALL,
    )(left, right)


def forward_back_kernel(
    normed_ref, og_ref, matrix_ref, down_ref,
    activated_ref, d_first_ref, d_second_ref, mine_ref, other_ref,
):
    width = matrix_ref.shape[1] // 4
    normed, og = normed_ref[...], og_ref[...]
    total = None
    for half, d_ref in enumerate((d_first_ref, d_second_ref)):
        start = 2 * half * width
        gate = dot(normed, matrix_ref[:, start : start + width])
        up = dot(normed, matrix_ref[:, start + width : start + 2 * width])
        d_act = dot_last(og, down_ref[half * width : (half + 1) * width])
        sigmoid = jax.nn.sigmoid(gate)
        silu = gate * sigmoid
        activated_ref[:, half * width : (half + 1) * width] = (silu * up).astype(BF)
        d_ref[:, :width] = (d_act * up * (sigmoid * (1.0 + gate * (1.0 - sigmoid)))).astype(BF)
        d_ref[:, width:] = (d_act * silu).astype(BF)
        back = dot_last(d_ref[...], matrix_ref[:, start : start + 2 * width])
        total = back if total is None else total + back
    store_halves(total, mine_ref, other_ref)


def forward_back(normed2, og_all, gateup_matrix, down_matrix):
    tokens, width = normed2.shape
    unit = down_matrix.shape[0]
    rows, steps = tokens // 4, 4
    specs, shapes = half_specs(rows, width, steps)
    return pl.pallas_call(
        forward_back_kernel,
        grid=(steps,),
        in_specs=[
            at_group((rows, width), 0),
            at_group((rows, width), 0),
            whole((width, 2 * unit)),
            whole((unit, width)),
        ],
        out_specs=[at_group((rows, unit), 0)] * 3 + specs,
        out_shape=[jax.ShapeDtypeStruct((tokens, unit), BF)] * 3 + shapes,
        compiler_params=params(48),
        cost_estimate=SMALL,
    )(normed2, og_all, gateup_matrix, down_matrix)


def gradient_kernel(left_ref, right_ref, out_ref):
    out_ref[...] = dot_rows(left_ref[...], right_ref[...]).astype(BF)


def gradient(left, right):
    tokens, rows = left.shape
    block = min(rows, 256)
    return pl.pallas_call(
        gradient_kernel,
        grid=(rows // block,),
        in_specs=[at_group((tokens, block), 1), whole(right.shape)],
        out_specs=at_group((block, right.shape[1]), 0),
        out_shape=jax.ShapeDtypeStruct((rows, right.shape[1]), BF),
        compiler_params=params(32),
        cost_estimate=SMALL,
    )(left, right)


def shards(
    hidden_in,
    out_grad,
    segments,
    qkv_weight,
    out_weight,
    gateup_weight,
    down_weight,
    gain_weight,
    qkv_first,
    out_first,
    gateup_first,
    down_first,
    gain_first,
    qkv_second,
    out_second,
    gateup_second,
    down_second,
    gain_second,
):
    seq = lax.axis_index("seq")
    rows = qkv_weight.shape[0]
    tok_local = hidden_in.shape[1]
    group_tok = tok_local * lax.axis_size("seq")
    span = TP * tok_local
    owner = seq * shard_size() + lax.axis_index("shard")


    x_own, og_own = hidden_in[0], out_grad[0]
    x_local = x_own.astype(F32)
    recent()

    gain_cols, width = gain_weight.shape[1], x_own.shape[1]
    known = jnp.zeros((2 + shard_size() * group_tok // width, width), BF)
    known = lax.dynamic_update_slice(known, gain_weight.astype(BF), (0, owner * gain_cols))
    ids_own = jnp.where(seq == 0, segments, 0).astype(BF)
    per_row = width // group_tok
    shard = lax.axis_index("shard")
    known = lax.dynamic_update_slice(
        known, ids_own, (2 + shard // per_row, shard % per_row * group_tok)
    )
    known = butterfly(known)
    gains = known[:2].astype(F32)
    came = recent()
    down_matrix = gather_places(after(down_weight.astype(BF), *came)).reshape(-1, width)
    held = after(og_own, *came[:2])
    og_mine = [og_own, *(from_column(held, k) for k in range(1, TP))]
    out_block = swap_roles(out_weight.astype(BF))
    pair = pair_halves(gateup_weight.astype(BF))
    qkv_pair = pair_qkv(qkv_weight.astype(BF))
    slot = recent()

    gateup_block = spread_halves(after(pair, *slot))
    held = after(qkv_pair, *slot)
    loads = [
        jnp.concatenate([x_own, qkv_piece(held, j).reshape(tok_local, -1)], axis=1) for j in range(TP)
    ]
    loads = [from_corner(loads[j], j) for j in range(TP)]
    x_mine = [entry[:, :width] for entry in loads]
    qkv_block = turn_corners([entry[:, width:].reshape(-1, HEAD_COLS) for entry in loads])
    qkv_block = jnp.swapaxes(qkv_block.reshape(TP, 2, rows, HEAD_COLS), 0, 1)
    slot = recent()

    qkv_matrix = collect_lines(after(qkv_block, *slot))
    gateup_matrix = collect_places(after(gateup_block, down_matrix))
    ids = known[2:].reshape(-1, group_tok).astype(jnp.int32)
    places = jnp.arange(group_tok, dtype=jnp.int32)

    def local_order(values):
        return jnp.where(seq == 0, values, jnp.roll(values, -tok_local, axis=-1))

    ids = [pick(ids, shard ^ j, 0) for j in range(TP)]
    positions = jnp.stack([local_order(positions_of(entry)) for entry in ids])
    ids = jnp.stack([local_order(entry) for entry in ids])
    places = local_order(places)
    marks = (places[:, None], places[None, :], ids[:, :, None], ids[:, None, :])
    cosine, sine = rotary(positions.reshape(-1))
    cosine, sine = cosine.reshape(TP, group_tok, HD), sine.reshape(TP, group_tok, HD)
    slot = recent()

    out_matrix = lay(
        [(line_place(line), block) for line, block in gather_lines(after(out_block, *slot))], 0
    ).reshape(GROUP * HD, -1)
    x_all = both_halves([x_mine[0], *(after(entry, *slot) for entry in x_mine[1:])])
    x_all = x_all.reshape(2, TP, tok_local, width)
    turned, lse, attended = attend(x_all, gains[:1], qkv_matrix, cosine, sine, marks)
    attended = attended.reshape(-1, GROUP * HD)
    slot = (*recent(), attended)

    met = meet_halves(*partial_product(after(attended, *slot), out_matrix))
    middle = x_local + met[0]
    for j in range(1, TP):
        middle = middle + from_corner(met[j].astype(BF), j).astype(F32)
    factor_two = norm_scale(middle)
    slot = recent()

    og_all = both_halves([after(entry, slot[0]) for entry in og_mine])

    normed2_own = after((middle * factor_two * gains[1]).astype(BF), *slot, *recent())
    normed2 = both_halves([from_column(normed2_own, k) for k in range(TP)])
    slot = recent()

    activated, d_gate_up_0, d_gate_up_1, d_mine, d_other = forward_back(
        after(normed2, *slot), og_all, gateup_matrix, down_matrix
    )

    d_met = meet_halves(d_mine, d_other)
    slot = recent()
    sends = [entry.astype(BF) for entry in d_met[1:]]
    grad_half_0 = gradient(after(normed2, d_other), d_gate_up_0)
    total_0 = unspread_places(after(grad_half_0, *slot), rows)
    out_mine, out_other = partial_product(after(activated, *slot, grad_half_0), down_matrix)
    d_normed2 = d_met[0]
    for k in range(1, TP):
        came = after(to_column(sends[k - 1], k), out_other)
        d_normed2 = d_normed2 + came.astype(F32)
    d_mid_part, d_gain_two = norm_back(d_normed2, middle, factor_two, gains[1])
    d_middle = og_own.astype(F32) + d_mid_part
    slot = recent()

    d_branch_own = after(d_middle.astype(BF), *slot)
    d_branch_mine = [from_corner(d_branch_own, j) for j in range(TP)]
    held = after(total_0, *slot, d_branch_own)
    laid_0 = lay_columns([from_column(column_piece(held, k), k) for k in range(TP)])
    grad_half_1 = gradient(after(normed2, *slot), d_gate_up_1)
    grad_down = gradient(after(activated, *slot), og_all)
    out_met = meet_halves(out_mine, after(out_other, *slot))
    slot = (*recent(), grad_half_1, grad_down)

    sends = [after(entry.astype(BF), *slot) for entry in out_met]
    result = middle + out_met[0]
    for k in range(1, TP):
        result = result + to_column(sends[k], k).astype(F32)
    output = result.astype(BF)[None]
    out_came = recent()
    total_1 = unspread_places(after(grad_half_1, *slot), rows, out_came)
    out_came = (*out_came, *recent()[:2])
    d_branch = both_halves([after(entry, *slot) for entry in d_branch_mine])
    in_mine, in_other, grad_qkv, grad_out, d_gain_one = attend_back(
        d_branch.reshape(2, TP, tok_local, width),
        out_matrix,
        qkv_matrix,
        x_all,
        gains[:1],
        attended.reshape(2, TP, tok_local, GROUP * HD),
        turned,
        lse,
        cosine,
        sine,
        marks,
    )
    in_other = after(in_other.reshape(-1, width), *out_came)
    in_met = meet_halves(in_mine.reshape(-1, width), in_other)
    slot = (*recent(), *out_came)

    d_normed = in_met[0]
    for j in range(1, TP):
        d_normed = d_normed + from_corner(after(in_met[j].astype(BF), *slot), j).astype(F32)
    came = recent()
    down_blocks = [
        pick(grad_down.reshape(place_size(), -1, width), place_index() ^ j, 0)
        for j in range(place_size())
    ]
    down_sum = None
    if place_size() == TP:
        near = [from_corner(after(down_blocks[j], *came), j) for j in (1, 2)]
        down_sum = sum(entry.astype(F32) for entry in (down_blocks[0], *near))
    down_came = recent()
    d_gains = jnp.concatenate([d_gain_one, d_gain_two[None]], axis=0)
    held = after(total_1, *slot)
    view = after(grad_out, *slot).reshape(place_size(), -1, width)
    if place_size() == TP:
        column, out_rows = column_index(), view.shape[1]
        rider = d_gains.reshape(2, 2, TP, TP, gain_cols)
        loads = [
            jnp.concatenate(
                [pick(view, (column - k) % TP, 0), column_piece(held, k).reshape(-1, width)], axis=0
            )
            for k in range(TP)
        ]
        loads = [ride(loads[k], pick(rider, (column - k) % TP, 2)) for k in range(TP)]
        loads = [from_column(loads[k], k) for k in range(TP)]
        loads = [alight(entry, 2 * out_rows, (2, 2, TP, gain_cols)) for entry in loads]
        rider = sum(extra.astype(F32) for _, extra in loads)
        grad_out = sum(load[:out_rows].astype(F32) for load, _ in loads)
        pieces = [load[out_rows:].reshape(2, rows, -1) for load, _ in loads]
    else:
        grad_out = scatter_lines(lambda line: pick(view, line_place(line), 0))
        pieces = [from_column(column_piece(held, k), k) for k in range(TP)]
        rider = jnp.zeros((2, 2, TP, gain_cols), F32)
    factor_one = norm_scale(x_local)
    d_in_part = norm_back(d_normed, x_local, factor_one, gains[0])[0]
    input_grad = (d_middle + d_in_part).astype(BF)[None]
    slot = (*recent(), *came)
    laid_1 = lay_columns(pieces)
    grad_gateup = join_halves([laid_0, laid_1]).astype(F32)

    if down_sum is None:
        grad_down = scatter_bits(down_blocks, 0, shard_bits(place_size()))
    else:
        grad_down = down_sum + from_corner(after(down_blocks[3], *slot, *down_came), 3).astype(F32)
    grad_out = swap_roles(after(grad_out.astype(BF), *slot)).astype(F32)
    grad_qkv, grad_gain = unspread_qkv(after(grad_qkv, *slot), rows, rider)
    grad_qkv = grad_qkv.astype(F32)
    if place_size() != TP:
        grad_gain = lax.dynamic_slice_in_dim(butterfly(d_gains), owner * gain_cols, gain_cols, 1)

    masters = (qkv_weight, out_weight, gateup_weight, down_weight, gain_weight)
    gradients = (grad_qkv, grad_out, grad_gateup, grad_down, grad_gain)
    new_ones, new_twos, updates = lamb_moments(
        masters,
        gradients,
        (qkv_first, out_first, gateup_first, down_first, gain_first),
        (qkv_second, out_second, gateup_second, down_second, gain_second),
    )

    def squares(arrays):
        matrices = jnp.stack([jnp.sum(entry * entry) for entry in arrays[:4]])
        return jnp.concatenate([matrices, jnp.sum(arrays[4] * arrays[4], axis=1)])

    norms = jnp.sqrt(butterfly(jnp.stack([squares(masters), squares(updates)])))
    ratios = norms[0] / norms[1]
    news = [masters[slot] - RATE * ratios[slot] * updates[slot] for slot in range(4)]
    news.append(masters[4] - RATE * ratios[4:6][:, None] * updates[4])
    copies = [entry.astype(BF) for entry in news]
    recent()
    return (output, input_grad, *news, *new_ones, *new_twos, *copies, norms)


def solution(mesh):
    rows, columns = P(("seq", "shard"), None), P(None, ("seq", "shard"))
    tokens = P("shard", "seq", None)
    states = (rows, rows, rows, rows, columns)
    return jax.shard_map(
        shards,
        mesh=mesh,
        in_specs=(tokens, tokens, P("shard", None)) + states * 3,
        out_specs=(tokens, tokens) + states * 4 + (P(),),
        check_vma=False,
    )
```

```python
import jax
import jax.numpy as jnp
from jax import lax
from jax.experimental import pallas as pl
from jax.experimental.pallas import tpu as pltpu
from jax.sharding import PartitionSpec as P

HQ = 16
KVH = 8
HD = 128
FF = 8192
NCONT = 2
STEP = 10
TP = 4


NORM_EPS = 1e-05
THETA = 1000000.0
BETA1 = 0.9
BETA2 = 0.999
ADAM_EPS = 1e-06
DECAY = 0.01
RATE = 0.5
MASKED = -1e30
GROUP = HQ // KVH
HEAD_COLS = (GROUP + 2) * HD
BF = jnp.bfloat16
F32 = jnp.float32


def dot(left, right):
    return jnp.dot(left, right, preferred_element_type=F32)


def dot_rows(left, right):
    return lax.dot_general(left, right, (((0,), (0,)), ((), ())), preferred_element_type=F32)


def dot_last(left, right):
    return lax.dot_general(left, right, (((1,), (1,)), ((), ())), preferred_element_type=F32)


def after(values, *others):
    return lax.optimization_barrier((values, *others))[0]


RECENT = []


def permute(values, axis, pairs):
    RECENT.append(lax.ppermute(values, axis, pairs))
    return RECENT[-1]


def recent():
    arrivals = tuple(RECENT)
    RECENT.clear()
    return arrivals


def shard_size():
    return lax.axis_size("shard")


def place_size():
    return shard_size() // TP


def shard_bits(count):
    return count.bit_length() - 1


def place_index():
    return lax.axis_index("shard") % place_size()


def column_index():
    return lax.axis_index("shard") // place_size()


def corner_index():
    return lax.axis_index("shard") % TP


def line_index():
    return lax.axis_index("shard") // TP


def line_place(line):
    middles = place_size() // TP
    return line % middles * TP + line // middles


def rotate(values, steps):
    count, places = shard_size(), place_size()
    pairs = [
        (entry, ((entry // places - steps) % TP) * places + entry % places)
        for entry in range(count)
    ]
    return permute(values, "shard", pairs)


def hop(values, change):
    return permute(values, "shard", [(i, i ^ change) for i in range(shard_size())])


def swap_roles(values):
    count, places = shard_size(), place_size()

    def partner(entry):
        column, middle, corner = entry // places, entry % places // TP, entry % TP
        return (corner * (places // TP) + middle) * TP + column

    return permute(values, "shard", [(i, partner(i)) for i in range(count)])


def flip(values):
    return permute(values, "seq", [(0, 1), (1, 0)])


def butterfly(values):
    for bit in reversed(range(shard_bits(shard_size()))):
        values = values + hop(values, 1 << bit)
    return values + flip(values)


def from_column(values, step):
    return rotate(values, step) if step else values


def to_column(values, step):
    return rotate(values, -step) if step else values


def from_corner(values, step):
    return hop(values, step) if step else values


def ride(load, extra):
    columns = load.shape[1]
    count = -(-extra.size // (16 * columns)) * 16 * columns
    extra = jnp.pad(extra.reshape(-1).astype(BF), (0, count - extra.size))
    return jnp.concatenate([load, extra.reshape(-1, columns)], axis=0)


def alight(load, rows, shape):
    size = 1
    for entry in shape:
        size *= entry
    return load[:rows], load[rows:].reshape(-1)[:size].reshape(shape)


def both_halves(mine):
    mine = jnp.concatenate(mine, axis=0)
    return jnp.concatenate([mine, flip(mine)], axis=0)


def meet_halves(mine, other):
    return jnp.split(mine + flip(other).astype(F32), TP)


def gather_bits(own, low_bit, bits):
    blocks = {0: own}
    for bit in range(bits):
        for entry in list(blocks):
            blocks[entry | (1 << bit)] = hop(blocks[entry], 1 << (low_bit + bit))
    return [blocks[entry] for entry in range(1 << bits)]


def scatter_bits(blocks, low_bit, bits):
    sums = {entry: block.astype(F32) for entry, block in enumerate(blocks)}
    for bit in reversed(range(bits)):
        for entry in range(1 << bit):
            came = hop(sums.pop(entry | (1 << bit)).astype(BF), 1 << (low_bit + bit))
            sums[entry] = sums[entry] + came.astype(F32)
    return sums[0]


def gather_places(own):
    places = place_size()
    groups = [[column * places + place for place in range(places)] for column in range(TP)]
    return lax.all_gather(own, "shard", axis_index_groups=groups)


def scatter_places(block_of, hold=()):
    blocks = [block_of(place_index() ^ entry) for entry in range(place_size())]
    if place_size() != TP:
        return scatter_bits(blocks, 0, shard_bits(place_size()))
    blocks[3] = after(blocks[3], *hold)
    total = blocks[0].astype(F32)
    for j in range(1, TP):
        total = total + from_corner(blocks[j], j).astype(F32)
    return total


def gather_lines(own):
    if place_size() == TP:
        return [((column_index() + k) % TP, from_column(own, k)) for k in range(TP)]
    blocks = gather_bits(own, 2, shard_bits(place_size()))
    return [(line_index() ^ entry, block) for entry, block in enumerate(blocks)]


def scatter_lines(block_of):
    if place_size() == TP:
        total = None
        for step in range(TP):
            came = to_column(block_of((column_index() + step) % TP), step).astype(F32)
            total = came if total is None else total + came
        return total
    return scatter_bits(
        [block_of(line_index() ^ entry) for entry in range(place_size())],
        2,
        shard_bits(place_size()),
    )


def lay(blocks, axis):
    shape = blocks[0][1].shape
    full = jnp.zeros(shape[:axis] + (len(blocks),) + shape[axis:], blocks[0][1].dtype)
    for index, block in blocks:
        starts = [0] * full.ndim
        starts[axis] = index
        full = lax.dynamic_update_slice(full, jnp.expand_dims(block, axis), starts)
    return full


def pick(values, index, axis):
    return lax.dynamic_index_in_dim(values, index, axis, keepdims=False)


def ordered_pair(mine, other):
    first = lax.axis_index("seq") == 0
    return jnp.stack([jnp.where(first, mine, other), jnp.where(first, other, mine)])


def turn_columns(blocks):
    twice = jnp.stack(blocks + blocks)
    return lax.dynamic_slice_in_dim(twice, (TP - column_index()) % TP, TP, 0)


def turn_corners(blocks):
    laid = jnp.stack(blocks)
    corner = corner_index()
    laid = jnp.where(corner % 2 == 1, laid[jnp.array([1, 0, 3, 2])], laid)
    return jnp.where(corner >= 2, laid[jnp.array([2, 3, 0, 1])], laid)


def columns_of(source, starts, size):
    return jnp.concatenate(
        [lax.dynamic_slice_in_dim(source, start, size, 1) for start in starts], axis=1
    )


def pair_qkv(weight):
    seq = lax.axis_index("seq")
    half = TP * HEAD_COLS
    mine = columns_of(weight, [seq * half], half)
    other = flip(columns_of(weight, [(1 - seq) * half], half))
    return ordered_pair(mine, other).reshape(-1, half)


def qkv_piece(pair, step):
    return columns_of(pair, [(corner_index() ^ step) * HEAD_COLS], HEAD_COLS)


def unspread_qkv(gradient, rows, rider, hold):
    view = gradient.reshape(2, place_size(), TP, rows, HEAD_COLS)
    total = scatter_lines(lambda line: pick(view, line, 1).reshape(-1, HEAD_COLS))
    total = after(total.astype(BF), *hold).reshape(2, TP, rows, HEAD_COLS)
    corner, seq = corner_index(), lax.axis_index("seq")
    count = rider.shape[-1]
    loads = [
        ride(pick(total, corner ^ j, 1).reshape(-1, HEAD_COLS), pick(rider, corner ^ j, 2))
        for j in range(TP)
    ]
    loads = [alight(from_corner(loads[j], j), 2 * rows, (2, 2, count)) for j in range(TP)]
    laid = turn_corners([load.reshape(2, rows, HEAD_COLS) for load, _ in loads])
    rider = sum(extra.astype(F32) for _, extra in loads)
    load = ride(pick(laid, 1 - seq, 1).reshape(-1, HEAD_COLS), pick(rider, 1 - seq, 1))
    other, extra = alight(flip(load), TP * rows, (2, count))
    rider = pick(rider, seq, 1) + extra.astype(F32)
    both = ordered_pair(pick(laid, seq, 1), other.reshape(TP, rows, HEAD_COLS))
    return jnp.concatenate([both[s, q] for s in range(2) for q in range(TP)], axis=1), rider


def pair_gateup(weight):
    seq, span = lax.axis_index("seq"), FF // 2
    mine = columns_of(weight, [seq * span, FF + seq * span], span)
    other = flip(columns_of(weight, [(1 - seq) * span, FF + (1 - seq) * span], span))
    return ordered_pair(mine, other).reshape(-1, FF)


def spread_gateup(pair, rider):
    column, span = column_index(), FF // (2 * TP)
    loads = []
    for k in range(TP):
        start = (column - k) % TP * span
        piece = columns_of(pair, [start, FF // 2 + start], span)
        loads.append(from_column(ride(piece, rider), k))
    loads = [alight(load, pair.shape[0], rider.shape) for load in loads]
    laid = turn_columns([load for load, _ in loads]).reshape(TP, 2, pair.shape[0] // 2, 2 * span)
    return jnp.swapaxes(laid, 0, 1), turn_columns([extra for _, extra in loads])


def collect_lines(block):
    shape = block.shape
    blocks = [
        (index, came.reshape(shape)) for index, came in gather_lines(block.reshape(-1, shape[-1]))
    ]
    return lay(blocks, 1).reshape(-1, shape[-1])


def collect_places(block):
    full = gather_places(block.reshape(-1, block.shape[-1]))
    full = full.reshape(-1, *block.shape)
    return jnp.transpose(full, (1, 2, 0, 3, 4)).reshape(-1, block.shape[-1])


def unspread_places(values, rows, hold=()):
    span = values.shape[1]
    view = values.reshape(2, TP, place_size(), rows, span)
    total = scatter_places(lambda place: pick(view, place, 2).reshape(-1, span), hold)
    return total.astype(BF).reshape(2, TP, rows, span)


def column_piece(total, step):
    return pick(total, (column_index() - step) % TP, 1)


def lay_columns(pieces):
    laid = turn_columns(pieces)
    seq = lax.axis_index("seq")
    return ordered_pair(pick(laid, seq, 1), flip(pick(laid, 1 - seq, 1)))


def join_halves(halves):
    width = halves[0].shape[-1] // 2
    return jnp.concatenate(
        [
            halves[half][s, c, :, gate * width : (gate + 1) * width]
            for gate in range(2)
            for s in range(2)
            for c in range(TP)
            for half in range(2)
        ],
        axis=1,
    )


def norm_scale(values):
    return lax.rsqrt(jnp.mean(values * values, axis=-1, keepdims=True) + NORM_EPS)


def positions_of(seg_row):
    labels = jnp.arange(NCONT + 1, dtype=jnp.int32)
    member = (seg_row[:, None] == labels[None, :]).astype(jnp.int32)
    counts = jnp.sum(member, axis=0)
    starts = jnp.cumsum(counts) - counts
    own_start = jnp.sum(member * starts[None, :], axis=1)
    places = jnp.arange(seg_row.shape[0], dtype=jnp.int32)
    return places - own_start + jnp.where(seg_row > 0, counts[0], 0)


def rotary(positions):
    half_size = HD // 2
    frequency = THETA ** (-(jnp.arange(half_size, dtype=F32) * (2.0 / HD)))
    angles = positions.astype(F32)[:, None] * frequency[None, :]
    angles = jnp.concatenate([angles, angles], axis=-1)
    return (jnp.cos(angles), jnp.sin(angles))


def norm_back(d_normed, inputs_f, factor_rows, gain_row):
    weighted = d_normed * gain_row
    d_inputs = factor_rows * weighted - inputs_f * factor_rows**3 * jnp.mean(
        weighted * inputs_f, axis=-1, keepdims=True
    )
    d_gain = jnp.sum(d_normed * inputs_f * factor_rows, axis=0)
    return (d_inputs, d_gain)


def lamb_moments(masters, gradients, moment_ones, moment_twos):
    decay_rates = (DECAY, DECAY, DECAY, DECAY, 0.0)
    new_ones, new_twos, updates = ([], [], [])
    for master, gradient, old_one, old_two, decay_rate in zip(
        masters, gradients, moment_ones, moment_twos, decay_rates
    ):
        new_one = BETA1 * old_one + (1.0 - BETA1) * gradient
        new_two = BETA2 * old_two + (1.0 - BETA2) * gradient * gradient
        update = (
            new_one / (1.0 - BETA1**STEP) / (jnp.sqrt(new_two / (1.0 - BETA2**STEP)) + ADAM_EPS)
            + decay_rate * master
        )
        new_ones.append(new_one)
        new_twos.append(new_two)
        updates.append(update)
    return (new_ones, new_twos, updates)


SMALL = pl.CostEstimate(flops=10**9, bytes_accessed=1, transcendentals=0)
MIB = 1 << 20


def params(mebibytes):
    return pltpu.CompilerParams(vmem_limit_bytes=mebibytes * MIB)


def whole(shape):
    return pl.BlockSpec(shape, lambda step: (0,) * len(shape), pipeline_mode=pl.Buffered(1))


def at_group(shape, axis):
    return pl.BlockSpec(shape, lambda step: tuple(step if d == axis else 0 for d in range(len(shape))))


def half_sign():
    lane = lax.broadcasted_iota(jnp.int32, (1, HD), 1)
    return jnp.where(lane < HD // 2, -1.0, 1.0)


def scores_of(query, key_rows, allowed):
    return jnp.where(allowed, dot_last(query, key_rows) * HD ** (-0.5), MASKED)


def allowed_of(place_col, place_row, id_col, id_row):
    return (place_row <= place_col) & ((id_row == 0) | (id_row == id_col))


def attend_kernel(
    x_ref, gain_ref, qkv_ref, cos_ref, sin_ref, place_col, place_row, id_col, id_row,
    turned_ref, lse_ref, attended_ref,
):
    tokens = cos_ref.shape[1]
    x = x_ref[...].reshape(tokens, -1).astype(F32)
    normed = (x * norm_scale(x) * gain_ref[...]).astype(BF)
    projected = dot(normed, qkv_ref[...])
    cosine, sine = cos_ref[0], sin_ref[0] * half_sign()
    turned = []
    for head in range(GROUP + 2):
        values = projected[:, head * HD : (head + 1) * HD]
        if head <= GROUP:
            values = values * cosine + pltpu.roll(values, HD // 2, 1) * sine
        turned.append(values.astype(BF))
        turned_ref[0, :, head * HD : (head + 1) * HD] = turned[head]
    allowed = allowed_of(place_col[...], place_row[...], id_col[0], id_row[0])
    for head in range(GROUP):
        scores = scores_of(turned[head], turned[GROUP], allowed)
        row_max = jnp.max(scores, axis=-1, keepdims=True)
        exponent = jnp.exp(scores - row_max)
        row_total = jnp.sum(exponent, axis=-1, keepdims=True)
        lse_ref[0, head] = row_max + jnp.log(row_total)
        rows_out = dot((exponent / row_total).astype(BF), turned[GROUP + 1]).astype(BF)
        attended_ref[:, 0, :, head * HD : (head + 1) * HD] = rows_out.reshape(2, tokens // 2, HD)


def attend(x_all, gain, qkv_matrix, cosine, sine, marks):
    _, groups, half_tok, width = x_all.shape
    tokens = 2 * half_tok
    by_half = lambda columns: at_group((2, 1, half_tok, columns), 1)
    return pl.pallas_call(
        attend_kernel,
        grid=(groups,),
        in_specs=[
            by_half(width),
            whole((1, width)),
            whole((width, HEAD_COLS)),
            at_group((1, tokens, HD), 0),
            at_group((1, tokens, HD), 0),
            whole((tokens, 1)),
            whole((1, tokens)),
            at_group((1, tokens, 1), 0),
            at_group((1, 1, tokens), 0),
        ],
        out_specs=[
            at_group((1, tokens, HEAD_COLS), 0),
            at_group((1, GROUP, tokens, 1), 0),
            by_half(GROUP * HD),
        ],
        out_shape=[
            jax.ShapeDtypeStruct((groups, tokens, HEAD_COLS), BF),
            jax.ShapeDtypeStruct((groups, GROUP, tokens, 1), F32),
            jax.ShapeDtypeStruct((2, groups, half_tok, GROUP * HD), BF),
        ],
        compiler_params=params(32),
        cost_estimate=SMALL,
    )(x_all, gain, qkv_matrix, cosine, sine, *marks)


def attend_back_kernel(
    branch_ref, out_ref, qkv_ref, x_ref, gain_ref, attended_ref, turned_ref, lse_ref, cos_ref, sin_ref,
    place_col, place_row, id_col, id_row,
    mine_ref, other_ref, grad_qkv_ref, grad_out_ref, grad_gain_ref, qkv_sum, out_sum,
):
    tokens = cos_ref.shape[1]
    factor = HD ** (-0.5)
    first = pl.program_id(0) == 0
    last = pl.program_id(0) == pl.num_programs(0) - 1
    branch = branch_ref[...].reshape(tokens, -1)
    d_attended = dot_last(branch, out_ref[...]).astype(BF)
    turned = [turned_ref[0, :, head * HD : (head + 1) * HD] for head in range(GROUP + 2)]
    key_rows, value_rows = turned[GROUP], turned[GROUP + 1]
    allowed = allowed_of(place_col[...], place_row[...], id_col[0], id_row[0])
    cosine, sine, sign = cos_ref[0], sin_ref[0], half_sign()

    def unrope(values):
        values = values.astype(BF).astype(F32)
        return (values * cosine - sign * pltpu.roll(values * sine, HD // 2, 1)).astype(BF)

    d_keys = d_values = None
    columns = []
    for head in range(GROUP):
        d_rows = d_attended[:, head * HD : (head + 1) * HD]
        probs = jnp.exp(scores_of(turned[head], key_rows, allowed) - lse_ref[0, head])
        d_probs = dot_last(d_rows, value_rows)
        row_sum = jnp.sum(probs * d_probs, axis=-1, keepdims=True)
        d_scores = (probs * (d_probs - row_sum)).astype(BF)
        columns.append(unrope(dot(d_scores, key_rows) * factor))
        key_part = dot_rows(d_scores, turned[head]) * factor
        value_part = dot_rows(probs.astype(BF), d_rows)
        d_keys = key_part if d_keys is None else d_keys + key_part
        d_values = value_part if d_values is None else d_values + value_part
    columns.append(unrope(d_keys))
    columns.append(d_values.astype(BF))
    projected = jnp.concatenate(columns, axis=1)
    d_normed = dot_last(projected, qkv_ref[...])
    mine_ref[0] = d_normed[: tokens // 2]
    other_ref[0] = d_normed[tokens // 2 :].astype(BF)

    @pl.when(first)
    def _():
        qkv_sum[...] = jnp.zeros_like(qkv_sum)
        out_sum[...] = jnp.zeros_like(out_sum)
        grad_gain_ref[...] = jnp.zeros_like(grad_gain_ref)

    x = x_ref[...].reshape(tokens, -1).astype(F32)
    scaled = x * norm_scale(x)
    grad_gain_ref[...] += jnp.sum(d_normed * scaled, axis=0, keepdims=True)
    qkv_sum[...] += dot_rows((scaled * gain_ref[...]).astype(BF), projected)
    out_sum[...] += dot_rows(attended_ref[...].reshape(tokens, -1), branch)

    @pl.when(last)
    def _():
        grad_qkv_ref[...] = qkv_sum[...].astype(BF)
        grad_out_ref[...] = out_sum[...].astype(BF)


def attend_back(d_branch, out_matrix, qkv_matrix, x_all, gain, attended, turned, lse, cosine, sine, marks):
    _, groups, half_tok, width = d_branch.shape
    tokens = 2 * half_tok
    return pl.pallas_call(
        attend_back_kernel,
        grid=(groups,),
        in_specs=[
            at_group((2, 1, half_tok, width), 1),
            whole((GROUP * HD, width)),
            whole((width, HEAD_COLS)),
            at_group((2, 1, half_tok, width), 1),
            whole((1, width)),
            at_group((2, 1, half_tok, GROUP * HD), 1),
            at_group((1, tokens, HEAD_COLS), 0),
            at_group((1, GROUP, tokens, 1), 0),
            at_group((1, tokens, HD), 0),
            at_group((1, tokens, HD), 0),
            whole((tokens, 1)),
            whole((1, tokens)),
            at_group((1, tokens, 1), 0),
            at_group((1, 1, tokens), 0),
        ],
        out_specs=[
            at_group((1, half_tok, width), 0),
            at_group((1, half_tok, width), 0),
            whole((width, HEAD_COLS)),
            whole((GROUP * HD, width)),
            whole((1, width)),
        ],
        out_shape=[
            jax.ShapeDtypeStruct((groups, half_tok, width), F32),
            jax.ShapeDtypeStruct((groups, half_tok, width), BF),
            jax.ShapeDtypeStruct((width, HEAD_COLS), BF),
            jax.ShapeDtypeStruct((GROUP * HD, width), BF),
            jax.ShapeDtypeStruct((1, width), F32),
        ],
        scratch_shapes=[pltpu.VMEM((width, HEAD_COLS), F32), pltpu.VMEM((GROUP * HD, width), F32)],
        compiler_params=params(48),
        cost_estimate=SMALL,
    )(d_branch, out_matrix, qkv_matrix, x_all, gain, attended, turned, lse, cosine, sine, *marks)


def half_specs(rows, columns, steps):
    first = pl.BlockSpec((rows, columns), lambda step: (jnp.minimum(step, steps // 2 - 1), 0))
    second = pl.BlockSpec((rows, columns), lambda step: (jnp.maximum(step - steps // 2, 0), 0))
    shapes = [
        jax.ShapeDtypeStruct((rows * steps // 2, columns), F32),
        jax.ShapeDtypeStruct((rows * steps // 2, columns), BF),
    ]
    return [first, second], shapes


def store_halves(values, mine_ref, other_ref):
    step, half = pl.program_id(0), pl.num_programs(0) // 2

    @pl.when(step < half)
    def _():
        mine_ref[...] = values

    @pl.when(step >= half)
    def _():
        other_ref[...] = values.astype(BF)


def partial_kernel(left_ref, right_ref, mine_ref, other_ref):
    store_halves(dot(left_ref[...], right_ref[...]), mine_ref, other_ref)


def partial_product(left, right):
    tokens, depth = left.shape
    rows, steps = tokens // 4, 4
    specs, shapes = half_specs(rows, right.shape[1], steps)
    return pl.pallas_call(
        partial_kernel,
        grid=(steps,),
        in_specs=[at_group((rows, depth), 0), whole(right.shape)],
        out_specs=specs,
        out_shape=shapes,
        compiler_params=params(32),
        cost_estimate=SMALL,
    )(left, right)


def forward_back_kernel(
    normed_ref, og_ref, matrix_ref, down_ref,
    activated_ref, d_first_ref, d_second_ref, mine_ref, other_ref,
):
    width = matrix_ref.shape[1] // 4
    normed, og = normed_ref[...], og_ref[...]
    total = None
    for half, d_ref in enumerate((d_first_ref, d_second_ref)):
        gate_matrix = matrix_ref[:, half * width : (half + 1) * width]
        up_matrix = matrix_ref[:, (2 + half) * width : (3 + half) * width]
        gate, up = dot(normed, gate_matrix), dot(normed, up_matrix)
        d_act = dot_last(og, down_ref[half * width : (half + 1) * width])
        sigmoid = jax.nn.sigmoid(gate)
        silu = gate * sigmoid
        activated_ref[:, half * width : (half + 1) * width] = (silu * up).astype(BF)
        d_ref[:, :width] = (d_act * up * (sigmoid * (1.0 + gate * (1.0 - sigmoid)))).astype(BF)
        d_ref[:, width:] = (d_act * silu).astype(BF)
        back = dot_last(d_ref[:, :width], gate_matrix) + dot_last(d_ref[:, width:], up_matrix)
        total = back if total is None else total + back
    store_halves(total, mine_ref, other_ref)


def forward_back(normed2, og_all, gateup_matrix, down_matrix):
    tokens, width = normed2.shape
    unit = down_matrix.shape[0]
    rows, steps = tokens // 4, 4
    specs, shapes = half_specs(rows, width, steps)
    return pl.pallas_call(
        forward_back_kernel,
        grid=(steps,),
        in_specs=[
            at_group((rows, width), 0),
            at_group((rows, width), 0),
            whole((width, 2 * unit)),
            whole((unit, width)),
        ],
        out_specs=[at_group((rows, unit), 0)] * 3 + specs,
        out_shape=[jax.ShapeDtypeStruct((tokens, unit), BF)] * 3 + shapes,
        compiler_params=params(48),
        cost_estimate=SMALL,
    )(normed2, og_all, gateup_matrix, down_matrix)


def gradient_kernel(left_ref, right_ref, out_ref):
    out_ref[...] = dot_rows(left_ref[...], right_ref[...]).astype(BF)


def gradient(left, right):
    tokens, rows = left.shape
    block = min(rows, 256)
    return pl.pallas_call(
        gradient_kernel,
        grid=(rows // block,),
        in_specs=[at_group((tokens, block), 1), whole(right.shape)],
        out_specs=at_group((block, right.shape[1]), 0),
        out_shape=jax.ShapeDtypeStruct((rows, right.shape[1]), BF),
        compiler_params=params(32),
        cost_estimate=SMALL,
    )(left, right)


def shards(
    hidden_in,
    out_grad,
    segments,
    qkv_weight,
    out_weight,
    gateup_weight,
    down_weight,
    gain_weight,
    qkv_first,
    out_first,
    gateup_first,
    down_first,
    gain_first,
    qkv_second,
    out_second,
    gateup_second,
    down_second,
    gain_second,
):
    seq = lax.axis_index("seq")
    rows = qkv_weight.shape[0]
    tok_local = hidden_in.shape[1]
    group_tok = tok_local * lax.axis_size("seq")
    span = TP * tok_local
    owner = seq * shard_size() + lax.axis_index("shard")


    x_own, og_own = hidden_in[0], out_grad[0]
    x_local = x_own.astype(F32)
    recent()

    gain_cols, width = gain_weight.shape[1], x_own.shape[1]
    packed = place_size() == TP
    shard = lax.axis_index("shard")
    gain_low = gain_weight.astype(BF)
    info = jnp.concatenate([gain_low.reshape(-1), segments.reshape(-1).astype(BF)])
    og_mine = [from_column(og_own, k) for k in range(TP)]
    came = recent()
    qkv_pair = pair_qkv(qkv_weight.astype(BF))
    pair = pair_gateup(gateup_weight.astype(BF))
    pairs_came = recent()
    loads = [
        jnp.concatenate([x_own, qkv_piece(qkv_pair, j).reshape(tok_local, -1)], axis=1)
        for j in range(TP)
    ]
    loads = [ride(load, info) for load in loads]
    loads[3] = after(loads[3], *came[:1])
    loads = [from_corner(loads[j], j) for j in range(TP)]
    loads = [alight(load, tok_local, info.shape) for load in loads]
    x_mine = [load[:, :width] for load, _ in loads]
    infos = turn_corners([extra for _, extra in loads])
    qkv_block = turn_corners([load[:, width:].reshape(-1, HEAD_COLS) for load, _ in loads])
    qkv_block = jnp.swapaxes(qkv_block.reshape(TP, 2, rows, HEAD_COLS), 0, 1)
    slot = (*came, *pairs_came, *recent())
    ids = [pick(infos, corner_index() ^ j, 0)[2 * gain_cols :].astype(jnp.int32) for j in range(TP)]

    down_matrix = gather_places(after(down_weight.astype(BF), *slot)).reshape(-1, width)
    gateup_block, infos = spread_gateup(after(pair, *slot), infos)
    out_block = swap_roles(after(out_weight.astype(BF), *slot))
    slot = recent()

    qkv_matrix = collect_lines(after(qkv_block, *slot))
    came = recent()
    gateup_matrix = collect_places(after(gateup_block, down_matrix))
    x_half = jnp.concatenate([after(x_mine[0], *slot), *x_mine[1:]], axis=0)
    x_other, infos_other = alight(flip(ride(x_half, infos)), span, infos.shape)
    x_all = jnp.concatenate([x_half, x_other], axis=0).reshape(2, TP, tok_local, width)
    if packed:
        gains = ordered_pair(infos, infos_other)[..., : 2 * gain_cols]
        gains = jnp.moveaxis(gains.reshape(-1, 2, gain_cols), 1, 0).reshape(2, width)
    else:
        gains = jnp.zeros((2, width), BF)
        gains = butterfly(lax.dynamic_update_slice(gains, gain_low, (0, owner * gain_cols)))
    gains = gains.astype(F32)
    slot = (*came, *recent())

    def local_order(values):
        return jnp.where(seq == 0, values, jnp.roll(values, -tok_local, axis=-1))

    positions = jnp.stack([local_order(positions_of(entry)) for entry in ids])
    ids = jnp.stack([local_order(entry) for entry in ids])
    places = local_order(jnp.arange(group_tok, dtype=jnp.int32))
    marks = (places[:, None], places[None, :], ids[:, :, None], ids[:, None, :])
    cosine, sine = rotary(positions.reshape(-1))
    cosine, sine = cosine.reshape(TP, group_tok, HD), sine.reshape(TP, group_tok, HD)

    out_matrix = lay(
        [(line_place(line), block) for line, block in gather_lines(after(out_block, *slot))], 0
    ).reshape(GROUP * HD, -1)
    turned, lse, attended = attend(x_all, gains[:1], qkv_matrix, cosine, sine, marks)
    attended = attended.reshape(-1, GROUP * HD)
    slot = (*recent(), attended)

    met = meet_halves(*partial_product(after(attended, *slot), out_matrix))
    middle = x_local + met[0]
    for j in range(1, TP):
        middle = middle + from_corner(met[j].astype(BF), j).astype(F32)
    factor_two = norm_scale(middle)
    slot = recent()

    og_all = both_halves([after(entry, slot[0]) for entry in og_mine])

    normed2_own = after((middle * factor_two * gains[1]).astype(BF), *slot, *recent())
    normed2 = [from_column(normed2_own, k) for k in range(TP)]
    normed2 = both_halves([after(normed2[0], gateup_matrix, *recent()), *normed2[1:]])
    slot = recent()

    activated, d_gate_up_0, d_gate_up_1, d_mine, d_other = forward_back(
        after(normed2, *slot), og_all, gateup_matrix, down_matrix
    )

    d_met = meet_halves(d_mine, d_other)
    slot = recent()
    sends = [entry.astype(BF) for entry in d_met[1:]]
    grad_half_0 = gradient(after(normed2, d_other), d_gate_up_0)
    total_0 = unspread_places(after(grad_half_0, *slot), rows)
    out_mine, out_other = partial_product(after(activated, *slot, grad_half_0), down_matrix)
    grad_half_1 = gradient(after(normed2, *slot, grad_half_0), d_gate_up_1)
    d_normed2 = d_met[0]
    for k in range(1, TP):
        came = after(to_column(sends[k - 1], k), out_other, grad_half_1)
        d_normed2 = d_normed2 + came.astype(F32)
    d_mid_part, d_gain_two = norm_back(d_normed2, middle, factor_two, gains[1])
    d_middle = og_own.astype(F32) + d_mid_part
    slot = recent()

    d_branch_own = after(d_middle.astype(BF), *slot)
    d_branch_mine = [from_corner(d_branch_own, j) for j in range(TP)]
    came = recent()
    held = after(total_0, *slot, d_branch_own)
    pieces = [column_piece(held, k) for k in range(TP)]
    pieces[3] = after(pieces[3], *came)
    laid_0 = lay_columns([from_column(pieces[k], k) for k in range(TP)])
    out_met = meet_halves(out_mine, after(out_other, *slot))
    slot = (*came, *recent())

    sends = [after(entry.astype(BF), *slot) for entry in out_met]
    result = middle + out_met[0]
    for k in range(1, TP):
        result = result + to_column(sends[k], k).astype(F32)
    output = result.astype(BF)[None]
    out_came = recent()
    total_1 = unspread_places(after(grad_half_1, *slot), rows)
    out_came = (*out_came, *recent())
    d_branch = both_halves([after(entry, *slot) for entry in d_branch_mine])
    in_mine, in_other, grad_qkv, grad_out, d_gain_one = attend_back(
        d_branch.reshape(2, TP, tok_local, width),
        out_matrix,
        qkv_matrix,
        x_all,
        gains[:1],
        attended.reshape(2, TP, tok_local, GROUP * HD),
        turned,
        lse,
        cosine,
        sine,
        marks,
    )
    grad_down = gradient(after(activated, *slot), og_all)
    in_other = after(in_other.reshape(-1, width), *out_came, grad_down)
    in_met = meet_halves(in_mine.reshape(-1, width), in_other)
    slot = (*recent(), *out_came)

    d_normed = in_met[0]
    for j in range(1, TP):
        d_normed = d_normed + from_corner(after(in_met[j].astype(BF), *slot), j).astype(F32)
    came = recent()
    down_blocks = [
        pick(grad_down.reshape(place_size(), -1, width), place_index() ^ j, 0)
        for j in range(place_size())
    ]
    down_sum = None
    if place_size() == TP:
        near = [from_corner(after(down_blocks[j], *came), j) for j in (1, 2)]
        down_sum = sum(entry.astype(F32) for entry in (down_blocks[0], *near))
    down_came = recent()
    d_gains = jnp.concatenate([d_gain_one, d_gain_two[None]], axis=0)
    held = after(total_1, *slot)
    view = after(grad_out, *slot).reshape(place_size(), -1, width)
    if place_size() == TP:
        column, out_rows = column_index(), view.shape[1]
        rider = d_gains.reshape(2, 2, TP, TP, gain_cols)
        loads = [
            jnp.concatenate(
                [pick(view, (column - k) % TP, 0), column_piece(held, k).reshape(-1, width)], axis=0
            )
            for k in range(TP)
        ]
        loads = [ride(loads[k], pick(rider, (column - k) % TP, 2)) for k in range(TP)]
        loads[3] = after(loads[3], *came)
        loads = [from_column(loads[k], k) for k in range(TP)]
        loads = [alight(entry, 2 * out_rows, (2, 2, TP, gain_cols)) for entry in loads]
        rider = sum(extra.astype(F32) for _, extra in loads)
        grad_out = sum(load[:out_rows].astype(F32) for load, _ in loads)
        pieces = [load[out_rows:].reshape(2, rows, -1) for load, _ in loads]
    else:
        grad_out = scatter_lines(lambda line: pick(view, line_place(line), 0))
        pieces = [from_column(column_piece(held, k), k) for k in range(TP)]
        rider = jnp.zeros((2, 2, TP, gain_cols), F32)
    factor_one = norm_scale(x_local)
    d_in_part = norm_back(d_normed, x_local, factor_one, gains[0])[0]
    input_grad = (d_middle + d_in_part).astype(BF)[None]
    slot = (*recent(), *came)
    laid_1 = lay_columns(pieces)
    grad_gateup = join_halves([laid_0, laid_1]).astype(F32)

    if down_sum is None:
        grad_down = scatter_bits(down_blocks, 0, shard_bits(place_size()))
    else:
        grad_down = down_sum + from_corner(after(down_blocks[3], *slot, *down_came), 3).astype(F32)
    grad_out = swap_roles(after(grad_out.astype(BF), *slot)).astype(F32)
    grad_qkv, grad_gain = unspread_qkv(after(grad_qkv, *slot), rows, rider, recent())
    grad_qkv = grad_qkv.astype(F32)
    if not packed:
        grad_gain = lax.dynamic_slice_in_dim(butterfly(d_gains), owner * gain_cols, gain_cols, 1)

    masters = (qkv_weight, out_weight, gateup_weight, down_weight, gain_weight)
    gradients = (grad_qkv, grad_out, grad_gateup, grad_down, grad_gain)
    new_ones, new_twos, updates = lamb_moments(
        masters,
        gradients,
        (qkv_first, out_first, gateup_first, down_first, gain_first),
        (qkv_second, out_second, gateup_second, down_second, gain_second),
    )

    def squares(arrays):
        return [jnp.sum(entry * entry) for entry in (*arrays[:4], *arrays[4])]

    norms = jnp.stack(squares(masters) + squares(updates)).reshape(2, -1)
    norms = jnp.sqrt(butterfly(norms))
    ratios = norms[0] / norms[1]
    news = [masters[slot] - RATE * ratios[slot] * updates[slot] for slot in range(4)]
    news.append(masters[4] - RATE * ratios[4:6][:, None] * updates[4])
    copies = [entry.astype(BF) for entry in news]
    recent()
    return (output, input_grad, *news, *new_ones, *new_twos, *copies, norms)


def solution(mesh):
    rows, columns = P(("seq", "shard"), None), P(None, ("seq", "shard"))
    tokens = P("shard", "seq", None)
    states = (rows, rows, rows, rows, columns)
    return jax.shard_map(
        shards,
        mesh=mesh,
        in_specs=(tokens, tokens, P("shard", None)) + states * 3,
        out_specs=(tokens, tokens) + states * 4 + (P(),),
        check_vma=False,
    )
```

```python
import jax
import jax.numpy as jnp
import numpy as np
from jax import lax
from jax.experimental import pallas as pl
from jax.experimental.pallas import tpu as pltpu
from jax.sharding import PartitionSpec as P

HQ = 16
KVH = 8
HD = 128
FF = 8192
NCONT = 2
STEP = 10
TP = 4


NORM_EPS = 1e-05
THETA = 1000000.0
BETA1 = 0.9
BETA2 = 0.999
ADAM_EPS = 1e-06
DECAY = 0.01
RATE = 0.5
MASKED = -1e30
GROUP = HQ // KVH
HEAD_COLS = (GROUP + 2) * HD
BF = jnp.bfloat16
F32 = jnp.float32


def dot(left, right):
    return jnp.dot(left, right, preferred_element_type=F32)


def dot_rows(left, right):
    return lax.dot_general(left, right, (((0,), (0,)), ((), ())), preferred_element_type=F32)


def dot_last(left, right):
    return lax.dot_general(left, right, (((1,), (1,)), ((), ())), preferred_element_type=F32)


def after(values, *others):
    return lax.optimization_barrier((values, *others))[0]


RECENT = []


def permute(values, axis, pairs):
    RECENT.append(lax.ppermute(values, axis, pairs))
    return RECENT[-1]


def recent():
    arrivals = tuple(RECENT)
    RECENT.clear()
    return arrivals


def shard_size():
    return lax.axis_size("shard")


def place_size():
    return shard_size() // TP


def shard_bits(count):
    return count.bit_length() - 1


def place_index():
    return lax.axis_index("shard") % place_size()


def column_index():
    return lax.axis_index("shard") // place_size()


def corner_index():
    return lax.axis_index("shard") % TP


def line_index():
    return lax.axis_index("shard") // TP


def line_place(line):
    middles = place_size() // TP
    return line % middles * TP + line // middles


def rotate(values, steps):
    count, places = shard_size(), place_size()
    pairs = [
        (entry, ((entry // places - steps) % TP) * places + entry % places)
        for entry in range(count)
    ]
    return permute(values, "shard", pairs)


def hop(values, change):
    return permute(values, "shard", [(i, i ^ change) for i in range(shard_size())])


def swap_roles(values):
    count, places = shard_size(), place_size()

    def partner(entry):
        column, middle, corner = entry // places, entry % places // TP, entry % TP
        return (corner * (places // TP) + middle) * TP + column

    return permute(values, "shard", [(i, partner(i)) for i in range(count)])


def flip(values):
    return permute(values, "seq", [(0, 1), (1, 0)])


def butterfly(values):
    for bit in reversed(range(shard_bits(shard_size()))):
        values = values + hop(values, 1 << bit)
    return values + flip(values)


def from_column(values, step):
    return rotate(values, step) if step else values


def to_column(values, step):
    return rotate(values, -step) if step else values


def from_corner(values, step):
    return hop(values, step) if step else values


def ride(load, extra):
    columns = load.shape[1]
    count = -(-extra.size // (16 * columns)) * 16 * columns
    extra = jnp.pad(extra.reshape(-1).astype(BF), (0, count - extra.size))
    return jnp.concatenate([load, extra.reshape(-1, columns)], axis=0)


def alight(load, rows, shape):
    size = 1
    for entry in shape:
        size *= entry
    return load[:rows], load[rows:].reshape(-1)[:size].reshape(shape)


def both_halves(mine):
    mine = jnp.concatenate(mine, axis=0)
    return jnp.concatenate([mine, flip(mine)], axis=0)


def meet_halves(mine, other):
    return jnp.split(mine + flip(other).astype(F32), TP)


def gather_bits(own, low_bit, bits):
    blocks = {0: own}
    for bit in range(bits):
        for entry in list(blocks):
            blocks[entry | (1 << bit)] = hop(blocks[entry], 1 << (low_bit + bit))
    return [blocks[entry] for entry in range(1 << bits)]


def scatter_bits(blocks, low_bit, bits):
    sums = {entry: block.astype(F32) for entry, block in enumerate(blocks)}
    for bit in reversed(range(bits)):
        for entry in range(1 << bit):
            came = hop(sums.pop(entry | (1 << bit)).astype(BF), 1 << (low_bit + bit))
            sums[entry] = sums[entry] + came.astype(F32)
    return sums[0]


def gather_places(own):
    places = place_size()
    groups = [[column * places + place for place in range(places)] for column in range(TP)]
    return lax.all_gather(own, "shard", axis_index_groups=groups)


def scatter_places(block_of, hold=()):
    blocks = [block_of(place_index() ^ entry) for entry in range(place_size())]
    if place_size() != TP:
        return scatter_bits(blocks, 0, shard_bits(place_size()))
    blocks[3] = after(blocks[3], *hold)
    total = blocks[0].astype(F32)
    for j in range(1, TP):
        total = total + from_corner(blocks[j], j).astype(F32)
    return total


def gather_lines(own):
    if place_size() == TP:
        return [((column_index() + k) % TP, from_column(own, k)) for k in range(TP)]
    blocks = gather_bits(own, 2, shard_bits(place_size()))
    return [(line_index() ^ entry, block) for entry, block in enumerate(blocks)]


def scatter_lines(block_of):
    if place_size() == TP:
        total = None
        for step in range(TP):
            came = to_column(block_of((column_index() + step) % TP), step).astype(F32)
            total = came if total is None else total + came
        return total
    return scatter_bits(
        [block_of(line_index() ^ entry) for entry in range(place_size())],
        2,
        shard_bits(place_size()),
    )


def lay(blocks, axis):
    shape = blocks[0][1].shape
    full = jnp.zeros(shape[:axis] + (len(blocks),) + shape[axis:], blocks[0][1].dtype)
    for index, block in blocks:
        starts = [0] * full.ndim
        starts[axis] = index
        full = lax.dynamic_update_slice(full, jnp.expand_dims(block, axis), starts)
    return full


def pick(values, index, axis):
    return lax.dynamic_index_in_dim(values, index, axis, keepdims=False)


def ordered_pair(mine, other):
    first = lax.axis_index("seq") == 0
    return jnp.stack([jnp.where(first, mine, other), jnp.where(first, other, mine)])


def turn_columns(blocks):
    twice = jnp.stack(blocks + blocks)
    return lax.dynamic_slice_in_dim(twice, (TP - column_index()) % TP, TP, 0)


def turn_corners(blocks):
    corner = corner_index()
    for bit in (1, 2):
        odd = corner // bit % 2 == 1
        blocks = [jnp.where(odd, blocks[j ^ bit], blocks[j]) for j in range(TP)]
    return jnp.stack(blocks)


def columns_of(source, starts, size):
    return jnp.concatenate(
        [lax.dynamic_slice_in_dim(source, start, size, 1) for start in starts], axis=1
    )


def pair_qkv(weight):
    seq = lax.axis_index("seq")
    half = TP * HEAD_COLS
    mine = columns_of(weight, [seq * half], half)
    other = flip(columns_of(weight, [(1 - seq) * half], half))
    return ordered_pair(mine, other).reshape(-1, half)


def qkv_piece(pair, step):
    return columns_of(pair, [(corner_index() ^ step) * HEAD_COLS], HEAD_COLS)


def unspread_qkv(gradient, rows, rider, hold):
    view = gradient.reshape(2, place_size(), TP, rows, HEAD_COLS)
    total = scatter_lines(lambda line: pick(view, line, 1).reshape(-1, HEAD_COLS))
    total = after(total.astype(BF), *hold).reshape(2, TP, rows, HEAD_COLS)
    corner, seq = corner_index(), lax.axis_index("seq")
    count = rider.shape[-1]
    loads = [
        ride(pick(total, corner ^ j, 1).reshape(-1, HEAD_COLS), pick(rider, corner ^ j, 2))
        for j in range(TP)
    ]
    loads = [alight(from_corner(loads[j], j), 2 * rows, (2, 2, count)) for j in range(TP)]
    laid = turn_corners([load.reshape(2, rows, HEAD_COLS) for load, _ in loads])
    rider = sum(extra.astype(F32) for _, extra in loads)
    load = ride(pick(laid, 1 - seq, 1).reshape(-1, HEAD_COLS), pick(rider, 1 - seq, 1))
    other, extra = alight(flip(load), TP * rows, (2, count))
    rider = pick(rider, seq, 1) + extra.astype(F32)
    both = ordered_pair(pick(laid, seq, 1), other.reshape(TP, rows, HEAD_COLS))
    return jnp.concatenate([both[s, q] for s in range(2) for q in range(TP)], axis=1), rider


def pair_gateup(weight):
    seq, span = lax.axis_index("seq"), FF // 2
    mine = columns_of(weight, [seq * span, FF + seq * span], span)
    other = flip(columns_of(weight, [(1 - seq) * span, FF + (1 - seq) * span], span))
    return ordered_pair(mine, other).reshape(-1, FF)


def spread_gateup(pair, rider):
    column, span = column_index(), FF // (2 * TP)
    loads = []
    for k in range(TP):
        start = (column - k) % TP * span
        piece = columns_of(pair, [start, FF // 2 + start], span)
        loads.append(from_column(ride(piece, rider), k))
    loads = [alight(load, pair.shape[0], rider.shape) for load in loads]
    return jnp.concatenate([load for load, _ in loads], axis=0), [extra for _, extra in loads]


def collect_lines(block):
    shape = block.shape
    blocks = [
        (index, came.reshape(shape)) for index, came in gather_lines(block.reshape(-1, shape[-1]))
    ]
    return lay(blocks, 1).reshape(-1, shape[-1])


def order_places(came):
    places, columns = place_size(), came.shape[-1]
    came = came.reshape(places, TP, 2, -1, columns)
    full = jnp.zeros((2, TP, places, came.shape[3], columns), came.dtype)
    for k in range(TP):
        part = jnp.swapaxes(came[:, k], 0, 1)[:, None]
        full = lax.dynamic_update_slice(full, part, (0, (column_index() + k) % TP, 0, 0, 0))
    return full.reshape(-1, columns)


def unspread_places(values, rows, hold=()):
    span = values.shape[1]
    view = values.reshape(2, TP, place_size(), rows, span)
    total = scatter_places(lambda place: pick(view, place, 2).reshape(-1, span), hold)
    return total.astype(BF).reshape(2, TP, rows, span)


def column_piece(total, step):
    return pick(total, (column_index() - step) % TP, 1)


def lay_columns(pieces):
    laid = turn_columns(pieces)
    seq = lax.axis_index("seq")
    return ordered_pair(pick(laid, seq, 1), flip(pick(laid, 1 - seq, 1)))


def join_halves(halves):
    width = halves[0].shape[-1] // 2
    return jnp.concatenate(
        [
            halves[half][s, c, :, gate * width : (gate + 1) * width]
            for gate in range(2)
            for s in range(2)
            for c in range(TP)
            for half in range(2)
        ],
        axis=1,
    )


def norm_scale(values):
    return lax.rsqrt(jnp.mean(values * values, axis=-1, keepdims=True) + NORM_EPS)


def positions_of(seg_row):
    labels = jnp.arange(NCONT + 1, dtype=jnp.int32)
    member = (seg_row[:, None] == labels[None, :]).astype(jnp.int32)
    counts = jnp.sum(member, axis=0)
    starts = jnp.cumsum(counts) - counts
    own_start = jnp.sum(member * starts[None, :], axis=1)
    places = jnp.arange(seg_row.shape[0], dtype=jnp.int32)
    return places - own_start + jnp.where(seg_row > 0, counts[0], 0)


def rotary(positions):
    half_size = HD // 2
    frequency = THETA ** (-(jnp.arange(half_size, dtype=F32) * (2.0 / HD)))
    angles = positions.astype(F32)[:, None] * frequency[None, :]
    angles = jnp.concatenate([angles, angles], axis=-1)
    return (jnp.cos(angles), jnp.sin(angles))


def norm_back(d_normed, inputs_f, factor_rows, gain_row):
    weighted = d_normed * gain_row
    d_inputs = factor_rows * weighted - inputs_f * factor_rows**3 * jnp.mean(
        weighted * inputs_f, axis=-1, keepdims=True
    )
    d_gain = jnp.sum(d_normed * inputs_f * factor_rows, axis=0)
    return (d_inputs, d_gain)


def lamb_moments(masters, gradients, moment_ones, moment_twos):
    decay_rates = (DECAY, DECAY, DECAY, DECAY, 0.0)
    new_ones, new_twos, updates = ([], [], [])
    for master, gradient, old_one, old_two, decay_rate in zip(
        masters, gradients, moment_ones, moment_twos, decay_rates
    ):
        new_one = BETA1 * old_one + (1.0 - BETA1) * gradient
        new_two = BETA2 * old_two + (1.0 - BETA2) * gradient * gradient
        update = (
            new_one / (1.0 - BETA1**STEP) / (jnp.sqrt(new_two / (1.0 - BETA2**STEP)) + ADAM_EPS)
            + decay_rate * master
        )
        new_ones.append(new_one)
        new_twos.append(new_two)
        updates.append(update)
    return (new_ones, new_twos, updates)


SMALL = pl.CostEstimate(flops=10**9, bytes_accessed=1, transcendentals=0)
MIB = 1 << 20


def params(mebibytes):
    return pltpu.CompilerParams(vmem_limit_bytes=mebibytes * MIB)


def whole(shape):
    return pl.BlockSpec(shape, lambda step: (0,) * len(shape), pipeline_mode=pl.Buffered(1))


def at_group(shape, axis):
    return pl.BlockSpec(shape, lambda step: tuple(step if d == axis else 0 for d in range(len(shape))))


def half_sign():
    lane = lax.broadcasted_iota(jnp.int32, (1, HD), 1)
    return jnp.where(lane < HD // 2, -1.0, 1.0)


def scores_of(query, key_rows, allowed):
    return jnp.where(allowed, dot_last(query, key_rows) * HD ** (-0.5), MASKED)


def allowed_of(place_col, place_row, id_col, id_row):
    return (place_row <= place_col) & ((id_row == 0) | (id_row == id_col))


def attend_kernel(
    x_ref, gain_ref, qkv_ref, cos_ref, sin_ref, place_col, place_row, id_col, id_row,
    turned_ref, lse_ref, attended_ref,
):
    tokens = cos_ref.shape[1]
    x = x_ref[...].reshape(tokens, -1).astype(F32)
    normed = (x * norm_scale(x) * gain_ref[...]).astype(BF)
    projected = dot(normed, qkv_ref[...])
    cosine, sine = cos_ref[0], sin_ref[0] * half_sign()
    turned = []
    for head in range(GROUP + 2):
        values = projected[:, head * HD : (head + 1) * HD]
        if head <= GROUP:
            values = values * cosine + pltpu.roll(values, HD // 2, 1) * sine
        turned.append(values.astype(BF))
        turned_ref[0, :, head * HD : (head + 1) * HD] = turned[head]
    allowed = allowed_of(place_col[...], place_row[...], id_col[0], id_row[0])
    for head in range(GROUP):
        scores = scores_of(turned[head], turned[GROUP], allowed)
        row_max = jnp.max(scores, axis=-1, keepdims=True)
        exponent = jnp.exp(scores - row_max)
        row_total = jnp.sum(exponent, axis=-1, keepdims=True)
        lse_ref[0, head] = row_max + jnp.log(row_total)
        rows_out = dot((exponent / row_total).astype(BF), turned[GROUP + 1]).astype(BF)
        attended_ref[:, 0, :, head * HD : (head + 1) * HD] = rows_out.reshape(2, tokens // 2, HD)


def attend(x_all, gain, qkv_matrix, cosine, sine, marks):
    _, groups, half_tok, width = x_all.shape
    tokens = 2 * half_tok
    by_half = lambda columns: at_group((2, 1, half_tok, columns), 1)
    return pl.pallas_call(
        attend_kernel,
        grid=(groups,),
        in_specs=[
            by_half(width),
            whole((1, width)),
            whole((width, HEAD_COLS)),
            at_group((1, tokens, HD), 0),
            at_group((1, tokens, HD), 0),
            whole((tokens, 1)),
            whole((1, tokens)),
            at_group((1, tokens, 1), 0),
            at_group((1, 1, tokens), 0),
        ],
        out_specs=[
            at_group((1, tokens, HEAD_COLS), 0),
            at_group((1, GROUP, tokens, 1), 0),
            by_half(GROUP * HD),
        ],
        out_shape=[
            jax.ShapeDtypeStruct((groups, tokens, HEAD_COLS), BF),
            jax.ShapeDtypeStruct((groups, GROUP, tokens, 1), F32),
            jax.ShapeDtypeStruct((2, groups, half_tok, GROUP * HD), BF),
        ],
        compiler_params=params(32),
        cost_estimate=SMALL,
    )(x_all, gain, qkv_matrix, cosine, sine, *marks)


def attend_back_kernel(
    branch_ref, out_ref, qkv_ref, x_ref, gain_ref, attended_ref, turned_ref, lse_ref, cos_ref, sin_ref,
    place_col, place_row, id_col, id_row,
    mine_ref, other_ref, grad_qkv_ref, grad_out_ref, grad_gain_ref, qkv_sum, out_sum,
):
    tokens = cos_ref.shape[1]
    factor = HD ** (-0.5)
    first = pl.program_id(0) == 0
    last = pl.program_id(0) == pl.num_programs(0) - 1
    branch = branch_ref[...].reshape(tokens, -1)
    d_attended = dot_last(branch, out_ref[...]).astype(BF)
    turned = [turned_ref[0, :, head * HD : (head + 1) * HD] for head in range(GROUP + 2)]
    key_rows, value_rows = turned[GROUP], turned[GROUP + 1]
    allowed = allowed_of(place_col[...], place_row[...], id_col[0], id_row[0])
    cosine, sine, sign = cos_ref[0], sin_ref[0], half_sign()

    def unrope(values):
        values = values.astype(BF).astype(F32)
        return (values * cosine - sign * pltpu.roll(values * sine, HD // 2, 1)).astype(BF)

    d_keys = d_values = None
    columns = []
    for head in range(GROUP):
        d_rows = d_attended[:, head * HD : (head + 1) * HD]
        probs = jnp.exp(scores_of(turned[head], key_rows, allowed) - lse_ref[0, head])
        d_probs = dot_last(d_rows, value_rows)
        row_sum = jnp.sum(probs * d_probs, axis=-1, keepdims=True)
        d_scores = (probs * (d_probs - row_sum)).astype(BF)
        columns.append(unrope(dot(d_scores, key_rows) * factor))
        key_part = dot_rows(d_scores, turned[head]) * factor
        value_part = dot_rows(probs.astype(BF), d_rows)
        d_keys = key_part if d_keys is None else d_keys + key_part
        d_values = value_part if d_values is None else d_values + value_part
    columns.append(unrope(d_keys))
    columns.append(d_values.astype(BF))
    projected = jnp.concatenate(columns, axis=1)
    d_normed = dot_last(projected, qkv_ref[...])
    mine_ref[0] = d_normed[: tokens // 2]
    other_ref[0] = d_normed[tokens // 2 :].astype(BF)

    @pl.when(first)
    def _():
        qkv_sum[...] = jnp.zeros_like(qkv_sum)
        out_sum[...] = jnp.zeros_like(out_sum)
        grad_gain_ref[...] = jnp.zeros_like(grad_gain_ref)

    x = x_ref[...].reshape(tokens, -1).astype(F32)
    scaled = x * norm_scale(x)
    grad_gain_ref[...] += jnp.sum(d_normed * scaled, axis=0, keepdims=True)
    qkv_sum[...] += dot_rows((scaled * gain_ref[...]).astype(BF), projected)
    out_sum[...] += dot_rows(attended_ref[...].reshape(tokens, -1), branch)

    @pl.when(last)
    def _():
        grad_qkv_ref[...] = qkv_sum[...].astype(BF)
        grad_out_ref[...] = out_sum[...].astype(BF)


def attend_back(d_branch, out_matrix, qkv_matrix, x_all, gain, attended, turned, lse, cosine, sine, marks):
    _, groups, half_tok, width = d_branch.shape
    tokens = 2 * half_tok
    return pl.pallas_call(
        attend_back_kernel,
        grid=(groups,),
        in_specs=[
            at_group((2, 1, half_tok, width), 1),
            whole((GROUP * HD, width)),
            whole((width, HEAD_COLS)),
            at_group((2, 1, half_tok, width), 1),
            whole((1, width)),
            at_group((2, 1, half_tok, GROUP * HD), 1),
            at_group((1, tokens, HEAD_COLS), 0),
            at_group((1, GROUP, tokens, 1), 0),
            at_group((1, tokens, HD), 0),
            at_group((1, tokens, HD), 0),
            whole((tokens, 1)),
            whole((1, tokens)),
            at_group((1, tokens, 1), 0),
            at_group((1, 1, tokens), 0),
        ],
        out_specs=[
            at_group((1, half_tok, width), 0),
            at_group((1, half_tok, width), 0),
            whole((width, HEAD_COLS)),
            whole((GROUP * HD, width)),
            whole((1, width)),
        ],
        out_shape=[
            jax.ShapeDtypeStruct((groups, half_tok, width), F32),
            jax.ShapeDtypeStruct((groups, half_tok, width), BF),
            jax.ShapeDtypeStruct((width, HEAD_COLS), BF),
            jax.ShapeDtypeStruct((GROUP * HD, width), BF),
            jax.ShapeDtypeStruct((1, width), F32),
        ],
        scratch_shapes=[pltpu.VMEM((width, HEAD_COLS), F32), pltpu.VMEM((GROUP * HD, width), F32)],
        compiler_params=params(48),
        cost_estimate=SMALL,
    )(d_branch, out_matrix, qkv_matrix, x_all, gain, attended, turned, lse, cosine, sine, *marks)


def half_specs(rows, columns, steps):
    first = pl.BlockSpec((rows, columns), lambda step: (jnp.minimum(step, steps // 2 - 1), 0))
    second = pl.BlockSpec((rows, columns), lambda step: (jnp.maximum(step - steps // 2, 0), 0))
    shapes = [
        jax.ShapeDtypeStruct((rows * steps // 2, columns), F32),
        jax.ShapeDtypeStruct((rows * steps // 2, columns), BF),
    ]
    return [first, second], shapes


def store_halves(values, mine_ref, other_ref):
    step, half = pl.program_id(0), pl.num_programs(0) // 2

    @pl.when(step < half)
    def _():
        mine_ref[...] = values

    @pl.when(step >= half)
    def _():
        other_ref[...] = values.astype(BF)


def partial_kernel(left_ref, right_ref, mine_ref, other_ref):
    store_halves(dot(left_ref[...], right_ref[...]), mine_ref, other_ref)


def partial_product(left, right):
    tokens, depth = left.shape
    rows, steps = tokens // 4, 4
    specs, shapes = half_specs(rows, right.shape[1], steps)
    return pl.pallas_call(
        partial_kernel,
        grid=(steps,),
        in_specs=[at_group((rows, depth), 0), whole(right.shape)],
        out_specs=specs,
        out_shape=shapes,
        compiler_params=params(32),
        cost_estimate=SMALL,
    )(left, right)


def forward_back_kernel(
    normed_ref, og_ref, matrix_ref, down_ref,
    activated_ref, d_first_ref, d_second_ref, mine_ref, other_ref,
):
    width = matrix_ref.shape[1] // 4
    normed, og = normed_ref[...], og_ref[...]
    total = None
    for half, d_ref in enumerate((d_first_ref, d_second_ref)):
        gate_matrix = matrix_ref[:, half * width : (half + 1) * width]
        up_matrix = matrix_ref[:, (2 + half) * width : (3 + half) * width]
        gate, up = dot(normed, gate_matrix), dot(normed, up_matrix)
        d_act = dot_last(og, down_ref[half * width : (half + 1) * width])
        sigmoid = jax.nn.sigmoid(gate)
        silu = gate * sigmoid
        activated_ref[:, half * width : (half + 1) * width] = (silu * up).astype(BF)
        d_ref[:, :width] = (d_act * up * (sigmoid * (1.0 + gate * (1.0 - sigmoid)))).astype(BF)
        d_ref[:, width:] = (d_act * silu).astype(BF)
        back = dot_last(d_ref[:, :width], gate_matrix) + dot_last(d_ref[:, width:], up_matrix)
        total = back if total is None else total + back
    store_halves(total, mine_ref, other_ref)


def forward_back(normed2, og_all, gateup_matrix, down_matrix):
    tokens, width = normed2.shape
    unit = down_matrix.shape[0]
    rows, steps = tokens // 4, 4
    specs, shapes = half_specs(rows, width, steps)
    return pl.pallas_call(
        forward_back_kernel,
        grid=(steps,),
        in_specs=[
            at_group((rows, width), 0),
            at_group((rows, width), 0),
            whole((width, 2 * unit)),
            whole((unit, width)),
        ],
        out_specs=[at_group((rows, unit), 0)] * 3 + specs,
        out_shape=[jax.ShapeDtypeStruct((tokens, unit), BF)] * 3 + shapes,
        compiler_params=params(48),
        cost_estimate=SMALL,
    )(normed2, og_all, gateup_matrix, down_matrix)


def gradient_kernel(left_ref, right_ref, out_ref):
    out_ref[...] = dot_rows(left_ref[...], right_ref[...]).astype(BF)


def gradient(left, right):
    tokens, rows = left.shape
    block = min(rows, 256)
    return pl.pallas_call(
        gradient_kernel,
        grid=(rows // block,),
        in_specs=[at_group((tokens, block), 1), whole(right.shape)],
        out_specs=at_group((block, right.shape[1]), 0),
        out_shape=jax.ShapeDtypeStruct((rows, right.shape[1]), BF),
        compiler_params=params(32),
        cost_estimate=SMALL,
    )(left, right)


def shards(
    hidden_in,
    out_grad,
    segments,
    qkv_weight,
    out_weight,
    gateup_weight,
    down_weight,
    gain_weight,
    qkv_first,
    out_first,
    gateup_first,
    down_first,
    gain_first,
    qkv_second,
    out_second,
    gateup_second,
    down_second,
    gain_second,
):
    seq = lax.axis_index("seq")
    rows = qkv_weight.shape[0]
    tok_local = hidden_in.shape[1]
    group_tok = tok_local * lax.axis_size("seq")
    span = TP * tok_local
    owner = seq * shard_size() + lax.axis_index("shard")


    x_own, og_own = hidden_in[0], out_grad[0]
    x_local = x_own.astype(F32)
    recent()

    gain_cols, width = gain_weight.shape[1], x_own.shape[1]
    packed = place_size() == TP
    shard = lax.axis_index("shard")
    gain_low = gain_weight.astype(BF)
    info = jnp.concatenate([gain_low.reshape(-1), segments.reshape(-1).astype(BF)])
    og_mine = [from_column(og_own, k) for k in range(TP)]
    came = recent()
    qkv_pair = pair_qkv(qkv_weight.astype(BF))
    pair = pair_gateup(gateup_weight.astype(BF))
    pairs_came = recent()
    loads = [
        jnp.concatenate([x_own, qkv_piece(qkv_pair, j).reshape(tok_local, -1)], axis=1)
        for j in range(TP)
    ]
    loads = [ride(load, info) for load in loads]
    loads[3] = after(loads[3], *came[:1])
    loads = [from_corner(loads[j], j) for j in range(TP)]
    loads = [alight(load, tok_local, info.shape) for load in loads]
    x_mine = [load[:, :width] for load, _ in loads]
    infos = jnp.stack([extra for _, extra in loads])
    qkv_block = turn_corners([load[:, width:].reshape(-1, HEAD_COLS) for load, _ in loads])
    qkv_block = jnp.swapaxes(qkv_block.reshape(TP, 2, rows, HEAD_COLS), 0, 1)
    slot = (*came, *pairs_came, *recent())
    ids = [infos[j, 2 * gain_cols :].astype(jnp.int32) for j in range(TP)]

    down_matrix = gather_places(after(down_weight.astype(BF), *slot)).reshape(-1, width)
    gateup_block, infos = spread_gateup(after(pair, *slot), infos)
    infos = jnp.stack(infos)
    out_block = swap_roles(after(out_weight.astype(BF), *slot))
    slot = (*recent(), down_matrix)

    qkv_matrix = collect_lines(after(qkv_block, *slot))
    came = recent()
    gateup_came = gather_places(after(gateup_block, down_matrix))
    gateup_matrix = order_places(gateup_came)
    x_half = jnp.concatenate([after(x_mine[0], *slot), *x_mine[1:]], axis=0)
    x_other, infos_other = alight(flip(ride(x_half, infos)), span, infos.shape)
    x_all = jnp.concatenate([x_half, x_other], axis=0).reshape(2, TP, tok_local, width)
    if packed:
        gains = ordered_pair(infos, infos_other)[..., : 2 * gain_cols]
        gains = turn_columns([turn_corners([gains[:, k, j] for j in range(TP)]) for k in range(TP)])
        gains = jnp.transpose(gains.reshape(TP, TP, 2, 2, gain_cols), (3, 2, 0, 1, 4)).reshape(2, width)
    else:
        gains = jnp.zeros((2, width), BF)
        gains = butterfly(lax.dynamic_update_slice(gains, gain_low, (0, owner * gain_cols)))
    gains = gains.astype(F32)
    slot = (*came, *recent())

    def local_order(values):
        return jnp.where(seq == 0, values, jnp.roll(values, -tok_local, axis=-1))

    positions = jnp.stack([local_order(positions_of(entry)) for entry in ids])
    ids = jnp.stack([local_order(entry) for entry in ids])
    places = local_order(jnp.arange(group_tok, dtype=jnp.int32))
    marks = (places[:, None], places[None, :], ids[:, :, None], ids[:, None, :])
    cosine, sine = rotary(positions.reshape(-1))
    cosine, sine = cosine.reshape(TP, group_tok, HD), sine.reshape(TP, group_tok, HD)

    out_matrix = lay(
        [(line_place(line), block) for line, block in gather_lines(after(out_block, *slot))], 0
    ).reshape(GROUP * HD, -1)
    turned, lse, attended = attend(x_all, gains[:1], qkv_matrix, cosine, sine, marks)
    attended = attended.reshape(-1, GROUP * HD)
    slot = (*recent(), attended)

    met = meet_halves(*partial_product(after(attended, *slot, gateup_came), out_matrix))
    middle = x_local + met[0]
    for j in range(1, TP):
        middle = middle + from_corner(met[j].astype(BF), j).astype(F32)
    factor_two = norm_scale(middle)
    slot = recent()

    og_all = both_halves([after(entry, slot[0]) for entry in og_mine])

    normed2_own = after((middle * factor_two * gains[1]).astype(BF), *slot, *recent())
    normed2 = [from_column(normed2_own, k) for k in range(TP)]
    normed2 = both_halves([after(normed2[0], gateup_matrix, *recent()), *normed2[1:]])
    slot = recent()

    activated, d_gate_up_0, d_gate_up_1, d_mine, d_other = forward_back(
        after(normed2, *slot), og_all, gateup_matrix, down_matrix
    )

    d_met = meet_halves(d_mine, d_other)
    slot = recent()
    sends = [entry.astype(BF) for entry in d_met[1:]]
    grad_half_0 = gradient(after(normed2, d_other), d_gate_up_0)
    total_0 = unspread_places(after(grad_half_0, *slot), rows)
    out_mine, out_other = partial_product(after(activated, *slot, grad_half_0), down_matrix)
    grad_half_1 = gradient(after(normed2, *slot, grad_half_0), d_gate_up_1)
    d_normed2 = d_met[0]
    for k in range(1, TP):
        came = after(to_column(sends[k - 1], k), out_other, grad_half_1)
        d_normed2 = d_normed2 + came.astype(F32)
    d_mid_part, d_gain_two = norm_back(d_normed2, middle, factor_two, gains[1])
    d_middle = og_own.astype(F32) + d_mid_part
    slot = recent()

    d_branch_own = after(d_middle.astype(BF), *slot)
    d_branch_mine = [from_corner(d_branch_own, j) for j in range(TP)]
    came = recent()
    held = after(total_0, *slot, d_branch_own)
    pieces = [column_piece(held, k) for k in range(TP)]
    pieces[3] = after(pieces[3], *came)
    laid_0 = lay_columns([from_column(pieces[k], k) for k in range(TP)])
    out_met = meet_halves(out_mine, after(out_other, *slot))
    slot = (*came, *recent())

    sends = [after(entry.astype(BF), *slot) for entry in out_met]
    result = middle + out_met[0]
    for k in range(1, TP):
        result = result + to_column(sends[k], k).astype(F32)
    output = result.astype(BF)[None]
    out_came = recent()
    total_1 = unspread_places(after(grad_half_1, *slot), rows, out_came[:1])
    out_came = (*out_came, *recent())
    d_branch = both_halves([after(entry, *slot) for entry in d_branch_mine])
    in_mine, in_other, grad_qkv, grad_out, d_gain_one = attend_back(
        d_branch.reshape(2, TP, tok_local, width),
        out_matrix,
        qkv_matrix,
        x_all,
        gains[:1],
        attended.reshape(2, TP, tok_local, GROUP * HD),
        turned,
        lse,
        cosine,
        sine,
        marks,
    )
    grad_down = gradient(after(activated, *slot), og_all)
    in_other = after(in_other.reshape(-1, width), *out_came, grad_down)
    in_met = meet_halves(in_mine.reshape(-1, width), in_other)
    slot = (*recent(), *out_came)

    d_normed = in_met[0]
    for j in range(1, TP):
        d_normed = d_normed + from_corner(after(in_met[j].astype(BF), *slot), j).astype(F32)
    came = recent()
    down_blocks = [
        pick(grad_down.reshape(place_size(), -1, width), place_index() ^ j, 0)
        for j in range(place_size())
    ]
    down_sum = None
    if place_size() == TP:
        near = [from_corner(after(down_blocks[j], *came), j) for j in (1, 2)]
        down_sum = sum(entry.astype(F32) for entry in (down_blocks[0], *near))
    down_came = recent()
    d_gains = jnp.concatenate([d_gain_one, d_gain_two[None]], axis=0)
    held = after(total_1, *slot)
    view = after(grad_out, *slot).reshape(place_size(), -1, width)
    if place_size() == TP:
        column, out_rows = column_index(), view.shape[1]
        rider = d_gains.reshape(2, 2, TP, TP, gain_cols)
        loads = [
            jnp.concatenate(
                [pick(view, (column - k) % TP, 0), column_piece(held, k).reshape(-1, width)], axis=0
            )
            for k in range(TP)
        ]
        loads = [ride(loads[k], pick(rider, (column - k) % TP, 2)) for k in range(TP)]
        loads[3] = after(loads[3], *came)
        loads = [from_column(loads[k], k) for k in range(TP)]
        loads = [alight(entry, 2 * out_rows, (2, 2, TP, gain_cols)) for entry in loads]
        rider = sum(extra.astype(F32) for _, extra in loads)
        grad_out = sum(load[:out_rows].astype(F32) for load, _ in loads)
        pieces = [load[out_rows:].reshape(2, rows, -1) for load, _ in loads]
    else:
        grad_out = scatter_lines(lambda line: pick(view, line_place(line), 0))
        pieces = [from_column(column_piece(held, k), k) for k in range(TP)]
        rider = jnp.zeros((2, 2, TP, gain_cols), F32)
    factor_one = norm_scale(x_local)
    d_in_part = norm_back(d_normed, x_local, factor_one, gains[0])[0]
    input_grad = (d_middle + d_in_part).astype(BF)[None]
    slot = (*recent(), *came)
    laid_1 = lay_columns(pieces)
    grad_gateup = join_halves([laid_0, laid_1]).astype(F32)

    if down_sum is None:
        grad_down = scatter_bits(down_blocks, 0, shard_bits(place_size()))
    else:
        grad_down = down_sum + from_corner(after(down_blocks[3], *slot, *down_came), 3).astype(F32)
    grad_out = swap_roles(after(grad_out.astype(BF), *slot)).astype(F32)
    grad_qkv, grad_gain = unspread_qkv(after(grad_qkv, *slot), rows, rider, recent())
    grad_qkv = grad_qkv.astype(F32)
    if not packed:
        grad_gain = lax.dynamic_slice_in_dim(butterfly(d_gains), owner * gain_cols, gain_cols, 1)

    masters = (qkv_weight, out_weight, gateup_weight, down_weight, gain_weight)
    gradients = (grad_qkv, grad_out, grad_gateup, grad_down, grad_gain)
    new_ones, new_twos, updates = lamb_moments(
        masters,
        gradients,
        (qkv_first, out_first, gateup_first, down_first, gain_first),
        (qkv_second, out_second, gateup_second, down_second, gain_second),
    )

    def squares(arrays):
        return [jnp.sum(entry * entry) for entry in (*arrays[:4], *arrays[4])]

    norms = jnp.zeros((2, 6), F32)
    for row, arrays in enumerate((masters, updates)):
        for column, total in enumerate(squares(arrays)):
            spot = np.zeros((2, 6), np.float32)
            spot[row, column] = 1.0
            norms = norms + total * spot
    norms = jnp.sqrt(butterfly(norms))
    ratios = norms[0] / norms[1]
    news = [masters[slot] - RATE * ratios[slot] * updates[slot] for slot in range(4)]
    news.append(masters[4] - RATE * ratios[4:6][:, None] * updates[4])
    copies = [entry.astype(BF) for entry in news]
    recent()
    return (output, input_grad, *news, *new_ones, *new_twos, *copies, norms)


def solution(mesh):
    rows, columns = P(("seq", "shard"), None), P(None, ("seq", "shard"))
    tokens = P("shard", "seq", None)
    states = (rows, rows, rows, rows, columns)
    return jax.shard_map(
        shards,
        mesh=mesh,
        in_specs=(tokens, tokens, P("shard", None)) + states * 3,
        out_specs=(tokens, tokens) + states * 4 + (P(),),
        check_vma=False,
    )
```

```python
import jax
import jax.numpy as jnp
import numpy as np
from jax import lax
from jax.experimental import pallas as pl
from jax.experimental.pallas import tpu as pltpu
from jax.sharding import PartitionSpec as P

HQ = 16
KVH = 8
HD = 128
FF = 8192
NCONT = 2
STEP = 10
TP = 4


NORM_EPS = 1e-05
THETA = 1000000.0
BETA1 = 0.9
BETA2 = 0.999
ADAM_EPS = 1e-06
DECAY = 0.01
RATE = 0.5
MASKED = -1e30
GROUP = HQ // KVH
HEAD_COLS = (GROUP + 2) * HD
BF = jnp.bfloat16
F32 = jnp.float32


def dot(left, right):
    return jnp.dot(left, right, preferred_element_type=F32)


def dot_rows(left, right):
    return lax.dot_general(left, right, (((0,), (0,)), ((), ())), preferred_element_type=F32)


def dot_last(left, right):
    return lax.dot_general(left, right, (((1,), (1,)), ((), ())), preferred_element_type=F32)


def after(values, *others):
    return lax.optimization_barrier((values, *others))[0]


RECENT = []


def permute(values, axis, pairs):
    RECENT.append(lax.ppermute(values, axis, pairs))
    return RECENT[-1]


def recent():
    arrivals = tuple(RECENT)
    RECENT.clear()
    return arrivals


def shard_size():
    return lax.axis_size("shard")


def place_size():
    return shard_size() // TP


def shard_bits(count):
    return count.bit_length() - 1


def place_index():
    return lax.axis_index("shard") % place_size()


def column_index():
    return lax.axis_index("shard") // place_size()


def corner_index():
    return lax.axis_index("shard") % TP


def line_index():
    return lax.axis_index("shard") // TP


def line_place(line):
    middles = place_size() // TP
    return line % middles * TP + line // middles


def rotate(values, steps):
    count, places = shard_size(), place_size()
    pairs = [
        (entry, ((entry // places - steps) % TP) * places + entry % places)
        for entry in range(count)
    ]
    return permute(values, "shard", pairs)


def hop(values, change):
    return permute(values, "shard", [(i, i ^ change) for i in range(shard_size())])


def swap_roles(values):
    count, places = shard_size(), place_size()

    def partner(entry):
        column, middle, corner = entry // places, entry % places // TP, entry % TP
        return (corner * (places // TP) + middle) * TP + column

    return permute(values, "shard", [(i, partner(i)) for i in range(count)])


def flip(values):
    return permute(values, "seq", [(0, 1), (1, 0)])


def butterfly(values):
    for bit in reversed(range(shard_bits(shard_size()))):
        values = values + hop(values, 1 << bit)
    return values + flip(values)


def from_column(values, step):
    return rotate(values, step) if step else values


def to_column(values, step):
    return rotate(values, -step) if step else values


def from_corner(values, step):
    return hop(values, step) if step else values


def ride(load, extra):
    columns = load.shape[1]
    count = -(-extra.size // (16 * columns)) * 16 * columns
    extra = jnp.pad(extra.reshape(-1).astype(BF), (0, count - extra.size))
    return jnp.concatenate([load, extra.reshape(-1, columns)], axis=0)


def alight(load, rows, shape):
    size = 1
    for entry in shape:
        size *= entry
    return load[:rows], load[rows:].reshape(-1)[:size].reshape(shape)


def both_halves(mine):
    mine = jnp.concatenate(mine, axis=0)
    return jnp.concatenate([mine, flip(mine)], axis=0)


def meet_halves(mine, other):
    return jnp.split(mine + flip(other).astype(F32), TP)


def gather_bits(own, low_bit, bits):
    blocks = {0: own}
    for bit in range(bits):
        for entry in list(blocks):
            blocks[entry | (1 << bit)] = hop(blocks[entry], 1 << (low_bit + bit))
    return [blocks[entry] for entry in range(1 << bits)]


def scatter_bits(blocks, low_bit, bits):
    sums = {entry: block.astype(F32) for entry, block in enumerate(blocks)}
    for bit in reversed(range(bits)):
        for entry in range(1 << bit):
            came = hop(sums.pop(entry | (1 << bit)).astype(BF), 1 << (low_bit + bit))
            sums[entry] = sums[entry] + came.astype(F32)
    return sums[0]


def gather_places(own):
    places = place_size()
    groups = [[column * places + place for place in range(places)] for column in range(TP)]
    return lax.all_gather(own, "shard", axis_index_groups=groups)


def scatter_places(block_of, hold=()):
    blocks = [block_of(place_index() ^ entry) for entry in range(place_size())]
    if place_size() != TP:
        return scatter_bits(blocks, 0, shard_bits(place_size()))
    blocks[3] = after(blocks[3], *hold)
    total = blocks[0].astype(F32)
    for j in range(1, TP):
        total = total + from_corner(blocks[j], j).astype(F32)
    return total


def gather_lines(own):
    if place_size() == TP:
        return [((column_index() + k) % TP, from_column(own, k)) for k in range(TP)]
    blocks = gather_bits(own, 2, shard_bits(place_size()))
    return [(line_index() ^ entry, block) for entry, block in enumerate(blocks)]


def scatter_lines(block_of):
    if place_size() == TP:
        total = None
        for step in range(TP):
            came = to_column(block_of((column_index() + step) % TP), step).astype(F32)
            total = came if total is None else total + came
        return total
    return scatter_bits(
        [block_of(line_index() ^ entry) for entry in range(place_size())],
        2,
        shard_bits(place_size()),
    )


def lay(blocks, axis):
    shape = blocks[0][1].shape
    full = jnp.zeros(shape[:axis] + (len(blocks),) + shape[axis:], blocks[0][1].dtype)
    for index, block in blocks:
        starts = [0] * full.ndim
        starts[axis] = index
        full = lax.dynamic_update_slice(full, jnp.expand_dims(block, axis), starts)
    return full


def pick(values, index, axis):
    return lax.dynamic_index_in_dim(values, index, axis, keepdims=False)


def ordered_pair(mine, other):
    first = lax.axis_index("seq") == 0
    return jnp.stack([jnp.where(first, mine, other), jnp.where(first, other, mine)])


def turn_columns(blocks):
    twice = jnp.stack(blocks + blocks)
    return lax.dynamic_slice_in_dim(twice, (TP - column_index()) % TP, TP, 0)


def turn_corners(blocks):
    corner = corner_index()
    for bit in (1, 2):
        odd = corner // bit % 2 == 1
        blocks = [jnp.where(odd, blocks[j ^ bit], blocks[j]) for j in range(TP)]
    return jnp.stack(blocks)


def columns_of(source, starts, size):
    return jnp.concatenate(
        [lax.dynamic_slice_in_dim(source, start, size, 1) for start in starts], axis=1
    )


def pair_qkv(weight):
    seq = lax.axis_index("seq")
    half = TP * HEAD_COLS
    mine = columns_of(weight, [seq * half], half)
    other = flip(columns_of(weight, [(1 - seq) * half], half))
    return ordered_pair(mine, other).reshape(-1, half)


def qkv_piece(pair, step):
    return columns_of(pair, [(corner_index() ^ step) * HEAD_COLS], HEAD_COLS)


def unspread_qkv(total, rows, rider):
    corner, seq = corner_index(), lax.axis_index("seq")
    count = rider.shape[-1]
    loads = [
        ride(pick(total, corner ^ j, 1).reshape(-1, HEAD_COLS), pick(rider, corner ^ j, 2))
        for j in range(TP)
    ]
    loads = [alight(from_corner(loads[j], j), 2 * rows, (2, 2, count)) for j in range(TP)]
    laid = turn_corners([load.reshape(2, rows, HEAD_COLS) for load, _ in loads])
    rider = sum(extra.astype(F32) for _, extra in loads)
    load = ride(pick(laid, 1 - seq, 1).reshape(-1, HEAD_COLS), pick(rider, 1 - seq, 1))
    other, extra = alight(flip(load), TP * rows, (2, count))
    rider = pick(rider, seq, 1) + extra.astype(F32)
    both = ordered_pair(pick(laid, seq, 1), other.reshape(TP, rows, HEAD_COLS))
    return jnp.concatenate([both[s, q] for s in range(2) for q in range(TP)], axis=1), rider


def pair_gateup(weight):
    seq, span = lax.axis_index("seq"), FF // 2
    mine = columns_of(weight, [seq * span, FF + seq * span], span)
    other = flip(columns_of(weight, [(1 - seq) * span, FF + (1 - seq) * span], span))
    return ordered_pair(mine, other).reshape(-1, FF)


def spread_gateup(pair, rider):
    column, span = column_index(), FF // (2 * TP)
    loads = []
    for k in range(TP):
        start = (column - k) % TP * span
        piece = columns_of(pair, [start, FF // 2 + start], span)
        loads.append(from_column(ride(piece, rider), k))
    loads = [alight(load, pair.shape[0], rider.shape) for load in loads]
    return jnp.concatenate([load for load, _ in loads], axis=0), [extra for _, extra in loads]


def collect_lines(block):
    shape = block.shape
    blocks = [
        (index, came.reshape(shape)) for index, came in gather_lines(block.reshape(-1, shape[-1]))
    ]
    return lay(blocks, 1).reshape(-1, shape[-1])


def order_places(came):
    places, columns = place_size(), came.shape[-1]
    came = came.reshape(places, TP, 2, -1, columns)
    full = jnp.zeros((2, TP, places, came.shape[3], columns), came.dtype)
    for k in range(TP):
        part = jnp.swapaxes(came[:, k], 0, 1)[:, None]
        full = lax.dynamic_update_slice(full, part, (0, (column_index() + k) % TP, 0, 0, 0))
    return full.reshape(-1, columns)


def unspread_places(values, rows, hold=()):
    span = values.shape[1]
    view = values.reshape(2, TP, place_size(), rows, span)
    total = scatter_places(lambda place: pick(view, place, 2).reshape(-1, span), hold)
    return total.astype(BF).reshape(2, TP, rows, span)


def column_piece(total, step):
    return pick(total, (column_index() - step) % TP, 1)


def lay_columns(pieces):
    laid = turn_columns(pieces)
    seq = lax.axis_index("seq")
    return ordered_pair(pick(laid, seq, 1), flip(pick(laid, 1 - seq, 1)))


def join_halves(halves):
    width = halves[0].shape[-1] // 2
    return jnp.concatenate(
        [
            halves[half][s, c, :, gate * width : (gate + 1) * width]
            for gate in range(2)
            for s in range(2)
            for c in range(TP)
            for half in range(2)
        ],
        axis=1,
    )


def norm_scale(values):
    return lax.rsqrt(jnp.mean(values * values, axis=-1, keepdims=True) + NORM_EPS)


def positions_of(seg_row):
    labels = jnp.arange(NCONT + 1, dtype=jnp.int32)
    member = (seg_row[:, None] == labels[None, :]).astype(jnp.int32)
    counts = jnp.sum(member, axis=0)
    starts = jnp.cumsum(counts) - counts
    own_start = jnp.sum(member * starts[None, :], axis=1)
    places = jnp.arange(seg_row.shape[0], dtype=jnp.int32)
    return places - own_start + jnp.where(seg_row > 0, counts[0], 0)


def rotary(positions):
    half_size = HD // 2
    frequency = THETA ** (-(jnp.arange(half_size, dtype=F32) * (2.0 / HD)))
    angles = positions.astype(F32)[:, None] * frequency[None, :]
    angles = jnp.concatenate([angles, angles], axis=-1)
    return (jnp.cos(angles), jnp.sin(angles))


def norm_back(d_normed, inputs_f, factor_rows, gain_row):
    weighted = d_normed * gain_row
    d_inputs = factor_rows * weighted - inputs_f * factor_rows**3 * jnp.mean(
        weighted * inputs_f, axis=-1, keepdims=True
    )
    d_gain = jnp.sum(d_normed * inputs_f * factor_rows, axis=0)
    return (d_inputs, d_gain)


def lamb_moments(masters, gradients, moment_ones, moment_twos):
    decay_rates = (DECAY, DECAY, DECAY, DECAY, 0.0)
    new_ones, new_twos, updates = ([], [], [])
    for master, gradient, old_one, old_two, decay_rate in zip(
        masters, gradients, moment_ones, moment_twos, decay_rates
    ):
        new_one = BETA1 * old_one + (1.0 - BETA1) * gradient
        new_two = BETA2 * old_two + (1.0 - BETA2) * gradient * gradient
        update = (
            new_one / (1.0 - BETA1**STEP) / (jnp.sqrt(new_two / (1.0 - BETA2**STEP)) + ADAM_EPS)
            + decay_rate * master
        )
        new_ones.append(new_one)
        new_twos.append(new_two)
        updates.append(update)
    return (new_ones, new_twos, updates)


SMALL = pl.CostEstimate(flops=10**9, bytes_accessed=1, transcendentals=0)
MIB = 1 << 20


def params(mebibytes):
    return pltpu.CompilerParams(vmem_limit_bytes=mebibytes * MIB)


def whole(shape):
    return pl.BlockSpec(shape, lambda step: (0,) * len(shape), pipeline_mode=pl.Buffered(1))


def at_group(shape, axis):
    return pl.BlockSpec(shape, lambda step: tuple(step if d == axis else 0 for d in range(len(shape))))


def half_sign():
    lane = lax.broadcasted_iota(jnp.int32, (1, HD), 1)
    return jnp.where(lane < HD // 2, -1.0, 1.0)


def scores_of(query, key_rows, allowed):
    return jnp.where(allowed, dot_last(query, key_rows) * HD ** (-0.5), MASKED)


def allowed_of(place_col, place_row, id_col, id_row):
    return (place_row <= place_col) & ((id_row == 0) | (id_row == id_col))


def attend_kernel(
    x_ref, gain_ref, qkv_ref, cos_ref, sin_ref, place_col, place_row, id_col, id_row,
    turned_ref, lse_ref, attended_ref,
):
    tokens = cos_ref.shape[1]
    x = x_ref[...].reshape(tokens, -1).astype(F32)
    normed = (x * norm_scale(x) * gain_ref[...]).astype(BF)
    projected = dot(normed, qkv_ref[...])
    cosine, sine = cos_ref[0], sin_ref[0] * half_sign()
    turned = []
    for head in range(GROUP + 2):
        values = projected[:, head * HD : (head + 1) * HD]
        if head <= GROUP:
            values = values * cosine + pltpu.roll(values, HD // 2, 1) * sine
        turned.append(values.astype(BF))
        turned_ref[0, :, head * HD : (head + 1) * HD] = turned[head]
    allowed = allowed_of(place_col[...], place_row[...], id_col[0], id_row[0])
    for head in range(GROUP):
        scores = scores_of(turned[head], turned[GROUP], allowed)
        row_max = jnp.max(scores, axis=-1, keepdims=True)
        exponent = jnp.exp(scores - row_max)
        row_total = jnp.sum(exponent, axis=-1, keepdims=True)
        lse_ref[0, head] = row_max + jnp.log(row_total)
        rows_out = dot((exponent / row_total).astype(BF), turned[GROUP + 1]).astype(BF)
        attended_ref[:, 0, :, head * HD : (head + 1) * HD] = rows_out.reshape(2, tokens // 2, HD)


def attend(x_all, gain, qkv_matrix, cosine, sine, marks):
    _, groups, half_tok, width = x_all.shape
    tokens = 2 * half_tok
    by_half = lambda columns: at_group((2, 1, half_tok, columns), 1)
    return pl.pallas_call(
        attend_kernel,
        grid=(groups,),
        in_specs=[
            by_half(width),
            whole((1, width)),
            whole((width, HEAD_COLS)),
            at_group((1, tokens, HD), 0),
            at_group((1, tokens, HD), 0),
            whole((tokens, 1)),
            whole((1, tokens)),
            at_group((1, tokens, 1), 0),
            at_group((1, 1, tokens), 0),
        ],
        out_specs=[
            at_group((1, tokens, HEAD_COLS), 0),
            at_group((1, GROUP, tokens, 1), 0),
            by_half(GROUP * HD),
        ],
        out_shape=[
            jax.ShapeDtypeStruct((groups, tokens, HEAD_COLS), BF),
            jax.ShapeDtypeStruct((groups, GROUP, tokens, 1), F32),
            jax.ShapeDtypeStruct((2, groups, half_tok, GROUP * HD), BF),
        ],
        compiler_params=params(32),
        cost_estimate=SMALL,
    )(x_all, gain, qkv_matrix, cosine, sine, *marks)


def attend_back_kernel(
    branch_ref, out_ref, qkv_ref, x_ref, gain_ref, attended_ref, turned_ref, lse_ref, cos_ref, sin_ref,
    place_col, place_row, id_col, id_row,
    mine_ref, other_ref, grad_qkv_ref, grad_out_ref, grad_gain_ref, qkv_sum, out_sum,
):
    tokens = cos_ref.shape[1]
    factor = HD ** (-0.5)
    first = pl.program_id(0) == 0
    last = pl.program_id(0) == pl.num_programs(0) - 1
    branch = branch_ref[...].reshape(tokens, -1)
    d_attended = dot_last(branch, out_ref[...]).astype(BF)
    turned = [turned_ref[0, :, head * HD : (head + 1) * HD] for head in range(GROUP + 2)]
    key_rows, value_rows = turned[GROUP], turned[GROUP + 1]
    allowed = allowed_of(place_col[...], place_row[...], id_col[0], id_row[0])
    cosine, sine, sign = cos_ref[0], sin_ref[0], half_sign()

    def unrope(values):
        values = values.astype(BF).astype(F32)
        return (values * cosine - sign * pltpu.roll(values * sine, HD // 2, 1)).astype(BF)

    d_keys = d_values = None
    columns = []
    for head in range(GROUP):
        d_rows = d_attended[:, head * HD : (head + 1) * HD]
        probs = jnp.exp(scores_of(turned[head], key_rows, allowed) - lse_ref[0, head])
        d_probs = dot_last(d_rows, value_rows)
        row_sum = jnp.sum(probs * d_probs, axis=-1, keepdims=True)
        d_scores = (probs * (d_probs - row_sum)).astype(BF)
        columns.append(unrope(dot(d_scores, key_rows) * factor))
        key_part = dot_rows(d_scores, turned[head]) * factor
        value_part = dot_rows(probs.astype(BF), d_rows)
        d_keys = key_part if d_keys is None else d_keys + key_part
        d_values = value_part if d_values is None else d_values + value_part
    columns.append(unrope(d_keys))
    columns.append(d_values.astype(BF))
    projected = jnp.concatenate(columns, axis=1)
    d_normed = dot_last(projected, qkv_ref[...])
    mine_ref[0] = d_normed[: tokens // 2]
    other_ref[0] = d_normed[tokens // 2 :].astype(BF)

    @pl.when(first)
    def _():
        qkv_sum[...] = jnp.zeros_like(qkv_sum)
        out_sum[...] = jnp.zeros_like(out_sum)
        grad_gain_ref[...] = jnp.zeros_like(grad_gain_ref)

    x = x_ref[...].reshape(tokens, -1).astype(F32)
    scaled = x * norm_scale(x)
    grad_gain_ref[...] += jnp.sum(d_normed * scaled, axis=0, keepdims=True)
    qkv_sum[...] += dot_rows((scaled * gain_ref[...]).astype(BF), projected)
    out_sum[...] += dot_rows(attended_ref[...].reshape(tokens, -1), branch)

    @pl.when(last)
    def _():
        grad_qkv_ref[...] = qkv_sum[...].astype(BF)
        grad_out_ref[...] = out_sum[...].astype(BF)


def attend_back(d_branch, out_matrix, qkv_matrix, x_all, gain, attended, turned, lse, cosine, sine, marks):
    _, groups, half_tok, width = d_branch.shape
    tokens = 2 * half_tok
    return pl.pallas_call(
        attend_back_kernel,
        grid=(groups,),
        in_specs=[
            at_group((2, 1, half_tok, width), 1),
            whole((GROUP * HD, width)),
            whole((width, HEAD_COLS)),
            at_group((2, 1, half_tok, width), 1),
            whole((1, width)),
            at_group((2, 1, half_tok, GROUP * HD), 1),
            at_group((1, tokens, HEAD_COLS), 0),
            at_group((1, GROUP, tokens, 1), 0),
            at_group((1, tokens, HD), 0),
            at_group((1, tokens, HD), 0),
            whole((tokens, 1)),
            whole((1, tokens)),
            at_group((1, tokens, 1), 0),
            at_group((1, 1, tokens), 0),
        ],
        out_specs=[
            at_group((1, half_tok, width), 0),
            at_group((1, half_tok, width), 0),
            whole((width, HEAD_COLS)),
            whole((GROUP * HD, width)),
            whole((1, width)),
        ],
        out_shape=[
            jax.ShapeDtypeStruct((groups, half_tok, width), F32),
            jax.ShapeDtypeStruct((groups, half_tok, width), BF),
            jax.ShapeDtypeStruct((width, HEAD_COLS), BF),
            jax.ShapeDtypeStruct((GROUP * HD, width), BF),
            jax.ShapeDtypeStruct((1, width), F32),
        ],
        scratch_shapes=[pltpu.VMEM((width, HEAD_COLS), F32), pltpu.VMEM((GROUP * HD, width), F32)],
        compiler_params=params(48),
        cost_estimate=SMALL,
    )(d_branch, out_matrix, qkv_matrix, x_all, gain, attended, turned, lse, cosine, sine, *marks)


def half_specs(rows, columns, steps):
    first = pl.BlockSpec((rows, columns), lambda step: (jnp.minimum(step, steps // 2 - 1), 0))
    second = pl.BlockSpec((rows, columns), lambda step: (jnp.maximum(step - steps // 2, 0), 0))
    shapes = [
        jax.ShapeDtypeStruct((rows * steps // 2, columns), F32),
        jax.ShapeDtypeStruct((rows * steps // 2, columns), BF),
    ]
    return [first, second], shapes


def store_halves(values, mine_ref, other_ref):
    step, half = pl.program_id(0), pl.num_programs(0) // 2

    @pl.when(step < half)
    def _():
        mine_ref[...] = values

    @pl.when(step >= half)
    def _():
        other_ref[...] = values.astype(BF)


def partial_kernel(left_ref, right_ref, mine_ref, other_ref):
    store_halves(dot(left_ref[...], right_ref[...]), mine_ref, other_ref)


def partial_product(left, right):
    tokens, depth = left.shape
    rows, steps = tokens // 4, 4
    specs, shapes = half_specs(rows, right.shape[1], steps)
    return pl.pallas_call(
        partial_kernel,
        grid=(steps,),
        in_specs=[at_group((rows, depth), 0), whole(right.shape)],
        out_specs=specs,
        out_shape=shapes,
        compiler_params=params(32),
        cost_estimate=SMALL,
    )(left, right)


def forward_back_kernel(
    normed_ref, og_ref, matrix_ref, down_ref,
    activated_ref, d_first_ref, d_second_ref, mine_ref, other_ref,
):
    width = matrix_ref.shape[1] // 4
    normed, og = normed_ref[...], og_ref[...]
    total = None
    for half, d_ref in enumerate((d_first_ref, d_second_ref)):
        gate_matrix = matrix_ref[:, half * width : (half + 1) * width]
        up_matrix = matrix_ref[:, (2 + half) * width : (3 + half) * width]
        gate, up = dot(normed, gate_matrix), dot(normed, up_matrix)
        d_act = dot_last(og, down_ref[half * width : (half + 1) * width])
        sigmoid = jax.nn.sigmoid(gate)
        silu = gate * sigmoid
        activated_ref[:, half * width : (half + 1) * width] = (silu * up).astype(BF)
        d_ref[:, :width] = (d_act * up * (sigmoid * (1.0 + gate * (1.0 - sigmoid)))).astype(BF)
        d_ref[:, width:] = (d_act * silu).astype(BF)
        back = dot_last(d_ref[:, :width], gate_matrix) + dot_last(d_ref[:, width:], up_matrix)
        total = back if total is None else total + back
    store_halves(total, mine_ref, other_ref)


def forward_back(normed2, og_all, gateup_matrix, down_matrix):
    tokens, width = normed2.shape
    unit = down_matrix.shape[0]
    rows, steps = tokens // 4, 4
    specs, shapes = half_specs(rows, width, steps)
    return pl.pallas_call(
        forward_back_kernel,
        grid=(steps,),
        in_specs=[
            at_group((rows, width), 0),
            at_group((rows, width), 0),
            whole((width, 2 * unit)),
            whole((unit, width)),
        ],
        out_specs=[at_group((rows, unit), 0)] * 3 + specs,
        out_shape=[jax.ShapeDtypeStruct((tokens, unit), BF)] * 3 + shapes,
        compiler_params=params(48),
        cost_estimate=SMALL,
    )(normed2, og_all, gateup_matrix, down_matrix)


def gradient_kernel(left_ref, right_ref, out_ref):
    out_ref[...] = dot_rows(left_ref[...], right_ref[...]).astype(BF)


def gradient(left, right):
    tokens, rows = left.shape
    block = min(rows, 256)
    return pl.pallas_call(
        gradient_kernel,
        grid=(rows // block,),
        in_specs=[at_group((tokens, block), 1), whole(right.shape)],
        out_specs=at_group((block, right.shape[1]), 0),
        out_shape=jax.ShapeDtypeStruct((rows, right.shape[1]), BF),
        compiler_params=params(32),
        cost_estimate=SMALL,
    )(left, right)


def shards(
    hidden_in,
    out_grad,
    segments,
    qkv_weight,
    out_weight,
    gateup_weight,
    down_weight,
    gain_weight,
    qkv_first,
    out_first,
    gateup_first,
    down_first,
    gain_first,
    qkv_second,
    out_second,
    gateup_second,
    down_second,
    gain_second,
):
    seq = lax.axis_index("seq")
    rows = qkv_weight.shape[0]
    tok_local = hidden_in.shape[1]
    group_tok = tok_local * lax.axis_size("seq")
    span = TP * tok_local
    owner = seq * shard_size() + lax.axis_index("shard")


    x_own, og_own = hidden_in[0], out_grad[0]
    x_local = x_own.astype(F32)
    recent()

    gain_cols, width = gain_weight.shape[1], x_own.shape[1]
    packed = place_size() == TP
    shard = lax.axis_index("shard")
    gain_low = gain_weight.astype(BF)
    info = jnp.concatenate([gain_low.reshape(-1), segments.reshape(-1).astype(BF)])
    og_mine = [og_own, from_column(og_own, 1), None, from_column(og_own, 3)]
    came = recent()
    qkv_pair = pair_qkv(qkv_weight.astype(BF))
    pair = pair_gateup(gateup_weight.astype(BF))
    pairs_came = recent()
    loads = [
        jnp.concatenate([x_own, qkv_piece(qkv_pair, j).reshape(tok_local, -1)], axis=1)
        for j in range(TP)
    ]
    loads = [ride(load, info) for load in loads]
    loads[3] = after(loads[3], *came[:1])
    loads = [from_corner(loads[j], j) for j in range(TP)]
    loads = [alight(load, tok_local, info.shape) for load in loads]
    x_mine = [load[:, :width] for load, _ in loads]
    infos = jnp.stack([extra for _, extra in loads])
    qkv_block = turn_corners([load[:, width:].reshape(-1, HEAD_COLS) for load, _ in loads])
    qkv_block = jnp.swapaxes(qkv_block.reshape(TP, 2, rows, HEAD_COLS), 0, 1)
    slot = (*came, *pairs_came, *recent())
    ids = [infos[j, 2 * gain_cols :].astype(jnp.int32) for j in range(TP)]

    down_matrix = gather_places(after(down_weight.astype(BF), *slot)).reshape(-1, width)
    gateup_block, infos = spread_gateup(after(pair, *slot), infos)
    infos = jnp.stack(infos)
    out_block = swap_roles(after(out_weight.astype(BF), *slot))
    slot = recent()

    qkv_matrix = collect_lines(after(qkv_block, *slot))
    came = recent()
    gateup_came = gather_places(after(gateup_block, down_matrix))
    gateup_matrix = order_places(gateup_came)
    x_half = jnp.concatenate([after(x_mine[0], *slot, down_matrix), *x_mine[1:]], axis=0)
    x_other, infos_other = alight(flip(ride(x_half, infos)), span, infos.shape)
    x_all = jnp.concatenate([x_half, x_other], axis=0).reshape(2, TP, tok_local, width)
    if packed:
        gains = ordered_pair(infos, infos_other)[..., : 2 * gain_cols]
        gains = turn_columns([turn_corners([gains[:, k, j] for j in range(TP)]) for k in range(TP)])
        gains = jnp.transpose(gains.reshape(TP, TP, 2, 2, gain_cols), (3, 2, 0, 1, 4)).reshape(2, width)
    else:
        gains = jnp.zeros((2, width), BF)
        gains = butterfly(lax.dynamic_update_slice(gains, gain_low, (0, owner * gain_cols)))
    gains = gains.astype(F32)
    slot = (*came, *recent(), x_all, gains)

    def local_order(values):
        return jnp.where(seq == 0, values, jnp.roll(values, -tok_local, axis=-1))

    positions = jnp.stack([local_order(positions_of(entry)) for entry in ids])
    ids = jnp.stack([local_order(entry) for entry in ids])
    places = local_order(jnp.arange(group_tok, dtype=jnp.int32))
    marks = (places[:, None], places[None, :], ids[:, :, None], ids[:, None, :])
    cosine, sine = rotary(positions.reshape(-1))
    cosine, sine = cosine.reshape(TP, group_tok, HD), sine.reshape(TP, group_tok, HD)

    out_matrix = lay(
        [(line_place(line), block) for line, block in gather_lines(after(out_block, *slot))], 0
    ).reshape(GROUP * HD, -1)
    og_mine[2] = from_column(after(og_own, *slot), 2)
    turned, lse, attended = attend(x_all, gains[:1], qkv_matrix, cosine, sine, marks)
    attended = attended.reshape(-1, GROUP * HD)
    slot = (*recent(), attended)

    met = meet_halves(*partial_product(after(attended, *slot, gateup_came), out_matrix))
    middle = x_local + met[0]
    for j in range(1, TP):
        middle = middle + from_corner(met[j].astype(BF), j).astype(F32)
    factor_two = norm_scale(middle)
    slot = recent()

    og_all = both_halves([after(entry, slot[0]) for entry in og_mine])

    normed2_own = after((middle * factor_two * gains[1]).astype(BF), *slot, *recent())
    normed2 = [from_column(normed2_own, k) for k in range(TP)]
    normed2 = both_halves([after(normed2[0], gateup_matrix, *recent()), *normed2[1:]])
    slot = recent()

    activated, d_gate_up_0, d_gate_up_1, d_mine, d_other = forward_back(
        after(normed2, *slot), og_all, gateup_matrix, down_matrix
    )

    d_met = meet_halves(d_mine, d_other)
    slot = recent()
    sends = [entry.astype(BF) for entry in d_met[1:]]
    grad_half_0 = gradient(after(normed2, d_other), d_gate_up_0)
    total_0 = unspread_places(after(grad_half_0, *slot), rows)
    out_mine, out_other = partial_product(after(activated, *slot, grad_half_0), down_matrix)
    grad_half_1 = gradient(after(normed2, *slot, grad_half_0), d_gate_up_1)
    d_normed2 = d_met[0]
    for k in range(1, TP):
        came = after(to_column(sends[k - 1], k), out_other, grad_half_1)
        d_normed2 = d_normed2 + came.astype(F32)
    d_mid_part, d_gain_two = norm_back(d_normed2, middle, factor_two, gains[1])
    d_middle = og_own.astype(F32) + d_mid_part
    slot = recent()

    d_branch_own = after(d_middle.astype(BF), *slot)
    d_branch_mine = [from_corner(d_branch_own, j) for j in range(TP)]
    came = recent()
    held = after(total_0, *slot, d_branch_own)
    pieces = [column_piece(held, k) for k in range(TP)]
    pieces[3] = after(pieces[3], *came)
    laid_0 = lay_columns([from_column(pieces[k], k) for k in range(TP)])
    out_met = meet_halves(out_mine, after(out_other, *slot))
    slot = (*came, *recent()[:3])

    sends = [after(entry.astype(BF), *slot) for entry in out_met]
    result = middle + out_met[0]
    for k in range(1, TP):
        result = result + to_column(sends[k], k).astype(F32)
    output = result.astype(BF)[None]
    out_came = recent()
    total_1 = unspread_places(after(grad_half_1, *slot), rows, out_came[:1])
    out_came = (*out_came, *recent())
    d_branch = both_halves([after(entry, *slot) for entry in d_branch_mine])
    in_mine, in_other, grad_qkv, grad_out, d_gain_one = attend_back(
        d_branch.reshape(2, TP, tok_local, width),
        out_matrix,
        qkv_matrix,
        x_all,
        gains[:1],
        attended.reshape(2, TP, tok_local, GROUP * HD),
        turned,
        lse,
        cosine,
        sine,
        marks,
    )
    grad_down = gradient(after(activated, *slot), og_all)
    in_other = after(in_other.reshape(-1, width), *out_came, grad_down)
    in_met = meet_halves(in_mine.reshape(-1, width), in_other)
    slot = (*recent(), *out_came)

    d_normed = in_met[0]
    for j in range(1, TP):
        d_normed = d_normed + from_corner(after(in_met[j].astype(BF), *slot), j).astype(F32)
    came = recent()
    d_gains = jnp.concatenate([d_gain_one, d_gain_two[None]], axis=0)
    qkv_view = after(grad_qkv, *slot).reshape(2, place_size(), TP, rows, HEAD_COLS)
    out_view = after(grad_out, *slot).reshape(place_size(), -1, width)
    if packed:
        rider = d_gains.reshape(2, 2, TP, TP, gain_cols)
        qkv_rows, loads = 2 * TP * rows, []
        for k in range(TP):
            line = (column_index() + k) % TP
            load = [pick(qkv_view, line, 1), pick(out_view, line, 0)]
            load = jnp.concatenate([entry.reshape(-1, HEAD_COLS) for entry in load], axis=0)
            loads.append(ride(load, pick(rider, line, 2)))
        sent_rows = qkv_rows + out_view.shape[1] * width // HEAD_COLS
        loads[3] = after(loads[3], *came)
        loads = [to_column(loads[k], k) for k in range(TP)]
        loads = [alight(entry, sent_rows, (2, 2, TP, gain_cols)) for entry in loads]
        rider = sum(extra.astype(F32) for _, extra in loads)
        qkv_total = sum(load[:qkv_rows].astype(F32) for load, _ in loads)
        grad_out = sum(load[qkv_rows:].astype(F32) for load, _ in loads).reshape(-1, width)
    else:
        qkv_total = scatter_lines(lambda line: pick(qkv_view, line, 1).reshape(-1, HEAD_COLS))
        grad_out = scatter_lines(lambda line: pick(out_view, line_place(line), 0))
        rider = jnp.zeros((2, 2, TP, gain_cols), F32)
    slot = recent()
    down_view = after(grad_down, *came).reshape(place_size(), -1, width)
    grad_down = scatter_places(lambda place: pick(down_view, place, 0), slot[:1])
    slot = (*came, *slot, *recent()[:2])
    factor_one = norm_scale(x_local)
    d_in_part = norm_back(d_normed, x_local, factor_one, gains[0])[0]
    input_grad = (d_middle + d_in_part).astype(BF)[None]

    held = after(total_1, *slot)
    laid_1 = lay_columns([from_column(column_piece(held, k), k) for k in range(TP)])
    grad_gateup = join_halves([laid_0, laid_1]).astype(F32)
    qkv_total = after(qkv_total.astype(BF), *slot).reshape(2, TP, rows, HEAD_COLS)
    grad_qkv, grad_gain = unspread_qkv(qkv_total, rows, rider)
    grad_qkv = grad_qkv.astype(F32)
    grad_out = swap_roles(after(grad_out.astype(BF), *slot)).astype(F32)
    if not packed:
        grad_gain = lax.dynamic_slice_in_dim(butterfly(d_gains), owner * gain_cols, gain_cols, 1)

    masters = (qkv_weight, out_weight, gateup_weight, down_weight, gain_weight)
    gradients = (grad_qkv, grad_out, grad_gateup, grad_down, grad_gain)
    new_ones, new_twos, updates = lamb_moments(
        masters,
        gradients,
        (qkv_first, out_first, gateup_first, down_first, gain_first),
        (qkv_second, out_second, gateup_second, down_second, gain_second),
    )

    def squares(arrays):
        return [jnp.sum(entry * entry) for entry in (*arrays[:4], *arrays[4])]


    def spots(entries):
        total = jnp.zeros((2, 6), F32)
        for row, column, value in entries:
            spot = np.zeros((2, 6), np.float32)
            spot[row, column] = 1.0
            total = total + value * spot
        return total

    entries = [
        (row, column, total)
        for row, arrays in enumerate((masters, updates))
        for column, total in enumerate(squares(arrays))
    ]
    known_first = lax.optimization_barrier(spots(entries[:6]))
    known_next = lax.optimization_barrier(spots([entries[7], entries[9]]))
    norms = known_first + known_next + spots([entries[6], entries[8], *entries[10:]])
    norms = jnp.sqrt(butterfly(norms))
    ratios = norms[0] / norms[1]
    news = [masters[slot] - RATE * ratios[slot] * updates[slot] for slot in range(4)]
    news.append(masters[4] - RATE * ratios[4:6][:, None] * updates[4])
    copies = [entry.astype(BF) for entry in news]
    recent()
    return (output, input_grad, *news, *new_ones, *new_twos, *copies, norms)


def solution(mesh):
    rows, columns = P(("seq", "shard"), None), P(None, ("seq", "shard"))
    tokens = P("shard", "seq", None)
    states = (rows, rows, rows, rows, columns)
    return jax.shard_map(
        shards,
        mesh=mesh,
        in_specs=(tokens, tokens, P("shard", None)) + states * 3,
        out_specs=(tokens, tokens) + states * 4 + (P(),),
        check_vma=False,
    )
```

```python
import jax
import jax.numpy as jnp
import numpy as np
from jax import lax
from jax.experimental import pallas as pl
from jax.experimental.pallas import tpu as pltpu
from jax.sharding import PartitionSpec as P

HQ = 16
KVH = 8
HD = 128
FF = 8192
NCONT = 2
STEP = 10
TP = 4


NORM_EPS = 1e-05
THETA = 1000000.0
BETA1 = 0.9
BETA2 = 0.999
ADAM_EPS = 1e-06
DECAY = 0.01
RATE = 0.5
MASKED = -1e30
GROUP = HQ // KVH
HEAD_COLS = (GROUP + 2) * HD
BF = jnp.bfloat16
F32 = jnp.float32


def dot(left, right):
    return jnp.dot(left, right, preferred_element_type=F32)


def dot_rows(left, right):
    return lax.dot_general(left, right, (((0,), (0,)), ((), ())), preferred_element_type=F32)


def dot_last(left, right):
    return lax.dot_general(left, right, (((1,), (1,)), ((), ())), preferred_element_type=F32)


def after(values, *others):
    return lax.optimization_barrier((values, *others))[0]


RECENT = []


def permute(values, axis, pairs):
    RECENT.append(lax.ppermute(values, axis, pairs))
    return RECENT[-1]


def recent():
    arrivals = tuple(RECENT)
    RECENT.clear()
    return arrivals


def shard_size():
    return lax.axis_size("shard")


def place_size():
    return shard_size() // TP


def shard_bits(count):
    return count.bit_length() - 1


def place_index():
    return lax.axis_index("shard") % place_size()


def column_index():
    return lax.axis_index("shard") // place_size()


def corner_index():
    return lax.axis_index("shard") % TP


def line_index():
    return lax.axis_index("shard") // TP


def line_place(line):
    middles = place_size() // TP
    return line % middles * TP + line // middles


def rotate(values, steps):
    count, places = shard_size(), place_size()
    pairs = [
        (entry, ((entry // places - steps) % TP) * places + entry % places)
        for entry in range(count)
    ]
    return permute(values, "shard", pairs)


def hop(values, change):
    return permute(values, "shard", [(i, i ^ change) for i in range(shard_size())])


def swap_roles(values):
    count, places = shard_size(), place_size()

    def partner(entry):
        column, middle, corner = entry // places, entry % places // TP, entry % TP
        return (corner * (places // TP) + middle) * TP + column

    return permute(values, "shard", [(i, partner(i)) for i in range(count)])


def flip(values):
    return permute(values, "seq", [(0, 1), (1, 0)])


def butterfly(values):
    for bit in reversed(range(shard_bits(shard_size()))):
        values = values + hop(values, 1 << bit)
    return values + flip(values)


def from_column(values, step):
    return rotate(values, step) if step else values


def to_column(values, step):
    return rotate(values, -step) if step else values


def from_corner(values, step):
    return hop(values, step) if step else values


def ride(load, extra):
    columns = load.shape[1]
    count = -(-extra.size // (16 * columns)) * 16 * columns
    extra = jnp.pad(extra.reshape(-1).astype(BF), (0, count - extra.size))
    return jnp.concatenate([load, extra.reshape(-1, columns)], axis=0)


def alight(load, rows, shape):
    size = 1
    for entry in shape:
        size *= entry
    return load[:rows], load[rows:].reshape(-1)[:size].reshape(shape)


def both_halves(mine):
    mine = jnp.concatenate(mine, axis=0)
    return jnp.concatenate([mine, flip(mine)], axis=0)


def meet_halves(mine, other):
    return jnp.split(mine + flip(other).astype(F32), TP)


def gather_bits(own, low_bit, bits):
    blocks = {0: own}
    for bit in range(bits):
        for entry in list(blocks):
            blocks[entry | (1 << bit)] = hop(blocks[entry], 1 << (low_bit + bit))
    return [blocks[entry] for entry in range(1 << bits)]


def scatter_bits(blocks, low_bit, bits):
    sums = {entry: block.astype(F32) for entry, block in enumerate(blocks)}
    for bit in reversed(range(bits)):
        for entry in range(1 << bit):
            came = hop(sums.pop(entry | (1 << bit)).astype(BF), 1 << (low_bit + bit))
            sums[entry] = sums[entry] + came.astype(F32)
    return sums[0]


def gather_places(own):
    places = place_size()
    groups = [[column * places + place for place in range(places)] for column in range(TP)]
    return lax.all_gather(own, "shard", axis_index_groups=groups)


def scatter_places(block_of, hold=(), finish=True):
    blocks = [block_of(place_index() ^ entry) for entry in range(place_size())]
    if place_size() != TP:
        total = scatter_bits(blocks, 0, shard_bits(place_size()))
        return total if finish else [total]
    blocks[3] = after(blocks[3], *hold)
    parts = [from_corner(blocks[j], j) for j in range(TP)]
    return sum(part.astype(F32) for part in parts) if finish else parts


def gather_lines(own):
    if place_size() == TP:
        return [((column_index() + k) % TP, from_column(own, k)) for k in range(TP)]
    blocks = gather_bits(own, 2, shard_bits(place_size()))
    return [(line_index() ^ entry, block) for entry, block in enumerate(blocks)]


def scatter_lines(block_of):
    if place_size() == TP:
        total = None
        for step in range(TP):
            came = to_column(block_of((column_index() + step) % TP), step).astype(F32)
            total = came if total is None else total + came
        return total
    return scatter_bits(
        [block_of(line_index() ^ entry) for entry in range(place_size())],
        2,
        shard_bits(place_size()),
    )


def lay(blocks, axis):
    shape = blocks[0][1].shape
    full = jnp.zeros(shape[:axis] + (len(blocks),) + shape[axis:], blocks[0][1].dtype)
    for index, block in blocks:
        starts = [0] * full.ndim
        starts[axis] = index
        full = lax.dynamic_update_slice(full, jnp.expand_dims(block, axis), starts)
    return full


def pick(values, index, axis):
    return lax.dynamic_index_in_dim(values, index, axis, keepdims=False)


def ordered_pair(mine, other):
    first = lax.axis_index("seq") == 0
    return jnp.stack([jnp.where(first, mine, other), jnp.where(first, other, mine)])


def turn_columns(blocks):
    twice = jnp.stack(blocks + blocks)
    return lax.dynamic_slice_in_dim(twice, (TP - column_index()) % TP, TP, 0)


def turn_corners(blocks):
    corner = corner_index()
    for bit in (1, 2):
        odd = corner // bit % 2 == 1
        blocks = [jnp.where(odd, blocks[j ^ bit], blocks[j]) for j in range(TP)]
    return jnp.stack(blocks)


def columns_of(source, starts, size):
    return jnp.concatenate(
        [lax.dynamic_slice_in_dim(source, start, size, 1) for start in starts], axis=1
    )


def pair_qkv(weight):
    seq = lax.axis_index("seq")
    half = TP * HEAD_COLS
    mine = columns_of(weight, [seq * half], half)
    other = flip(columns_of(weight, [(1 - seq) * half], half))
    return ordered_pair(mine, other).reshape(-1, half)


def qkv_piece(pair, step):
    return columns_of(pair, [(corner_index() ^ step) * HEAD_COLS], HEAD_COLS)


def unspread_qkv(total, rows, rider):
    corner, seq = corner_index(), lax.axis_index("seq")
    count = rider.shape[-1]
    loads = [
        ride(pick(total, corner ^ j, 1).reshape(-1, HEAD_COLS), pick(rider, corner ^ j, 2))
        for j in range(TP)
    ]
    loads = [alight(from_corner(loads[j], j), 2 * rows, (2, 2, count)) for j in range(TP)]
    laid = turn_corners([load.reshape(2, rows, HEAD_COLS) for load, _ in loads])
    rider = sum(extra.astype(F32) for _, extra in loads)
    load = ride(pick(laid, 1 - seq, 1).reshape(-1, HEAD_COLS), pick(rider, 1 - seq, 1))
    other, extra = alight(flip(load), TP * rows, (2, count))
    rider = pick(rider, seq, 1) + extra.astype(F32)
    both = ordered_pair(pick(laid, seq, 1), other.reshape(TP, rows, HEAD_COLS))
    return jnp.concatenate([both[s, q] for s in range(2) for q in range(TP)], axis=1), rider


def pair_gateup(weight):
    seq, span = lax.axis_index("seq"), FF // 2
    mine = columns_of(weight, [seq * span, FF + seq * span], span)
    other = flip(columns_of(weight, [(1 - seq) * span, FF + (1 - seq) * span], span))
    return ordered_pair(mine, other).reshape(-1, FF)


def spread_gateup(pair, rider):
    column, span = column_index(), FF // (2 * TP)
    loads = []
    for k in range(TP):
        start = (column - k) % TP * span
        piece = columns_of(pair, [start, FF // 2 + start], span)
        loads.append(from_column(ride(piece, rider), k))
    loads = [alight(load, pair.shape[0], rider.shape) for load in loads]
    return jnp.concatenate([load for load, _ in loads], axis=0), [extra for _, extra in loads]


def collect_lines(block):
    shape = block.shape
    blocks = [
        (index, came.reshape(shape)) for index, came in gather_lines(block.reshape(-1, shape[-1]))
    ]
    return lay(blocks, 1).reshape(-1, shape[-1])


def order_places(came):
    places, columns = place_size(), came.shape[-1]
    came = came.reshape(places, TP, 2, -1, columns)
    full = jnp.zeros((2, TP, places, came.shape[3], columns), came.dtype)
    for k in range(TP):
        part = jnp.swapaxes(came[:, k], 0, 1)[:, None]
        full = lax.dynamic_update_slice(full, part, (0, (column_index() + k) % TP, 0, 0, 0))
    return full.reshape(-1, columns)


def place_parts(values, rows, hold=()):
    span = values.shape[1]
    view = values.reshape(2, TP, place_size(), rows, span)
    return scatter_places(lambda place: pick(view, place, 2).reshape(-1, span), hold, False)


def place_total(parts, rows):
    total = sum(part.astype(F32) for part in parts)
    return total.astype(BF).reshape(2, TP, rows, -1)


def column_piece(total, step):
    return pick(total, (column_index() - step) % TP, 1)


def lay_columns(pieces):
    laid = turn_columns(pieces)
    seq = lax.axis_index("seq")
    return ordered_pair(pick(laid, seq, 1), flip(pick(laid, 1 - seq, 1)))


def norm_scale(values):
    return lax.rsqrt(jnp.mean(values * values, axis=-1, keepdims=True) + NORM_EPS)


def positions_of(seg_row):
    labels = jnp.arange(NCONT + 1, dtype=jnp.int32)
    member = (seg_row[:, None] == labels[None, :]).astype(jnp.int32)
    counts = jnp.sum(member, axis=0)
    starts = jnp.cumsum(counts) - counts
    own_start = jnp.sum(member * starts[None, :], axis=1)
    places = jnp.arange(seg_row.shape[0], dtype=jnp.int32)
    return places - own_start + jnp.where(seg_row > 0, counts[0], 0)


def rotary(positions):
    half_size = HD // 2
    frequency = THETA ** (-(jnp.arange(half_size, dtype=F32) * (2.0 / HD)))
    angles = positions.astype(F32)[:, None] * frequency[None, :]
    angles = jnp.concatenate([angles, angles], axis=-1)
    return (jnp.cos(angles), jnp.sin(angles))


def norm_back(d_normed, inputs_f, factor_rows, gain_row):
    weighted = d_normed * gain_row
    d_inputs = factor_rows * weighted - inputs_f * factor_rows**3 * jnp.mean(
        weighted * inputs_f, axis=-1, keepdims=True
    )
    d_gain = jnp.sum(d_normed * inputs_f * factor_rows, axis=0)
    return (d_inputs, d_gain)


def lamb_step(master, gradient, old_one, old_two, decay_rate):
    new_one = BETA1 * old_one + (1.0 - BETA1) * gradient
    new_two = BETA2 * old_two + (1.0 - BETA2) * gradient * gradient
    update = (
        new_one / (1.0 - BETA1**STEP) / (jnp.sqrt(new_two / (1.0 - BETA2**STEP)) + ADAM_EPS)
        + decay_rate * master
    )
    return new_one, new_two, update


SMALL = pl.CostEstimate(flops=10**9, bytes_accessed=1, transcendentals=0)
MIB = 1 << 20


def params(mebibytes):
    return pltpu.CompilerParams(vmem_limit_bytes=mebibytes * MIB)


def whole(shape):
    return pl.BlockSpec(shape, lambda step: (0,) * len(shape), pipeline_mode=pl.Buffered(1))


def at_group(shape, axis):
    return pl.BlockSpec(shape, lambda step: tuple(step if d == axis else 0 for d in range(len(shape))))


def half_sign():
    lane = lax.broadcasted_iota(jnp.int32, (1, HD), 1)
    return jnp.where(lane < HD // 2, -1.0, 1.0)


def scores_of(query, key_rows, allowed):
    return jnp.where(allowed, dot_last(query, key_rows) * HD ** (-0.5), MASKED)


def allowed_of(place_col, place_row, id_col, id_row):
    return (place_row <= place_col) & ((id_row == 0) | (id_row == id_col))


def attend_kernel(
    x_ref, gain_ref, qkv_ref, cos_ref, sin_ref, place_col, place_row, id_col, id_row,
    turned_ref, lse_ref, attended_ref,
):
    tokens = cos_ref.shape[1]
    x = x_ref[...].reshape(tokens, -1).astype(F32)
    normed = (x * norm_scale(x) * gain_ref[...]).astype(BF)
    projected = dot(normed, qkv_ref[...])
    cosine, sine = cos_ref[0], sin_ref[0] * half_sign()
    turned = []
    for head in range(GROUP + 2):
        values = projected[:, head * HD : (head + 1) * HD]
        if head <= GROUP:
            values = values * cosine + pltpu.roll(values, HD // 2, 1) * sine
        turned.append(values.astype(BF))
        turned_ref[0, :, head * HD : (head + 1) * HD] = turned[head]
    allowed = allowed_of(place_col[...], place_row[...], id_col[0], id_row[0])
    for head in range(GROUP):
        scores = scores_of(turned[head], turned[GROUP], allowed)
        row_max = jnp.max(scores, axis=-1, keepdims=True)
        exponent = jnp.exp(scores - row_max)
        row_total = jnp.sum(exponent, axis=-1, keepdims=True)
        lse_ref[0, head] = row_max + jnp.log(row_total)
        rows_out = dot((exponent / row_total).astype(BF), turned[GROUP + 1]).astype(BF)
        attended_ref[:, 0, :, head * HD : (head + 1) * HD] = rows_out.reshape(2, tokens // 2, HD)


def attend(x_all, gain, qkv_matrix, cosine, sine, marks):
    _, groups, half_tok, width = x_all.shape
    tokens = 2 * half_tok
    by_half = lambda columns: at_group((2, 1, half_tok, columns), 1)
    return pl.pallas_call(
        attend_kernel,
        grid=(groups,),
        in_specs=[
            by_half(width),
            whole((1, width)),
            whole((width, HEAD_COLS)),
            at_group((1, tokens, HD), 0),
            at_group((1, tokens, HD), 0),
            whole((tokens, 1)),
            whole((1, tokens)),
            at_group((1, tokens, 1), 0),
            at_group((1, 1, tokens), 0),
        ],
        out_specs=[
            at_group((1, tokens, HEAD_COLS), 0),
            at_group((1, GROUP, tokens, 1), 0),
            by_half(GROUP * HD),
        ],
        out_shape=[
            jax.ShapeDtypeStruct((groups, tokens, HEAD_COLS), BF),
            jax.ShapeDtypeStruct((groups, GROUP, tokens, 1), F32),
            jax.ShapeDtypeStruct((2, groups, half_tok, GROUP * HD), BF),
        ],
        compiler_params=params(32),
        cost_estimate=SMALL,
    )(x_all, gain, qkv_matrix, cosine, sine, *marks)


def attend_back_kernel(
    branch_ref, out_ref, qkv_ref, x_ref, gain_ref, attended_ref, turned_ref, lse_ref, cos_ref, sin_ref,
    place_col, place_row, id_col, id_row,
    mine_ref, other_ref, grad_qkv_ref, grad_out_ref, grad_gain_ref, qkv_sum, out_sum,
):
    tokens = cos_ref.shape[1]
    factor = HD ** (-0.5)
    first = pl.program_id(0) == 0
    last = pl.program_id(0) == pl.num_programs(0) - 1
    branch = branch_ref[...].reshape(tokens, -1)
    d_attended = dot_last(branch, out_ref[...]).astype(BF)
    turned = [turned_ref[0, :, head * HD : (head + 1) * HD] for head in range(GROUP + 2)]
    key_rows, value_rows = turned[GROUP], turned[GROUP + 1]
    allowed = allowed_of(place_col[...], place_row[...], id_col[0], id_row[0])
    cosine, sine, sign = cos_ref[0], sin_ref[0], half_sign()

    def unrope(values):
        values = values.astype(BF).astype(F32)
        return (values * cosine - sign * pltpu.roll(values * sine, HD // 2, 1)).astype(BF)

    d_keys = d_values = None
    columns = []
    for head in range(GROUP):
        d_rows = d_attended[:, head * HD : (head + 1) * HD]
        probs = jnp.exp(scores_of(turned[head], key_rows, allowed) - lse_ref[0, head])
        d_probs = dot_last(d_rows, value_rows)
        row_sum = jnp.sum(probs * d_probs, axis=-1, keepdims=True)
        d_scores = (probs * (d_probs - row_sum)).astype(BF)
        columns.append(unrope(dot(d_scores, key_rows) * factor))
        key_part = dot_rows(d_scores, turned[head]) * factor
        value_part = dot_rows(probs.astype(BF), d_rows)
        d_keys = key_part if d_keys is None else d_keys + key_part
        d_values = value_part if d_values is None else d_values + value_part
    columns.append(unrope(d_keys))
    columns.append(d_values.astype(BF))
    projected = jnp.concatenate(columns, axis=1)
    d_normed = dot_last(projected, qkv_ref[...])
    mine_ref[0] = d_normed[: tokens // 2]
    other_ref[0] = d_normed[tokens // 2 :].astype(BF)

    @pl.when(first)
    def _():
        qkv_sum[...] = jnp.zeros_like(qkv_sum)
        out_sum[...] = jnp.zeros_like(out_sum)
        grad_gain_ref[...] = jnp.zeros_like(grad_gain_ref)

    x = x_ref[...].reshape(tokens, -1).astype(F32)
    scaled = x * norm_scale(x)
    grad_gain_ref[...] += jnp.sum(d_normed * scaled, axis=0, keepdims=True)
    qkv_sum[...] += dot_rows((scaled * gain_ref[...]).astype(BF), projected)
    out_sum[...] += dot_rows(attended_ref[...].reshape(tokens, -1), branch)

    @pl.when(last)
    def _():
        grad_qkv_ref[...] = qkv_sum[...].astype(BF)
        grad_out_ref[...] = out_sum[...].astype(BF)


def attend_back(d_branch, out_matrix, qkv_matrix, x_all, gain, attended, turned, lse, cosine, sine, marks):
    _, groups, half_tok, width = d_branch.shape
    tokens = 2 * half_tok
    return pl.pallas_call(
        attend_back_kernel,
        grid=(groups,),
        in_specs=[
            at_group((2, 1, half_tok, width), 1),
            whole((GROUP * HD, width)),
            whole((width, HEAD_COLS)),
            at_group((2, 1, half_tok, width), 1),
            whole((1, width)),
            at_group((2, 1, half_tok, GROUP * HD), 1),
            at_group((1, tokens, HEAD_COLS), 0),
            at_group((1, GROUP, tokens, 1), 0),
            at_group((1, tokens, HD), 0),
            at_group((1, tokens, HD), 0),
            whole((tokens, 1)),
            whole((1, tokens)),
            at_group((1, tokens, 1), 0),
            at_group((1, 1, tokens), 0),
        ],
        out_specs=[
            at_group((1, half_tok, width), 0),
            at_group((1, half_tok, width), 0),
            whole((width, HEAD_COLS)),
            whole((GROUP * HD, width)),
            whole((1, width)),
        ],
        out_shape=[
            jax.ShapeDtypeStruct((groups, half_tok, width), F32),
            jax.ShapeDtypeStruct((groups, half_tok, width), BF),
            jax.ShapeDtypeStruct((width, HEAD_COLS), BF),
            jax.ShapeDtypeStruct((GROUP * HD, width), BF),
            jax.ShapeDtypeStruct((1, width), F32),
        ],
        scratch_shapes=[pltpu.VMEM((width, HEAD_COLS), F32), pltpu.VMEM((GROUP * HD, width), F32)],
        compiler_params=params(48),
        cost_estimate=SMALL,
    )(d_branch, out_matrix, qkv_matrix, x_all, gain, attended, turned, lse, cosine, sine, *marks)


def half_specs(rows, columns, steps):
    first = pl.BlockSpec((rows, columns), lambda step: (jnp.minimum(step, steps // 2 - 1), 0))
    second = pl.BlockSpec((rows, columns), lambda step: (jnp.maximum(step - steps // 2, 0), 0))
    shapes = [
        jax.ShapeDtypeStruct((rows * steps // 2, columns), F32),
        jax.ShapeDtypeStruct((rows * steps // 2, columns), BF),
    ]
    return [first, second], shapes


def store_halves(values, mine_ref, other_ref):
    step, half = pl.program_id(0), pl.num_programs(0) // 2

    @pl.when(step < half)
    def _():
        mine_ref[...] = values

    @pl.when(step >= half)
    def _():
        other_ref[...] = values.astype(BF)


def partial_kernel(left_ref, right_ref, mine_ref, other_ref):
    store_halves(dot(left_ref[...], right_ref[...]), mine_ref, other_ref)


def partial_product(left, right):
    tokens, depth = left.shape
    rows, steps = tokens // 4, 4
    specs, shapes = half_specs(rows, right.shape[1], steps)
    return pl.pallas_call(
        partial_kernel,
        grid=(steps,),
        in_specs=[at_group((rows, depth), 0), whole(right.shape)],
        out_specs=specs,
        out_shape=shapes,
        compiler_params=params(32),
        cost_estimate=SMALL,
    )(left, right)


def forward_back_kernel(
    normed_ref, og_ref, matrix_ref, down_ref,
    activated_ref, d_first_ref, d_second_ref, mine_ref, other_ref,
):
    width = matrix_ref.shape[1] // 4
    normed, og = normed_ref[...], og_ref[...]
    total = None
    for half, d_ref in enumerate((d_first_ref, d_second_ref)):
        gate_matrix = matrix_ref[:, half * width : (half + 1) * width]
        up_matrix = matrix_ref[:, (2 + half) * width : (3 + half) * width]
        gate, up = dot(normed, gate_matrix), dot(normed, up_matrix)
        d_act = dot_last(og, down_ref[half * width : (half + 1) * width])
        sigmoid = jax.nn.sigmoid(gate)
        silu = gate * sigmoid
        activated_ref[:, half * width : (half + 1) * width] = (silu * up).astype(BF)
        d_ref[:, :width] = (d_act * up * (sigmoid * (1.0 + gate * (1.0 - sigmoid)))).astype(BF)
        d_ref[:, width:] = (d_act * silu).astype(BF)
        back = dot_last(d_ref[:, :width], gate_matrix) + dot_last(d_ref[:, width:], up_matrix)
        total = back if total is None else total + back
    store_halves(total, mine_ref, other_ref)


def forward_back(normed2, og_all, gateup_matrix, down_matrix):
    tokens, width = normed2.shape
    unit = down_matrix.shape[0]
    rows, steps = tokens // 4, 4
    specs, shapes = half_specs(rows, width, steps)
    return pl.pallas_call(
        forward_back_kernel,
        grid=(steps,),
        in_specs=[
            at_group((rows, width), 0),
            at_group((rows, width), 0),
            whole((width, 2 * unit)),
            whole((unit, width)),
        ],
        out_specs=[at_group((rows, unit), 0)] * 3 + specs,
        out_shape=[jax.ShapeDtypeStruct((tokens, unit), BF)] * 3 + shapes,
        compiler_params=params(48),
        cost_estimate=SMALL,
    )(normed2, og_all, gateup_matrix, down_matrix)


def gradient_kernel(left_ref, right_ref, out_ref):
    out_ref[...] = dot_rows(left_ref[...], right_ref[...]).astype(BF)


def gradient(left, right):
    tokens, rows = left.shape
    block = min(rows, 256)
    return pl.pallas_call(
        gradient_kernel,
        grid=(rows // block,),
        in_specs=[at_group((tokens, block), 1), whole(right.shape)],
        out_specs=at_group((block, right.shape[1]), 0),
        out_shape=jax.ShapeDtypeStruct((rows, right.shape[1]), BF),
        compiler_params=params(32),
        cost_estimate=SMALL,
    )(left, right)


def lamb_kernel(
    master_ref, one_ref, two_ref, first_ref, second_ref, new_one_ref, new_two_ref, update_ref, sums_ref
):
    gradient = jnp.concatenate([first_ref[0, 0], second_ref[0, 0]], axis=1).astype(F32)
    master = master_ref[...]
    new_one, new_two, update = lamb_step(master, gradient, one_ref[...], two_ref[...], DECAY)
    new_one_ref[...], new_two_ref[...], update_ref[...] = new_one, new_two, update

    @pl.when(pl.program_id(0) == 0)
    def _():
        sums_ref[...] = jnp.zeros_like(sums_ref)

    sums_ref[0:1] += jnp.sum(master * master, axis=0, keepdims=True)
    sums_ref[1:2] += jnp.sum(update * update, axis=0, keepdims=True)


def lamb_gateup(master, old_one, old_two, halves):
    rows, columns = master.shape
    span = columns // (4 * TP)
    state = pl.BlockSpec((rows, span), lambda step: (0, step))
    piece = pl.BlockSpec(
        (1, 1, rows, span // 2), lambda step: (step // TP % 2, step % TP, 0, step // (2 * TP))
    )
    shape = jax.ShapeDtypeStruct(master.shape, F32)
    return pl.pallas_call(
        lamb_kernel,
        grid=(4 * TP,),
        in_specs=[state] * 3 + [piece] * 2,
        out_specs=[state] * 3 + [whole((2, span))],
        out_shape=[shape] * 3 + [jax.ShapeDtypeStruct((2, span), F32)],
        compiler_params=params(32),
        cost_estimate=SMALL,
    )(master, old_one, old_two, *halves)


def shards(
    hidden_in,
    out_grad,
    segments,
    qkv_weight,
    out_weight,
    gateup_weight,
    down_weight,
    gain_weight,
    qkv_first,
    out_first,
    gateup_first,
    down_first,
    gain_first,
    qkv_second,
    out_second,
    gateup_second,
    down_second,
    gain_second,
):
    seq = lax.axis_index("seq")
    rows = qkv_weight.shape[0]
    tok_local = hidden_in.shape[1]
    group_tok = tok_local * lax.axis_size("seq")
    span = TP * tok_local
    owner = seq * shard_size() + lax.axis_index("shard")


    x_own, og_own = hidden_in[0], out_grad[0]
    x_local = x_own.astype(F32)
    recent()

    gain_cols, width = gain_weight.shape[1], x_own.shape[1]
    packed = place_size() == TP
    shard = lax.axis_index("shard")
    gain_low = gain_weight.astype(BF)
    info = jnp.concatenate([gain_low.reshape(-1), segments.reshape(-1).astype(BF)])
    og_mine = [og_own, from_column(og_own, 1), None, from_column(og_own, 3)]
    came = recent()
    qkv_pair = pair_qkv(qkv_weight.astype(BF))
    pair = pair_gateup(gateup_weight.astype(BF))
    pairs_came = recent()
    loads = [
        jnp.concatenate([x_own, qkv_piece(qkv_pair, j).reshape(tok_local, -1)], axis=1)
        for j in range(TP)
    ]
    loads = [ride(load, info) for load in loads]
    loads[3] = after(loads[3], *came[:1])
    loads = [from_corner(loads[j], j) for j in range(TP)]
    loads = [alight(load, tok_local, info.shape) for load in loads]
    x_mine = [load[:, :width] for load, _ in loads]
    infos = jnp.stack([extra for _, extra in loads])
    qkv_block = turn_corners([load[:, width:].reshape(-1, HEAD_COLS) for load, _ in loads])
    qkv_block = jnp.swapaxes(qkv_block.reshape(TP, 2, rows, HEAD_COLS), 0, 1)
    slot = (*came, *pairs_came, *recent())
    ids = [infos[j, 2 * gain_cols :].astype(jnp.int32) for j in range(TP)]

    down_matrix = gather_places(after(down_weight.astype(BF), *slot)).reshape(-1, width)
    gateup_block, infos = spread_gateup(after(pair, *slot), infos)
    infos = jnp.stack(infos)
    out_block = swap_roles(after(out_weight.astype(BF), *slot))
    slot = recent()

    qkv_matrix = collect_lines(after(qkv_block, *slot))
    came = recent()
    gateup_came = gather_places(after(gateup_block, down_matrix))
    gateup_matrix = order_places(gateup_came)
    x_half = jnp.concatenate([after(x_mine[0], *slot, down_matrix), *x_mine[1:]], axis=0)
    x_other, infos_other = alight(flip(ride(x_half, infos)), span, infos.shape)
    x_all = jnp.concatenate([x_half, x_other], axis=0).reshape(2, TP, tok_local, width)
    if packed:
        gains = ordered_pair(infos, infos_other)[..., : 2 * gain_cols]
        gains = turn_columns([turn_corners([gains[:, k, j] for j in range(TP)]) for k in range(TP)])
        gains = jnp.transpose(gains.reshape(TP, TP, 2, 2, gain_cols), (3, 2, 0, 1, 4)).reshape(2, width)
    else:
        gains = jnp.zeros((2, width), BF)
        gains = butterfly(lax.dynamic_update_slice(gains, gain_low, (0, owner * gain_cols)))
    gains = gains.astype(F32)
    slot = (*came, *recent(), x_all, gains)

    def local_order(values):
        return jnp.where(seq == 0, values, jnp.roll(values, -tok_local, axis=-1))

    positions = jnp.stack([local_order(positions_of(entry)) for entry in ids])
    ids = jnp.stack([local_order(entry) for entry in ids])
    places = local_order(jnp.arange(group_tok, dtype=jnp.int32))
    marks = (places[:, None], places[None, :], ids[:, :, None], ids[:, None, :])
    cosine, sine = rotary(positions.reshape(-1))
    cosine, sine = cosine.reshape(TP, group_tok, HD), sine.reshape(TP, group_tok, HD)

    out_matrix = lay(
        [(line_place(line), block) for line, block in gather_lines(after(out_block, *slot))], 0
    ).reshape(GROUP * HD, -1)
    came = recent()
    og_mine[2] = from_column(after(og_own, *slot), 2)
    recent()
    turned, lse, attended = attend(x_all, gains[:1], qkv_matrix, cosine, sine, marks)
    attended = attended.reshape(-1, GROUP * HD)
    slot = (*came, attended)

    met = meet_halves(*partial_product(after(attended, *slot, gateup_came), out_matrix))
    middle = x_local + met[0]
    for j in range(1, TP):
        middle = middle + from_corner(met[j].astype(BF), j).astype(F32)
    factor_two = norm_scale(middle)
    slot = recent()

    og_all = both_halves([after(entry, *slot) for entry in og_mine])
    recent()

    normed2_own = after((middle * factor_two * gains[1]).astype(BF), *slot, og_mine[2])
    normed2 = [from_column(normed2_own, k) for k in range(TP)]
    normed2 = both_halves([after(normed2[0], gateup_matrix, *recent()), *normed2[1:]])
    slot = recent()

    activated, d_gate_up_0, d_gate_up_1, d_mine, d_other = forward_back(
        after(normed2, *slot), og_all, gateup_matrix, down_matrix
    )

    d_met = meet_halves(d_mine, d_other)
    slot = recent()
    sends = [entry.astype(BF) for entry in d_met[1:]]
    grad_half_0 = gradient(after(normed2, d_other), d_gate_up_0)
    total_0 = place_total(place_parts(after(grad_half_0, *slot), rows), rows)
    out_mine, out_other = partial_product(after(activated, *slot, grad_half_0), down_matrix)
    grad_half_1 = gradient(after(normed2, *slot, grad_half_0), d_gate_up_1)
    d_normed2 = d_met[0]
    for k in range(1, TP):
        came = after(to_column(sends[k - 1], k), out_other, grad_half_1)
        d_normed2 = d_normed2 + came.astype(F32)
    d_mid_part, d_gain_two = norm_back(d_normed2, middle, factor_two, gains[1])
    d_middle = og_own.astype(F32) + d_mid_part
    slot = recent()

    d_branch_own = after(d_middle.astype(BF), *slot)
    d_branch_mine = [from_corner(d_branch_own, j) for j in range(TP)]
    came = recent()
    held = after(total_0, *slot, d_branch_own)
    pieces = [column_piece(held, k) for k in range(TP)]
    pieces[3] = after(pieces[3], *came)
    laid_0 = lay_columns([from_column(pieces[k], k) for k in range(TP)])
    out_met = meet_halves(out_mine, after(out_other, *slot))
    slot = (*came, *recent()[:3])

    sends = [after(entry.astype(BF), *slot) for entry in out_met]
    result = middle + out_met[0]
    for k in range(1, TP):
        result = result + to_column(sends[k], k).astype(F32)
    output = result.astype(BF)[None]
    out_came = recent()
    parts_1 = place_parts(after(grad_half_1, *slot), rows, out_came[:1])
    out_came = (*out_came, *recent())
    d_branch = both_halves([after(entry, *slot) for entry in d_branch_mine])
    in_mine, in_other, grad_qkv, grad_out, d_gain_one = attend_back(
        d_branch.reshape(2, TP, tok_local, width),
        out_matrix,
        qkv_matrix,
        x_all,
        gains[:1],
        attended.reshape(2, TP, tok_local, GROUP * HD),
        turned,
        lse,
        cosine,
        sine,
        marks,
    )
    grad_down = gradient(after(activated, *slot), og_all)
    in_other = after(in_other.reshape(-1, width), *out_came, grad_down)
    in_met = meet_halves(in_mine.reshape(-1, width), in_other)
    slot = (*recent(), *out_came)

    d_normed = in_met[0]
    for j in range(1, TP):
        d_normed = d_normed + from_corner(after(in_met[j].astype(BF), *slot), j).astype(F32)
    came = recent()
    d_gains = jnp.concatenate([d_gain_one, d_gain_two[None]], axis=0)
    qkv_view = after(grad_qkv, *slot).reshape(2, place_size(), TP, rows, HEAD_COLS)
    out_view = after(grad_out, *slot).reshape(place_size(), -1, width)
    if packed:
        rider = d_gains.reshape(2, 2, TP, TP, gain_cols)
        qkv_rows, loads = 2 * TP * rows, []
        for k in range(TP):
            line = (column_index() + k) % TP
            load = [pick(qkv_view, line, 1), pick(out_view, line, 0)]
            load = jnp.concatenate([entry.reshape(-1, HEAD_COLS) for entry in load], axis=0)
            loads.append(ride(load, pick(rider, line, 2)))
        sent_rows = qkv_rows + out_view.shape[1] * width // HEAD_COLS
        loads[3] = after(loads[3], *came)
        loads = [to_column(loads[k], k) for k in range(TP)]
        loads = [alight(entry, sent_rows, (2, 2, TP, gain_cols)) for entry in loads]
        rider = sum(extra.astype(F32) for _, extra in loads)
        qkv_total = sum(load[:qkv_rows].astype(F32) for load, _ in loads)
        grad_out = sum(load[qkv_rows:].astype(F32) for load, _ in loads).reshape(-1, width)
    else:
        qkv_total = scatter_lines(lambda line: pick(qkv_view, line, 1).reshape(-1, HEAD_COLS))
        grad_out = scatter_lines(lambda line: pick(out_view, line_place(line), 0))
        rider = jnp.zeros((2, 2, TP, gain_cols), F32)
    slot = recent()
    down_view = after(grad_down, *came).reshape(place_size(), -1, width)
    grad_down = scatter_places(lambda place: pick(down_view, place, 0), slot[:1])
    slot = (*came, *slot, *recent()[:2])
    factor_one = norm_scale(x_local)
    d_in_part = norm_back(d_normed, x_local, factor_one, gains[0])[0]
    input_grad = (d_middle + d_in_part).astype(BF)[None]

    held = after(place_total([after(part, *came) for part in parts_1], rows), *slot)
    laid_1 = lay_columns([from_column(column_piece(held, k), k) for k in range(TP)])
    qkv_total = after(qkv_total.astype(BF), *slot).reshape(2, TP, rows, HEAD_COLS)
    grad_qkv, grad_gain = unspread_qkv(qkv_total, rows, rider)
    grad_qkv = grad_qkv.astype(F32)
    grad_out = swap_roles(after(grad_out.astype(BF), *slot)).astype(F32)
    if not packed:
        grad_gain = lax.dynamic_slice_in_dim(butterfly(d_gains), owner * gain_cols, gain_cols, 1)

    masters = (qkv_weight, out_weight, gateup_weight, down_weight, gain_weight)
    gateup_one, gateup_two, gateup_update, gateup_sums = lamb_gateup(
        gateup_weight, gateup_first, gateup_second, [laid_0, laid_1]
    )
    steps = [
        lamb_step(*entry)
        for entry in (
            (qkv_weight, grad_qkv, qkv_first, qkv_second, DECAY),
            (out_weight, grad_out, out_first, out_second, DECAY),
            (down_weight, grad_down, down_first, down_second, DECAY),
            (gain_weight, grad_gain, gain_first, gain_second, 0.0),
        )
    ]
    steps.insert(2, (gateup_one, gateup_two, gateup_update))
    new_ones, new_twos, updates = zip(*steps)

    def squares(arrays):
        return [jnp.sum(entry * entry) for entry in arrays]

    totals = [
        [*squares(entry[:2]), jnp.sum(gateup_sums[row]), *squares((entry[3], *entry[4]))]
        for row, entry in enumerate((masters, updates))
    ]

    def spots(entries):
        total = jnp.zeros((2, 6), F32)
        for row, column, value in entries:
            spot = np.zeros((2, 6), np.float32)
            spot[row, column] = 1.0
            total = total + value * spot
        return total

    entries = [
        (row, column, total)
        for row in range(2)
        for column, total in enumerate(totals[row])
    ]
    early = [entries[slot] for slot in (0, 1, 3, 4, 5, 6, 7, 9, 10, 11)]
    norms = lax.optimization_barrier(spots(early)) + spots([entries[2], entries[8]])
    norms = jnp.sqrt(butterfly(norms))
    ratios = norms[0] / norms[1]
    news = [masters[slot] - RATE * ratios[slot] * updates[slot] for slot in range(4)]
    news.append(masters[4] - RATE * ratios[4:6][:, None] * updates[4])
    copies = [entry.astype(BF) for entry in news]
    recent()
    return (output, input_grad, *news, *new_ones, *new_twos, *copies, norms)


def solution(mesh):
    rows, columns = P(("seq", "shard"), None), P(None, ("seq", "shard"))
    tokens = P("shard", "seq", None)
    states = (rows, rows, rows, rows, columns)
    return jax.shard_map(
        shards,
        mesh=mesh,
        in_specs=(tokens, tokens, P("shard", None)) + states * 3,
        out_specs=(tokens, tokens) + states * 4 + (P(),),
        check_vma=False,
    )
```

```python
import jax
import jax.numpy as jnp
import numpy as np
from jax import lax
from jax.experimental import pallas as pl
from jax.experimental.pallas import tpu as pltpu
from jax.sharding import PartitionSpec as P

HQ = 16
KVH = 8
HD = 128
FF = 8192
NCONT = 2
STEP = 10
TP = 4


NORM_EPS = 1e-05
THETA = 1000000.0
BETA1 = 0.9
BETA2 = 0.999
ADAM_EPS = 1e-06
DECAY = 0.01
RATE = 0.5
MASKED = -1e30
GROUP = HQ // KVH
HEAD_COLS = (GROUP + 2) * HD
BF = jnp.bfloat16
F32 = jnp.float32


def dot(left, right):
    return jnp.dot(left, right, preferred_element_type=F32)


def dot_rows(left, right):
    return lax.dot_general(left, right, (((0,), (0,)), ((), ())), preferred_element_type=F32)


def dot_last(left, right):
    return lax.dot_general(left, right, (((1,), (1,)), ((), ())), preferred_element_type=F32)


def after(values, *others):
    return lax.optimization_barrier((values, *others))[0]


RECENT = []


def permute(values, axis, pairs):
    RECENT.append(lax.ppermute(values, axis, pairs))
    return RECENT[-1]


def recent():
    arrivals = tuple(RECENT)
    RECENT.clear()
    return arrivals


def shard_size():
    return lax.axis_size("shard")


def place_size():
    return shard_size() // TP


def shard_bits(count):
    return count.bit_length() - 1


def place_index():
    return lax.axis_index("shard") % place_size()


def column_index():
    return lax.axis_index("shard") // place_size()


def corner_index():
    return lax.axis_index("shard") % TP


def line_index():
    return lax.axis_index("shard") // TP


def line_place(line):
    middles = place_size() // TP
    return line % middles * TP + line // middles


def rotate(values, steps):
    count, places = shard_size(), place_size()
    pairs = [
        (entry, ((entry // places - steps) % TP) * places + entry % places)
        for entry in range(count)
    ]
    return permute(values, "shard", pairs)


def hop(values, change):
    return permute(values, "shard", [(i, i ^ change) for i in range(shard_size())])


def swap_roles(values):
    count, places = shard_size(), place_size()

    def partner(entry):
        column, middle, corner = entry // places, entry % places // TP, entry % TP
        return (corner * (places // TP) + middle) * TP + column

    return permute(values, "shard", [(i, partner(i)) for i in range(count)])


def flip(values):
    return permute(values, "seq", [(0, 1), (1, 0)])


def butterfly(values):
    for bit in reversed(range(shard_bits(shard_size()))):
        values = values + hop(values, 1 << bit)
    return values + flip(values)


def from_column(values, step):
    return rotate(values, step) if step else values


def to_column(values, step):
    return rotate(values, -step) if step else values


def from_corner(values, step):
    return hop(values, step) if step else values


def ride(load, extra):
    columns = load.shape[1]
    count = -(-extra.size // (16 * columns)) * 16 * columns
    extra = jnp.pad(extra.reshape(-1).astype(BF), (0, count - extra.size))
    return jnp.concatenate([load, extra.reshape(-1, columns)], axis=0)


def alight(load, rows, shape):
    size = 1
    for entry in shape:
        size *= entry
    return load[:rows], load[rows:].reshape(-1)[:size].reshape(shape)


def both_halves(mine):
    mine = jnp.concatenate(mine, axis=0)
    return jnp.concatenate([mine, flip(mine)], axis=0)


def meet_halves(mine, other):
    return jnp.split(mine.astype(F32) + flip(other).astype(F32), TP)


def gather_bits(own, low_bit, bits):
    blocks = {0: own}
    for bit in range(bits):
        for entry in list(blocks):
            blocks[entry | (1 << bit)] = hop(blocks[entry], 1 << (low_bit + bit))
    return [blocks[entry] for entry in range(1 << bits)]


def scatter_bits(blocks, low_bit, bits):
    sums = {entry: block.astype(F32) for entry, block in enumerate(blocks)}
    for bit in reversed(range(bits)):
        for entry in range(1 << bit):
            came = hop(sums.pop(entry | (1 << bit)).astype(BF), 1 << (low_bit + bit))
            sums[entry] = sums[entry] + came.astype(F32)
    return sums[0]


def gather_places(own):
    places = place_size()
    groups = [[column * places + place for place in range(places)] for column in range(TP)]
    return lax.all_gather(own, "shard", axis_index_groups=groups)


def scatter_places(block_of, hold=(), finish=True):
    blocks = [block_of(place_index() ^ entry) for entry in range(place_size())]
    if place_size() != TP:
        total = scatter_bits(blocks, 0, shard_bits(place_size()))
        return total if finish else [total]
    blocks[3] = after(blocks[3], *hold)
    parts = [from_corner(blocks[j], j) for j in range(TP)]
    return sum(part.astype(F32) for part in parts) if finish else parts


def gather_lines(own):
    if place_size() == TP:
        return [((column_index() + k) % TP, from_column(own, k)) for k in range(TP)]
    blocks = gather_bits(own, 2, shard_bits(place_size()))
    return [(line_index() ^ entry, block) for entry, block in enumerate(blocks)]


def scatter_lines(block_of):
    if place_size() == TP:
        total = None
        for step in range(TP):
            came = to_column(block_of((column_index() + step) % TP), step).astype(F32)
            total = came if total is None else total + came
        return total
    return scatter_bits(
        [block_of(line_index() ^ entry) for entry in range(place_size())],
        2,
        shard_bits(place_size()),
    )


def lay(blocks, axis):
    shape = blocks[0][1].shape
    full = jnp.zeros(shape[:axis] + (len(blocks),) + shape[axis:], blocks[0][1].dtype)
    for index, block in blocks:
        starts = [0] * full.ndim
        starts[axis] = index
        full = lax.dynamic_update_slice(full, jnp.expand_dims(block, axis), starts)
    return full


def pick(values, index, axis):
    return lax.dynamic_index_in_dim(values, index, axis, keepdims=False)


def ordered_pair(mine, other):
    first = lax.axis_index("seq") == 0
    return jnp.stack([jnp.where(first, mine, other), jnp.where(first, other, mine)])


def turn_columns(blocks):
    twice = jnp.stack(blocks + blocks)
    return lax.dynamic_slice_in_dim(twice, (TP - column_index()) % TP, TP, 0)


def turn_corners(blocks):
    corner = corner_index()
    for bit in (1, 2):
        odd = corner // bit % 2 == 1
        blocks = [jnp.where(odd, blocks[j ^ bit], blocks[j]) for j in range(TP)]
    return jnp.stack(blocks)


def columns_of(source, starts, size):
    return jnp.concatenate(
        [lax.dynamic_slice_in_dim(source, start, size, 1) for start in starts], axis=1
    )


def pair_qkv(weight):
    seq = lax.axis_index("seq")
    half = TP * HEAD_COLS
    mine = columns_of(weight, [seq * half], half)
    other = flip(columns_of(weight, [(1 - seq) * half], half))
    return ordered_pair(mine, other).reshape(-1, half)


def qkv_piece(pair, step):
    return columns_of(pair, [(corner_index() ^ step) * HEAD_COLS], HEAD_COLS)


def unspread_qkv(total, rows, rider):
    corner, seq = corner_index(), lax.axis_index("seq")
    count = rider.shape[-1]
    loads = [
        ride(pick(total, corner ^ j, 1).reshape(-1, HEAD_COLS), pick(rider, corner ^ j, 2))
        for j in range(TP)
    ]
    loads = [alight(from_corner(loads[j], j), 2 * rows, (2, 2, count)) for j in range(TP)]
    laid = turn_corners([load.reshape(2, rows, HEAD_COLS) for load, _ in loads])
    rider = sum(extra.astype(F32) for _, extra in loads)
    load = ride(pick(laid, 1 - seq, 1).reshape(-1, HEAD_COLS), pick(rider, 1 - seq, 1))
    other, extra = alight(flip(load), TP * rows, (2, count))
    rider = pick(rider, seq, 1) + extra.astype(F32)
    both = ordered_pair(pick(laid, seq, 1), other.reshape(TP, rows, HEAD_COLS))
    return jnp.concatenate([both[s, q] for s in range(2) for q in range(TP)], axis=1), rider


def pair_gateup(weight):
    seq, span = lax.axis_index("seq"), FF // 2
    mine = columns_of(weight, [seq * span, FF + seq * span], span)
    other = flip(columns_of(weight, [(1 - seq) * span, FF + (1 - seq) * span], span))
    return ordered_pair(mine, other).reshape(-1, FF)


def spread_gateup(pair, rider):
    column, span = column_index(), FF // (2 * TP)
    loads = []
    for k in range(TP):
        start = (column - k) % TP * span
        piece = columns_of(pair, [start, FF // 2 + start], span)
        loads.append(from_column(ride(piece, rider), k))
    loads = [alight(load, pair.shape[0], rider.shape) for load in loads]
    return jnp.concatenate([load for load, _ in loads], axis=0), [extra for _, extra in loads]


def collect_lines(block):
    shape = block.shape
    blocks = [
        (index, came.reshape(shape)) for index, came in gather_lines(block.reshape(-1, shape[-1]))
    ]
    return lay(blocks, 1).reshape(-1, shape[-1])


def order_places(came):
    places, columns = place_size(), came.shape[-1]
    came = came.reshape(places, TP, 2, -1, columns)
    full = jnp.zeros((2, TP, places, came.shape[3], columns), came.dtype)
    for k in range(TP):
        part = jnp.swapaxes(came[:, k], 0, 1)[:, None]
        full = lax.dynamic_update_slice(full, part, (0, (column_index() + k) % TP, 0, 0, 0))
    return full.reshape(-1, columns)


def place_parts(values, rows, hold=()):
    span = values.shape[1]
    view = values.reshape(2, TP, place_size(), rows, span)
    return scatter_places(lambda place: pick(view, place, 2).reshape(-1, span), hold, False)


def place_total(parts, rows):
    total = sum(part.astype(F32) for part in parts)
    return total.astype(BF).reshape(2, TP, rows, -1)


def column_piece(total, step):
    return pick(total, (column_index() - step) % TP, 1)


def lay_columns(pieces):
    laid = turn_columns(pieces)
    seq = lax.axis_index("seq")
    return ordered_pair(pick(laid, seq, 1), flip(pick(laid, 1 - seq, 1)))


def norm_scale(values):
    return lax.rsqrt(jnp.mean(values * values, axis=-1, keepdims=True) + NORM_EPS)


def positions_of(seg_row):
    labels = jnp.arange(NCONT + 1, dtype=jnp.int32)
    member = (seg_row[:, None] == labels[None, :]).astype(jnp.int32)
    counts = jnp.sum(member, axis=0)
    starts = jnp.cumsum(counts) - counts
    own_start = jnp.sum(member * starts[None, :], axis=1)
    places = jnp.arange(seg_row.shape[0], dtype=jnp.int32)
    return places - own_start + jnp.where(seg_row > 0, counts[0], 0)


def rotary(positions):
    half_size = HD // 2
    frequency = THETA ** (-(jnp.arange(half_size, dtype=F32) * (2.0 / HD)))
    angles = positions.astype(F32)[:, None] * frequency[None, :]
    angles = jnp.concatenate([angles, angles], axis=-1)
    return (jnp.cos(angles), jnp.sin(angles))


def norm_back(d_normed, inputs_f, factor_rows, gain_row):
    weighted = d_normed * gain_row
    d_inputs = factor_rows * weighted - inputs_f * factor_rows**3 * jnp.mean(
        weighted * inputs_f, axis=-1, keepdims=True
    )
    d_gain = jnp.sum(d_normed * inputs_f * factor_rows, axis=0)
    return (d_inputs, d_gain)


def lamb_step(master, gradient, old_one, old_two, decay_rate):
    new_one = BETA1 * old_one + (1.0 - BETA1) * gradient
    new_two = BETA2 * old_two + (1.0 - BETA2) * gradient * gradient
    update = (
        new_one / (1.0 - BETA1**STEP) / (jnp.sqrt(new_two / (1.0 - BETA2**STEP)) + ADAM_EPS)
        + decay_rate * master
    )
    return new_one, new_two, update


SMALL = pl.CostEstimate(flops=10**9, bytes_accessed=1, transcendentals=0)
MIB = 1 << 20


def params(mebibytes):
    return pltpu.CompilerParams(vmem_limit_bytes=mebibytes * MIB)


def whole(shape):
    return pl.BlockSpec(shape, lambda step: (0,) * len(shape), pipeline_mode=pl.Buffered(1))


def at_group(shape, axis):
    return pl.BlockSpec(shape, lambda step: tuple(step if d == axis else 0 for d in range(len(shape))))


def half_sign():
    lane = lax.broadcasted_iota(jnp.int32, (1, HD), 1)
    return jnp.where(lane < HD // 2, -1.0, 1.0)


def scores_of(query, key_rows, allowed):
    return jnp.where(allowed, dot_last(query, key_rows) * HD ** (-0.5), MASKED)


def allowed_of(place_col, place_row, id_col, id_row):
    return (place_row <= place_col) & ((id_row == 0) | (id_row == id_col))


def attend_kernel(
    x_ref, gain_ref, qkv_ref, cos_ref, sin_ref, place_col, place_row, id_col, id_row,
    turned_ref, lse_ref, attended_ref,
):
    tokens = cos_ref.shape[1]
    x = x_ref[...].reshape(tokens, -1).astype(F32)
    normed = (x * norm_scale(x) * gain_ref[...]).astype(BF)
    projected = dot(normed, qkv_ref[...])
    cosine, sine = cos_ref[0], sin_ref[0] * half_sign()
    turned = []
    for head in range(GROUP + 2):
        values = projected[:, head * HD : (head + 1) * HD]
        if head <= GROUP:
            values = values * cosine + pltpu.roll(values, HD // 2, 1) * sine
        turned.append(values.astype(BF))
        turned_ref[0, :, head * HD : (head + 1) * HD] = turned[head]
    allowed = allowed_of(place_col[...], place_row[...], id_col[0], id_row[0])
    for head in range(GROUP):
        scores = scores_of(turned[head], turned[GROUP], allowed)
        row_max = jnp.max(scores, axis=-1, keepdims=True)
        exponent = jnp.exp(scores - row_max)
        row_total = jnp.sum(exponent, axis=-1, keepdims=True)
        lse_ref[0, head] = row_max + jnp.log(row_total)
        rows_out = dot((exponent / row_total).astype(BF), turned[GROUP + 1]).astype(BF)
        attended_ref[:, 0, :, head * HD : (head + 1) * HD] = rows_out.reshape(2, tokens // 2, HD)


def attend(x_all, gain, qkv_matrix, cosine, sine, marks):
    _, groups, half_tok, width = x_all.shape
    tokens = 2 * half_tok
    by_half = lambda columns: at_group((2, 1, half_tok, columns), 1)
    return pl.pallas_call(
        attend_kernel,
        grid=(groups,),
        in_specs=[
            by_half(width),
            whole((1, width)),
            whole((width, HEAD_COLS)),
            at_group((1, tokens, HD), 0),
            at_group((1, tokens, HD), 0),
            whole((tokens, 1)),
            whole((1, tokens)),
            at_group((1, tokens, 1), 0),
            at_group((1, 1, tokens), 0),
        ],
        out_specs=[
            at_group((1, tokens, HEAD_COLS), 0),
            at_group((1, GROUP, tokens, 1), 0),
            by_half(GROUP * HD),
        ],
        out_shape=[
            jax.ShapeDtypeStruct((groups, tokens, HEAD_COLS), BF),
            jax.ShapeDtypeStruct((groups, GROUP, tokens, 1), F32),
            jax.ShapeDtypeStruct((2, groups, half_tok, GROUP * HD), BF),
        ],
        compiler_params=params(32),
        cost_estimate=SMALL,
    )(x_all, gain, qkv_matrix, cosine, sine, *marks)


def attend_back_kernel(
    branch_ref, out_ref, qkv_ref, x_ref, gain_ref, attended_ref, turned_ref, lse_ref, cos_ref, sin_ref,
    place_col, place_row, id_col, id_row,
    mine_ref, other_ref, grad_qkv_ref, grad_out_ref, grad_gain_ref, qkv_sum, out_sum,
):
    tokens = cos_ref.shape[1]
    factor = HD ** (-0.5)
    first = pl.program_id(0) == 0
    last = pl.program_id(0) == pl.num_programs(0) - 1
    branch = branch_ref[...].reshape(tokens, -1)
    d_attended = dot_last(branch, out_ref[...]).astype(BF)
    turned = [turned_ref[0, :, head * HD : (head + 1) * HD] for head in range(GROUP + 2)]
    key_rows, value_rows = turned[GROUP], turned[GROUP + 1]
    allowed = allowed_of(place_col[...], place_row[...], id_col[0], id_row[0])
    cosine, sine, sign = cos_ref[0], sin_ref[0], half_sign()

    def unrope(values):
        values = values.astype(BF).astype(F32)
        return (values * cosine - sign * pltpu.roll(values * sine, HD // 2, 1)).astype(BF)

    d_keys = d_values = None
    columns = []
    for head in range(GROUP):
        d_rows = d_attended[:, head * HD : (head + 1) * HD]
        probs = jnp.exp(scores_of(turned[head], key_rows, allowed) - lse_ref[0, head])
        d_probs = dot_last(d_rows, value_rows)
        row_sum = jnp.sum(probs * d_probs, axis=-1, keepdims=True)
        d_scores = (probs * (d_probs - row_sum)).astype(BF)
        columns.append(unrope(dot(d_scores, key_rows) * factor))
        key_part = dot_rows(d_scores, turned[head]) * factor
        value_part = dot_rows(probs.astype(BF), d_rows)
        d_keys = key_part if d_keys is None else d_keys + key_part
        d_values = value_part if d_values is None else d_values + value_part
    columns.append(unrope(d_keys))
    columns.append(d_values.astype(BF))
    projected = jnp.concatenate(columns, axis=1)
    d_normed = dot_last(projected, qkv_ref[...])
    mine_ref[0] = d_normed[: tokens // 2].astype(BF)
    other_ref[0] = d_normed[tokens // 2 :].astype(BF)

    @pl.when(first)
    def _():
        qkv_sum[...] = jnp.zeros_like(qkv_sum)
        out_sum[...] = jnp.zeros_like(out_sum)
        grad_gain_ref[...] = jnp.zeros_like(grad_gain_ref)

    x = x_ref[...].reshape(tokens, -1).astype(F32)
    scaled = x * norm_scale(x)
    grad_gain_ref[...] += jnp.sum(d_normed * scaled, axis=0, keepdims=True)
    qkv_sum[...] += dot_rows((scaled * gain_ref[...]).astype(BF), projected)
    out_sum[...] += dot_rows(attended_ref[...].reshape(tokens, -1), branch)

    @pl.when(last)
    def _():
        grad_qkv_ref[...] = qkv_sum[...].astype(BF)
        grad_out_ref[...] = out_sum[...].astype(BF)


def attend_back(d_branch, out_matrix, qkv_matrix, x_all, gain, attended, turned, lse, cosine, sine, marks):
    _, groups, half_tok, width = d_branch.shape
    tokens = 2 * half_tok
    return pl.pallas_call(
        attend_back_kernel,
        grid=(groups,),
        in_specs=[
            at_group((2, 1, half_tok, width), 1),
            whole((GROUP * HD, width)),
            whole((width, HEAD_COLS)),
            at_group((2, 1, half_tok, width), 1),
            whole((1, width)),
            at_group((2, 1, half_tok, GROUP * HD), 1),
            at_group((1, tokens, HEAD_COLS), 0),
            at_group((1, GROUP, tokens, 1), 0),
            at_group((1, tokens, HD), 0),
            at_group((1, tokens, HD), 0),
            whole((tokens, 1)),
            whole((1, tokens)),
            at_group((1, tokens, 1), 0),
            at_group((1, 1, tokens), 0),
        ],
        out_specs=[
            at_group((1, half_tok, width), 0),
            at_group((1, half_tok, width), 0),
            whole((width, HEAD_COLS)),
            whole((GROUP * HD, width)),
            whole((1, width)),
        ],
        out_shape=[
            jax.ShapeDtypeStruct((groups, half_tok, width), BF),
            jax.ShapeDtypeStruct((groups, half_tok, width), BF),
            jax.ShapeDtypeStruct((width, HEAD_COLS), BF),
            jax.ShapeDtypeStruct((GROUP * HD, width), BF),
            jax.ShapeDtypeStruct((1, width), F32),
        ],
        scratch_shapes=[pltpu.VMEM((width, HEAD_COLS), F32), pltpu.VMEM((GROUP * HD, width), F32)],
        compiler_params=params(48),
        cost_estimate=SMALL,
    )(d_branch, out_matrix, qkv_matrix, x_all, gain, attended, turned, lse, cosine, sine, *marks)


def half_specs(rows, columns, steps):
    first = pl.BlockSpec((rows, columns), lambda step: (jnp.minimum(step, steps // 2 - 1), 0))
    second = pl.BlockSpec((rows, columns), lambda step: (jnp.maximum(step - steps // 2, 0), 0))
    shapes = [
        jax.ShapeDtypeStruct((rows * steps // 2, columns), BF),
        jax.ShapeDtypeStruct((rows * steps // 2, columns), BF),
    ]
    return [first, second], shapes


def store_halves(values, mine_ref, other_ref):
    step, half = pl.program_id(0), pl.num_programs(0) // 2

    @pl.when(step < half)
    def _():
        mine_ref[...] = values.astype(BF)

    @pl.when(step >= half)
    def _():
        other_ref[...] = values.astype(BF)


def partial_kernel(left_ref, right_ref, mine_ref, other_ref):
    store_halves(dot(left_ref[...], right_ref[...]), mine_ref, other_ref)


def partial_product(left, right):
    tokens, depth = left.shape
    rows, steps = tokens // 4, 4
    specs, shapes = half_specs(rows, right.shape[1], steps)
    return pl.pallas_call(
        partial_kernel,
        grid=(steps,),
        in_specs=[at_group((rows, depth), 0), whole(right.shape)],
        out_specs=specs,
        out_shape=shapes,
        compiler_params=params(32),
        cost_estimate=SMALL,
    )(left, right)


def forward_back_kernel(
    normed_ref, og_ref, matrix_ref, down_ref,
    activated_ref, d_first_ref, d_second_ref, mine_ref, other_ref,
):
    width = matrix_ref.shape[1] // 4
    normed, og = normed_ref[...], og_ref[...]
    total = None
    for half, d_ref in enumerate((d_first_ref, d_second_ref)):
        gate_matrix = matrix_ref[:, half * width : (half + 1) * width]
        up_matrix = matrix_ref[:, (2 + half) * width : (3 + half) * width]
        gate, up = dot(normed, gate_matrix), dot(normed, up_matrix)
        d_act = dot_last(og, down_ref[half * width : (half + 1) * width])
        sigmoid = jax.nn.sigmoid(gate)
        silu = gate * sigmoid
        activated_ref[:, half * width : (half + 1) * width] = (silu * up).astype(BF)
        d_ref[:, :width] = (d_act * up * (sigmoid * (1.0 + gate * (1.0 - sigmoid)))).astype(BF)
        d_ref[:, width:] = (d_act * silu).astype(BF)
        back = dot_last(d_ref[:, :width], gate_matrix) + dot_last(d_ref[:, width:], up_matrix)
        total = back if total is None else total + back
    store_halves(total, mine_ref, other_ref)


def forward_back(normed2, og_all, gateup_matrix, down_matrix):
    tokens, width = normed2.shape
    unit = down_matrix.shape[0]
    rows, steps = tokens // 4, 4
    specs, shapes = half_specs(rows, width, steps)
    return pl.pallas_call(
        forward_back_kernel,
        grid=(steps,),
        in_specs=[
            at_group((rows, width), 0),
            at_group((rows, width), 0),
            whole((width, 2 * unit)),
            whole((unit, width)),
        ],
        out_specs=[at_group((rows, unit), 0)] * 3 + specs,
        out_shape=[jax.ShapeDtypeStruct((tokens, unit), BF)] * 3 + shapes,
        compiler_params=params(48),
        cost_estimate=SMALL,
    )(normed2, og_all, gateup_matrix, down_matrix)


def gradient_kernel(left_ref, right_ref, out_ref):
    out_ref[...] = dot_rows(left_ref[...], right_ref[...]).astype(BF)


def gradient(left, right):
    tokens, rows = left.shape
    block = min(rows, 256)
    return pl.pallas_call(
        gradient_kernel,
        grid=(rows // block,),
        in_specs=[at_group((tokens, block), 1), whole(right.shape)],
        out_specs=at_group((block, right.shape[1]), 0),
        out_shape=jax.ShapeDtypeStruct((rows, right.shape[1]), BF),
        compiler_params=params(32),
        cost_estimate=SMALL,
    )(left, right)


def lamb_kernel(
    master_ref, one_ref, two_ref, first_ref, second_ref, new_one_ref, new_two_ref, update_ref, sums_ref
):
    gradient = jnp.concatenate([first_ref[0, 0], second_ref[0, 0]], axis=1).astype(F32)
    master = master_ref[...]
    new_one, new_two, update = lamb_step(master, gradient, one_ref[...], two_ref[...], DECAY)
    new_one_ref[...], new_two_ref[...], update_ref[...] = new_one, new_two, update

    @pl.when(pl.program_id(0) == 0)
    def _():
        sums_ref[...] = jnp.zeros_like(sums_ref)

    sums_ref[0:1] += jnp.sum(master * master, axis=0, keepdims=True)
    sums_ref[1:2] += jnp.sum(update * update, axis=0, keepdims=True)


def lamb_gateup(master, old_one, old_two, halves):
    rows, columns = master.shape
    span = columns // (4 * TP)
    state = pl.BlockSpec((rows, span), lambda step: (0, step))
    piece = pl.BlockSpec(
        (1, 1, rows, span // 2), lambda step: (step // TP % 2, step % TP, 0, step // (2 * TP))
    )
    shape = jax.ShapeDtypeStruct(master.shape, F32)
    return pl.pallas_call(
        lamb_kernel,
        grid=(4 * TP,),
        in_specs=[state] * 3 + [piece] * 2,
        out_specs=[state] * 3 + [whole((2, span))],
        out_shape=[shape] * 3 + [jax.ShapeDtypeStruct((2, span), F32)],
        compiler_params=params(32),
        cost_estimate=SMALL,
    )(master, old_one, old_two, *halves)


def shards(
    hidden_in,
    out_grad,
    segments,
    qkv_weight,
    out_weight,
    gateup_weight,
    down_weight,
    gain_weight,
    qkv_first,
    out_first,
    gateup_first,
    down_first,
    gain_first,
    qkv_second,
    out_second,
    gateup_second,
    down_second,
    gain_second,
):
    seq = lax.axis_index("seq")
    rows = qkv_weight.shape[0]
    tok_local = hidden_in.shape[1]
    group_tok = tok_local * lax.axis_size("seq")
    span = TP * tok_local
    owner = seq * shard_size() + lax.axis_index("shard")


    x_own, og_own = hidden_in[0], out_grad[0]
    x_local = x_own.astype(F32)
    recent()

    gain_cols, width = gain_weight.shape[1], x_own.shape[1]
    packed = place_size() == TP
    shard = lax.axis_index("shard")
    gain_low = gain_weight.astype(BF)
    info = jnp.concatenate([gain_low.reshape(-1), segments.reshape(-1).astype(BF)])
    og_mine = [og_own, from_column(og_own, 1), None, from_column(og_own, 3)]
    came = recent()
    qkv_pair = pair_qkv(qkv_weight.astype(BF))
    pair = pair_gateup(gateup_weight.astype(BF))
    pairs_came = recent()
    loads = [
        jnp.concatenate([x_own, qkv_piece(qkv_pair, j).reshape(tok_local, -1)], axis=1)
        for j in range(TP)
    ]
    loads = [ride(load, info) for load in loads]
    loads[3] = after(loads[3], *came[:1])
    loads = [from_corner(loads[j], j) for j in range(TP)]
    loads = [alight(load, tok_local, info.shape) for load in loads]
    x_mine = [load[:, :width] for load, _ in loads]
    infos = jnp.stack([extra for _, extra in loads])
    qkv_block = turn_corners([load[:, width:].reshape(-1, HEAD_COLS) for load, _ in loads])
    qkv_block = jnp.swapaxes(qkv_block.reshape(TP, 2, rows, HEAD_COLS), 0, 1)
    slot = (*came, *pairs_came, *recent())
    ids = [infos[j, 2 * gain_cols :].astype(jnp.int32) for j in range(TP)]

    down_matrix = gather_places(after(down_weight.astype(BF), *slot)).reshape(-1, width)
    gateup_block, infos = spread_gateup(after(pair, *slot), infos)
    infos = jnp.stack(infos)
    out_block = swap_roles(after(out_weight.astype(BF), *slot))
    slot = recent()

    qkv_matrix = collect_lines(after(qkv_block, *slot))
    came = recent()
    gateup_came = gather_places(after(gateup_block, down_matrix))
    gateup_matrix = order_places(gateup_came)
    x_half = jnp.concatenate([after(x_mine[0], *slot, down_matrix), *x_mine[1:]], axis=0)
    x_other, infos_other = alight(flip(ride(x_half, infos)), span, infos.shape)
    x_all = jnp.concatenate([x_half, x_other], axis=0).reshape(2, TP, tok_local, width)
    if packed:
        gains = ordered_pair(infos, infos_other)[..., : 2 * gain_cols]
        gains = turn_columns([turn_corners([gains[:, k, j] for j in range(TP)]) for k in range(TP)])
        gains = jnp.transpose(gains.reshape(TP, TP, 2, 2, gain_cols), (3, 2, 0, 1, 4)).reshape(2, width)
    else:
        gains = jnp.zeros((2, width), BF)
        gains = butterfly(lax.dynamic_update_slice(gains, gain_low, (0, owner * gain_cols)))
    gains = gains.astype(F32)
    slot = (*came, *recent(), x_all, gains)

    def local_order(values):
        return jnp.where(seq == 0, values, jnp.roll(values, -tok_local, axis=-1))

    positions = jnp.stack([local_order(positions_of(entry)) for entry in ids])
    ids = jnp.stack([local_order(entry) for entry in ids])
    places = local_order(jnp.arange(group_tok, dtype=jnp.int32))
    marks = (places[:, None], places[None, :], ids[:, :, None], ids[:, None, :])
    cosine, sine = rotary(positions.reshape(-1))
    cosine, sine = cosine.reshape(TP, group_tok, HD), sine.reshape(TP, group_tok, HD)

    out_matrix = lay(
        [(line_place(line), block) for line, block in gather_lines(after(out_block, *slot))], 0
    ).reshape(GROUP * HD, -1)
    came = recent()
    og_mine[2] = from_column(after(og_own, *slot), 2)
    recent()
    turned, lse, attended = attend(x_all, gains[:1], qkv_matrix, cosine, sine, marks)
    attended = attended.reshape(-1, GROUP * HD)
    slot = (*came, attended)

    met = meet_halves(*partial_product(after(attended, *slot, gateup_came), out_matrix))
    middle = x_local + met[0]
    for j in range(1, TP):
        middle = middle + from_corner(met[j].astype(BF), j).astype(F32)
    factor_two = norm_scale(middle)
    slot = recent()

    og_all = both_halves([after(entry, *slot) for entry in og_mine])
    recent()

    normed2_own = after((middle * factor_two * gains[1]).astype(BF), *slot, og_mine[2])
    normed2 = [from_column(normed2_own, k) for k in range(TP)]
    normed2 = both_halves([after(normed2[0], gateup_matrix, *recent()), *normed2[1:]])
    slot = recent()

    activated, d_gate_up_0, d_gate_up_1, d_mine, d_other = forward_back(
        after(normed2, *slot), og_all, gateup_matrix, down_matrix
    )

    d_met = meet_halves(d_mine, d_other)
    slot = recent()
    sends = [entry.astype(BF) for entry in d_met[1:]]
    grad_half_0 = gradient(after(normed2, d_other), d_gate_up_0)
    total_0 = place_total(place_parts(after(grad_half_0, *slot), rows), rows)
    out_mine, out_other = partial_product(after(activated, *slot, grad_half_0), down_matrix)
    grad_half_1 = gradient(after(normed2, *slot, grad_half_0), d_gate_up_1)
    d_normed2 = d_met[0]
    for k in range(1, TP):
        came = after(to_column(sends[k - 1], k), out_other, grad_half_1)
        d_normed2 = d_normed2 + came.astype(F32)
    d_mid_part, d_gain_two = norm_back(d_normed2, middle, factor_two, gains[1])
    d_middle = og_own.astype(F32) + d_mid_part
    slot = recent()

    d_branch_own = after(d_middle.astype(BF), *slot)
    d_branch_mine = [from_corner(d_branch_own, j) for j in range(TP)]
    came = recent()
    held = after(total_0, *slot, d_branch_own)
    pieces = [column_piece(held, k) for k in range(TP)]
    out_met = meet_halves(out_mine, after(out_other, *slot))
    pieces[3] = after(pieces[3], *came, *recent())
    pieces_0 = [from_column(pieces[k], k) for k in range(TP)]
    slot = (*came, *recent())

    sends = [after(entry.astype(BF), *slot) for entry in out_met]
    result = middle + out_met[0]
    for k in range(1, TP):
        send = sends[k] if k < 3 else after(sends[k], RECENT[0])
        result = result + to_column(send, k).astype(F32)
    output = result.astype(BF)[None]
    out_came = recent()
    parts_1 = place_parts(after(grad_half_1, *slot), rows)
    out_came = (*out_came, *recent())
    d_branch = both_halves([after(entry, *slot) for entry in d_branch_mine])
    in_mine, in_other, grad_qkv, grad_out, d_gain_one = attend_back(
        d_branch.reshape(2, TP, tok_local, width),
        out_matrix,
        qkv_matrix,
        x_all,
        gains[:1],
        attended.reshape(2, TP, tok_local, GROUP * HD),
        turned,
        lse,
        cosine,
        sine,
        marks,
    )
    grad_down = gradient(after(activated, *slot), og_all)
    in_other = after(in_other.reshape(-1, width), *out_came, grad_down)
    in_met = meet_halves(in_mine.reshape(-1, width), in_other)
    slot = (*recent(), *out_came)

    d_normed = in_met[0]
    for j in range(1, TP):
        d_normed = d_normed + from_corner(after(in_met[j].astype(BF), *slot), j).astype(F32)
    came = recent()
    laid_0 = lay_columns([after(piece, *came) for piece in pieces_0])
    recent()
    d_gains = jnp.concatenate([d_gain_one, d_gain_two[None]], axis=0)
    qkv_view = after(grad_qkv, *slot).reshape(2, place_size(), TP, rows, HEAD_COLS)
    out_view = after(grad_out, *slot).reshape(place_size(), -1, width)
    if packed:
        rider = d_gains.reshape(2, 2, TP, TP, gain_cols)
        qkv_rows, loads = 2 * TP * rows, []
        for k in range(TP):
            line = (column_index() + k) % TP
            load = [pick(qkv_view, line, 1), pick(out_view, line, 0)]
            load = jnp.concatenate([entry.reshape(-1, HEAD_COLS) for entry in load], axis=0)
            loads.append(ride(load, pick(rider, line, 2)))
        sent_rows = qkv_rows + out_view.shape[1] * width // HEAD_COLS
        loads[3] = after(loads[3], *came)
        loads = [to_column(loads[k], k) for k in range(TP)]
        loads = [alight(entry, sent_rows, (2, 2, TP, gain_cols)) for entry in loads]
        rider = sum(extra.astype(F32) for _, extra in loads)
        qkv_total = sum(load[:qkv_rows].astype(F32) for load, _ in loads)
        grad_out = sum(load[qkv_rows:].astype(F32) for load, _ in loads).reshape(-1, width)
    else:
        qkv_total = scatter_lines(lambda line: pick(qkv_view, line, 1).reshape(-1, HEAD_COLS))
        grad_out = scatter_lines(lambda line: pick(out_view, line_place(line), 0))
        rider = jnp.zeros((2, 2, TP, gain_cols), F32)
    slot = recent()
    down_view = after(grad_down, *came).reshape(place_size(), -1, width)
    grad_down = scatter_places(lambda place: pick(down_view, place, 0), slot[:1])
    slot = (*came, *slot, *recent()[:2])
    factor_one = norm_scale(x_local)
    d_in_part = norm_back(d_normed, x_local, factor_one, gains[0])[0]
    input_grad = (d_middle + d_in_part).astype(BF)[None]

    held = after(place_total([after(part, *came) for part in parts_1], rows), *slot)
    recent()
    pieces_1 = [from_column(column_piece(held, k), k) for k in range(TP)]
    qkv_total = after(qkv_total.astype(BF), *slot, *recent()).reshape(2, TP, rows, HEAD_COLS)
    grad_qkv, grad_gain = unspread_qkv(qkv_total, rows, rider)
    grad_qkv = grad_qkv.astype(F32)
    laid_1 = lay_columns(pieces_1)
    grad_out = swap_roles(after(grad_out.astype(BF), *slot)).astype(F32)
    if not packed:
        grad_gain = lax.dynamic_slice_in_dim(butterfly(d_gains), owner * gain_cols, gain_cols, 1)

    masters = (qkv_weight, out_weight, gateup_weight, down_weight, gain_weight)
    gateup_one, gateup_two, gateup_update, gateup_sums = lamb_gateup(
        gateup_weight, gateup_first, gateup_second, [laid_0, laid_1]
    )
    steps = [
        lamb_step(*entry)
        for entry in (
            (qkv_weight, grad_qkv, qkv_first, qkv_second, DECAY),
            (out_weight, grad_out, out_first, out_second, DECAY),
            (down_weight, grad_down, down_first, down_second, DECAY),
            (gain_weight, grad_gain, gain_first, gain_second, 0.0),
        )
    ]
    steps.insert(2, (gateup_one, gateup_two, gateup_update))
    new_ones, new_twos, updates = zip(*steps)

    def squares(arrays):
        return [jnp.sum(entry * entry) for entry in arrays]

    totals = [
        [*squares(entry[:2]), jnp.sum(gateup_sums[row]), *squares((entry[3], *entry[4]))]
        for row, entry in enumerate((masters, updates))
    ]

    def spots(entries):
        total = jnp.zeros((2, 6), F32)
        for row, column, value in entries:
            spot = np.zeros((2, 6), np.float32)
            spot[row, column] = 1.0
            total = total + value * spot
        return total

    entries = [
        (row, column, total)
        for row in range(2)
        for column, total in enumerate(totals[row])
    ]
    early = [entries[slot] for slot in (0, 1, 3, 4, 5, 6, 7, 9, 10, 11)]
    norms = lax.optimization_barrier(spots(early)) + spots([entries[2], entries[8]])
    norms = jnp.sqrt(butterfly(norms))
    ratios = norms[0] / norms[1]
    news = [masters[slot] - RATE * ratios[slot] * updates[slot] for slot in range(4)]
    news.append(masters[4] - RATE * ratios[4:6][:, None] * updates[4])
    copies = [entry.astype(BF) for entry in news]
    recent()
    return (output, input_grad, *news, *new_ones, *new_twos, *copies, norms)


def solution(mesh):
    rows, columns = P(("seq", "shard"), None), P(None, ("seq", "shard"))
    tokens = P("shard", "seq", None)
    states = (rows, rows, rows, rows, columns)
    return jax.shard_map(
        shards,
        mesh=mesh,
        in_specs=(tokens, tokens, P("shard", None)) + states * 3,
        out_specs=(tokens, tokens) + states * 4 + (P(),),
        check_vma=False,
    )
```
